512 devices in a mesh: seq: 4 (over x), tok: 128 (over y, z, core).
Axes of the slice: x: 4, y: 4, z: 16, core: 2. Of those that a mesh axis runs over, the one named last changes fastest.
Arguments:
- tokens: bfloat16 [4, 16384, 768], P('seq', 'tok'), may hold values from -32 to 32
- w_shared: bfloat16 [768, 384], replicated, may hold values from -0.21875 to 0.21875
- w_value: bfloat16 [768, 384], replicated, may hold values from -0.21875 to 0.21875
- cluster_ids: int32 [4, 6, 16384], P('seq', None, 'tok'), may hold values from 0 to 127, as said below
- slot_index: int32 [4, 6, 16384], P('seq', None, 'tok'), may hold values from 0 to 255, as said below
- cotangent: bfloat16 [4, 16384, 384], P('seq', 'tok'), may hold values from -6 to 6
Outputs:
- attention: bfloat16 [4, 16384, 384], P('seq', 'tok')
- grad_tokens: bfloat16 [4, 16384, 768], P('seq', 'tok')
- grad_shared: bfloat16 [768, 384], replicated
- grad_value: bfloat16 [768, 384], replicated
The draws below stay inside these ranges and needn't reach their ends.
Inputs may be any that keep to these rules, and one draw needn't show every extreme that they name: `cluster_ids`: every cluster of a sequence and head holds at most 256 tokens, and some cluster exactly 256; the 128 tokens of one device hold at most 2 tokens of one cluster of one head, and some exactly 2. `slot_index`: the tokens of a cluster are numbered 0, 1, 2 and so on in order of position.
All inputs are finite; a program needn't handle non-finite values.
Results may differ from the reference program's by a relative error of at most 0.014.
The reference program's roundings to bfloat16 on the way count: a program that leaves them out, or rounds other values in their place, can miss the bound.
Values may be sent and summed in bfloat16 or wider, within the bound.
No kernel may reach another device: no remote copies, remote signals or barrier semaphores. Data moves between devices by JAX's collectives and lax.ppermute only.
A program may use at most 64 MiB of HBM per device.

```python
import jax
import jax.numpy as jnp
from jax import lax

D = 768
H = 6
HD = 64
TOK_DEV = 128
SEQS = 4
SEQLEN = 16384
CLUST = 128
CAP = 256
PEER_ROWS = 2


def one_route(route_key):
    key_perm, key_shift, key_target, key_shuffle = jax.random.split(route_key, 4)
    cluster_count = CLUST
    block_rows = TOK_DEV
    half_most = PEER_ROWS // 2
    relabel = jax.random.permutation(key_perm, cluster_count).astype(jnp.int32)
    spread_shift = jax.random.randint(key_shift, (cluster_count, cluster_count // 2), -half_most, half_most + 1).astype(jnp.int32)
    full_target = jax.random.randint(key_target, (), 0, cluster_count).astype(jnp.int32)
    part_ids = jnp.arange(cluster_count, dtype=jnp.int32)
    sources = (full_target - part_ids) % cluster_count
    forced = jnp.where(part_ids % 2 == 0, half_most, -half_most).astype(jnp.int32)
    spread_shift = spread_shift.at[sources, part_ids // 2].set(forced)
    part_sizes = jnp.stack([half_most + spread_shift, half_most - spread_shift], axis=-1).reshape(cluster_count, cluster_count)
    part_ends = jnp.cumsum(part_sizes, axis=1)
    local_pos = jnp.arange(block_rows, dtype=jnp.int32)
    part_of = jnp.sum((part_ends[:, None, :] <= local_pos[None, :, None]).astype(jnp.int32), axis=-1)
    chosen = relabel[(part_ids[:, None] + part_of) % cluster_count]
    shuffles = jax.vmap(lambda shuffle_key: jax.random.permutation(shuffle_key, block_rows).astype(jnp.int32))(jax.random.split(key_shuffle, cluster_count))
    assigned = jnp.zeros((cluster_count, block_rows), jnp.int32).at[part_ids[:, None], shuffles].set(chosen)
    assigned = assigned.reshape(cluster_count * block_rows)
    one_hot = (assigned[:, None] == part_ids[None, :]).astype(jnp.int32)
    running = jnp.cumsum(one_hot, axis=0) - one_hot
    numbered = jnp.sum(running * one_hot, axis=1).astype(jnp.int32)
    return (assigned, numbered)


def routing(key):
    route_keys = jax.random.split(key, SEQS * H)
    assigned, numbered = lax.map(one_route, route_keys)
    return (assigned.reshape(SEQS, H, SEQLEN), numbered.reshape(SEQS, H, SEQLEN))


def draw_cluster_ids(key, part):
    assigned, numbered = routing(key)
    return assigned


def draw_slot_index(key, part):
    assigned, numbered = routing(key)
    return numbered


def draw_tokens(key, part):
    key = jax.random.fold_in(key, 3)
    drawn = jnp.clip(jax.random.normal(key, (SEQS, SEQLEN, D), jnp.float32), -4.0, 4.0)
    return drawn.astype(jnp.bfloat16)


def block_levels(key, extent, shards, low, top_value):
    gain = 1.0
    for axis_at, blocks in shards:
        steps = jax.random.uniform(jax.random.fold_in(jax.random.fold_in(key, 6), axis_at), (blocks,), jnp.float32, low / len(shards), top_value / len(shards))
        gain = gain * jnp.repeat(jnp.exp(steps), extent[axis_at] // blocks).reshape((-1,) + (1,) * (len(extent) - 1 - axis_at))
    return gain


def gaussian(key, extent, width, reach, cuts=(), held_as=jnp.bfloat16):
    values = width * jax.random.normal(key, extent, jnp.float32)
    if cuts:
        values = values * block_levels(key, extent, cuts, -0.22, 0.18)
    return jnp.clip(values, -reach, reach).astype(held_as)


def setup_inputs(seed: int = 0) -> dict:
    arg_keys = jax.random.split(jax.random.key(seed), 7)
    return {
        "tokens": draw_tokens(jax.random.fold_in(arg_keys[6], 71), 0),
        "w_shared": gaussian(arg_keys[1], (D, H * HD), D ** -0.5, 0.21875),
        "w_value": gaussian(arg_keys[2], (D, H * HD), D ** -0.5, 0.21875),
        "cluster_ids": draw_cluster_ids(jax.random.fold_in(arg_keys[6], 71), 0),
        "slot_index": draw_slot_index(jax.random.fold_in(arg_keys[6], 71), 0),
        "cotangent": gaussian(arg_keys[5], (SEQS, SEQLEN, H * HD), 1.0, 6.0, ((0, 4), (1, 128))),
    }


def cluster_block(pieces):
    shared_rows, value_rows, grad_rows = pieces
    block_size = shared_rows.shape[0]
    score_scale = shared_rows.shape[1] ** -0.5
    ordinal = jnp.arange(block_size)
    allowed = ordinal[None, :] <= ordinal[:, None]
    scores = jnp.dot(shared_rows, shared_rows.T, preferred_element_type=jnp.float32) * score_scale
    scores = jnp.where(allowed, scores, -1e30)
    highest = jnp.max(scores, axis=1, keepdims=True)
    weights = jnp.exp(scores - highest)
    attn_weights = (weights / jnp.sum(weights, axis=1, keepdims=True)).astype(jnp.bfloat16)
    output = jnp.dot(attn_weights, value_rows, preferred_element_type=jnp.float32).astype(jnp.bfloat16)
    d_prob = jnp.dot(grad_rows, value_rows.T, preferred_element_type=jnp.float32)
    wide_weights = attn_weights.astype(jnp.float32)
    row_delta = jnp.sum(wide_weights * d_prob, axis=1, keepdims=True)
    d_score = (wide_weights * (d_prob - row_delta)).astype(jnp.bfloat16)
    both_sides = jnp.dot(d_score, shared_rows, preferred_element_type=jnp.float32) + jnp.dot(d_score.T, shared_rows, preferred_element_type=jnp.float32)
    d_shared = (both_sides * score_scale).astype(jnp.bfloat16)
    d_value = jnp.dot(attn_weights.T, grad_rows, preferred_element_type=jnp.float32).astype(jnp.bfloat16)
    return output, d_shared, d_value


def reference(tokens, w_shared, w_value, cluster_ids, slot_index, cotangent):
    flat_tokens = tokens.reshape(SEQS * SEQLEN, D)
    shared = jnp.dot(flat_tokens, w_shared, preferred_element_type=jnp.float32).astype(jnp.bfloat16).reshape(SEQS, SEQLEN, H, HD)
    value = jnp.dot(flat_tokens, w_value, preferred_element_type=jnp.float32).astype(jnp.bfloat16).reshape(SEQS, SEQLEN, H, HD)
    grad_all = cotangent.reshape(SEQS, SEQLEN, H, HD)
    out_seqs = []
    dsh_seqs = []
    dva_seqs = []
    for seq_index in range(SEQS):
        out_heads = []
        dsh_heads = []
        dva_heads = []
        for head_index in range(H):
            flat_slot = (cluster_ids[seq_index, head_index].astype(jnp.int32) * CAP + slot_index[seq_index, head_index].astype(jnp.int32)).astype(jnp.int32)

            def to_blocks(matrix):
                spread = jnp.zeros((CLUST * CAP, HD), matrix.dtype).at[flat_slot].set(matrix)
                return spread.reshape(CLUST, CAP, HD)

            blocks = lax.map(cluster_block, (to_blocks(shared[seq_index, :, head_index]), to_blocks(value[seq_index, :, head_index]), to_blocks(grad_all[seq_index, :, head_index])))
            unpacked = [block.reshape(CLUST * CAP, HD)[flat_slot] for block in blocks]
            out_heads.append(unpacked[0])
            dsh_heads.append(unpacked[1])
            dva_heads.append(unpacked[2])
        out_seqs.append(jnp.stack(out_heads, axis=1).reshape(SEQLEN, H * HD))
        dsh_seqs.append(jnp.stack(dsh_heads, axis=1).reshape(SEQLEN, H * HD))
        dva_seqs.append(jnp.stack(dva_heads, axis=1).reshape(SEQLEN, H * HD))
    attention = jnp.stack(out_seqs, axis=0)
    d_shared = jnp.stack(dsh_seqs, axis=0).reshape(SEQS * SEQLEN, H * HD)
    d_value = jnp.stack(dva_seqs, axis=0).reshape(SEQS * SEQLEN, H * HD)
    grad_tokens = jnp.dot(d_shared, w_shared.T, preferred_element_type=jnp.float32) + jnp.dot(d_value, w_value.T, preferred_element_type=jnp.float32)
    grad_tokens = grad_tokens.astype(jnp.bfloat16).reshape(SEQS, SEQLEN, D)
    grad_shared = jnp.dot(flat_tokens.T, d_shared, preferred_element_type=jnp.float32).astype(jnp.bfloat16)
    grad_value = jnp.dot(flat_tokens.T, d_value, preferred_element_type=jnp.float32).astype(jnp.bfloat16)
    return attention, grad_tokens, grad_shared, grad_value
```

```python
import jax
import jax.numpy as jnp
from jax import lax
from jax.experimental import pallas as pl
from jax.experimental.pallas import tpu as pltpu
from jax.sharding import Mesh
from jax.sharding import PartitionSpec as P

F32 = jnp.float32
BF16 = jnp.bfloat16
HEADS = 6
HEAD = 64
ROWS = 256
LOCAL = 128
WIDTH = 768
PROJ = 384
UNUSED = 65536.0
PLANE = ("y", "c")
TOK = ("y", "z", "c")


def iota(shape, dim):
    return lax.broadcasted_iota(jnp.int32, shape, dim)


def dot(a, b, dims=((1,), (0,))):
    return lax.dot_general(a, b, (dims, ((), ())), preferred_element_type=F32)


def send_kernel(tok_ref, ws_ref, wv_ref, cluster_ref, cot_ref, out_ref, dest_ref):
    tokens = tok_ref[...]
    shared = dot(tokens, ws_ref[...]).astype(BF16)
    value = dot(tokens, wv_ref[...]).astype(BF16)
    cot = cot_ref[...]
    sub = iota((LOCAL, LOCAL), 0)
    lane = iota((LOCAL, LOCAL), 1)
    sub_rows = iota((ROWS, LOCAL), 0)
    lane_rows = iota((ROWS, LOCAL), 1)
    blank = jnp.zeros((LOCAL, HEAD), BF16)
    pending = None
    for h in range(HEADS):
        cluster = cluster_ref[h : h + 1, :]
        member = (sub == cluster).astype(BF16)
        same = dot(member, member, ((0,), (0,)))
        order = jnp.sum(jnp.where(sub < lane, same, 0.0), axis=0, keepdims=True)
        dest = cluster * 2 + order.astype(jnp.int32)
        dest_ref[h : h + 1, :] = dest
        hit = sub_rows == dest
        used = jnp.sum(jnp.where(hit, 1.0, 0.0), axis=1, keepdims=True)
        cols = slice(h * HEAD, (h + 1) * HEAD)
        tail = [cot[:, cols], blank] if h % 2 == 0 else [blank, cot[:, cols]]
        packed = jnp.concatenate([shared[:, cols], value[:, cols]] + tail, axis=1)
        moved = dot(hit.astype(BF16), packed)
        mark = (lane_rows == 0) & (used < 0.5)
        out_ref[h] = jnp.where(mark, UNUSED, moved[:, :LOCAL]).astype(BF16)
        if h % 2 == 0:
            pending = moved[:, LOCAL:]
        else:
            out_ref[HEADS + h // 2] = (pending + moved[:, LOCAL:]).astype(BF16)


def attend_kernel(in_ref, out_ref):
    lane_rows = iota((ROWS, LOCAL), 1)
    causal = iota((ROWS, ROWS), 1) <= iota((ROWS, ROWS), 0)
    pending = None
    for h in range(HEADS):
        block = in_ref[h]
        empty = block[:, :1].astype(F32) > 32768.0
        first = lane_rows == 0
        block = jnp.where(empty & first, 0.0, block.astype(F32)).astype(BF16)
        shared = block[:, :HEAD]
        value = block[:, HEAD:]
        pair = in_ref[HEADS + h // 2]
        cot = pair[:, :HEAD] if h % 2 == 0 else pair[:, HEAD:]
        bias_lane = lane_rows == HEAD
        head_lanes = lane_rows < HEAD
        wide = block.astype(F32)
        query = jnp.where(head_lanes, wide, jnp.where(bias_lane, 1.0, 0.0)).astype(BF16)
        key = jnp.where(
            head_lanes, wide, jnp.where(bias_lane & empty, -1e30, 0.0)
        ).astype(BF16)
        scores = dot(query, key, ((1,), (1,))) * 0.125
        scores = jnp.where(causal, scores, -1e30)
        highest = jnp.max(scores, axis=1, keepdims=True)
        weights = jnp.exp(scores - highest)
        probs = (weights / jnp.sum(weights, axis=1, keepdims=True)).astype(BF16)
        out = dot(probs, value)
        d_prob = dot(cot, value, ((1,), (1,)))
        wide_probs = probs.astype(F32)
        delta = jnp.sum(wide_probs * d_prob, axis=1, keepdims=True)
        d_score = (wide_probs * (d_prob - delta)).astype(BF16)
        both = dot(d_score, shared) + dot(d_score, shared, ((0,), (0,)))
        d_shared = (both * 0.125).astype(BF16)
        d_value = dot(probs, cot, ((0,), (0,))).astype(BF16)
        out_ref[h] = jnp.concatenate([d_shared, d_value], axis=1)
        if h % 2 == 0:
            pending = out.astype(BF16)
        else:
            out_ref[HEADS + h // 2] = jnp.concatenate([pending, out.astype(BF16)], axis=1)


def return_kernel(in_ref, dest_ref, ws_ref, wv_ref, att_ref, grad_ref, dt_ref):
    sub_rows = iota((ROWS, LOCAL), 0)
    lane = iota((LOCAL, LOCAL), 1)
    d_shared = []
    d_value = []
    pending = None
    for h in range(HEADS):
        route = (sub_rows == dest_ref[h : h + 1, :]).astype(BF16)
        block = in_ref[h]
        turned = dot(block, route, ((0,), (0,))).astype(BF16)
        dt_ref[h * HEAD : (h + 1) * HEAD, :] = turned[:HEAD]
        dt_ref[PROJ + h * HEAD : PROJ + (h + 1) * HEAD, :] = turned[HEAD:]
        rows = dot(route, block, ((0,), (0,))).astype(BF16)
        d_shared.append(rows[:, :HEAD])
        d_value.append(rows[:, HEAD:])
        pair = dot(route, in_ref[HEADS + h // 2], ((0,), (0,)))
        if h % 2 == 0:
            pending = pair
        else:
            k = h // 2
            att_ref[:, k * LOCAL : (k + 1) * LOCAL] = jnp.where(
                lane < HEAD, pending, pair
            ).astype(BF16)
    left = jnp.concatenate(d_shared, axis=1)
    right = jnp.concatenate(d_value, axis=1)
    total = dot(left, ws_ref[...], ((1,), (1,))) + dot(right, wv_ref[...], ((1,), (1,)))
    grad_ref[...] = total.astype(BF16)


def partial_kernel(dt_ref, tok_ref, out_ref):
    total = dot(dt_ref[0], tok_ref[0])
    for s in range(1, dt_ref.shape[0]):
        total = total + dot(dt_ref[s], tok_ref[s])
    part = total.astype(BF16)
    columns = part.shape[0]
    for k in range(WIDTH // LOCAL):
        out_ref[k * columns : (k + 1) * columns, :] = part[:, k * LOCAL : (k + 1) * LOCAL]


def call(kernel, out, *args):
    return pl.pallas_call(
        kernel,
        out_shape=out,
        compiler_params=pltpu.CompilerParams(vmem_limit_bytes=48 * 1024 * 1024),
    )(*args)


def shape(*dims):
    return jax.ShapeDtypeStruct(dims, BF16)


def swap(rows, axes):
    return lax.all_to_all(rows, axes, split_axis=0, concat_axis=0, tiled=True)


def body(tokens, w_shared, w_value, cluster_ids, slot_index, cotangent):
    rows = tokens[0]
    plane_rows = lax.all_gather(rows, PLANE, axis=0, tiled=False)
    sent, dest = call(
        send_kernel,
        (shape(9, ROWS, LOCAL), jax.ShapeDtypeStruct((HEADS, LOCAL), jnp.int32)),
        rows,
        w_shared,
        w_value,
        cluster_ids[0],
        cotangent[0],
    )

    def route(blocks):
        split = blocks.reshape(9, LOCAL, 2, LOCAL)
        moved = lax.all_to_all(split, TOK, split_axis=1, concat_axis=1, tiled=True)
        return moved.reshape(9, ROWS, LOCAL)

    worked = call(attend_kernel, shape(9, ROWS, LOCAL), route(sent))
    attention, grad_tokens, turned = call(
        return_kernel,
        (shape(LOCAL, PROJ), shape(LOCAL, WIDTH), shape(WIDTH, LOCAL)),
        route(worked),
        dest,
        w_shared,
        w_value,
    )
    columns = WIDTH // 8
    mixed = swap(turned.reshape(8, columns, LOCAL), PLANE)
    part = call(partial_kernel, shape(6 * columns, LOCAL), mixed, plane_rows)
    pieces = swap(part.reshape(64, 9, LOCAL), ("x", "z"))
    piece = jnp.sum(pieces.astype(F32), axis=0).astype(BF16)
    block = swap(jnp.broadcast_to(piece[None], (64, 9, LOCAL)), ("x", "z"))
    block = block.reshape(1, 6 * columns, LOCAL)
    whole = swap(jnp.broadcast_to(block, (8, 6 * columns, LOCAL)), PLANE)
    whole = whole.reshape(8, 6, columns, LOCAL).transpose(1, 3, 0, 2).reshape(WIDTH, WIDTH)
    return (attention[None], grad_tokens[None], whole[:, :PROJ], whole[:, PROJ:])


def solution(mesh):
    fine = Mesh(mesh.devices.reshape(4, 4, 16, 2), ("x", "y", "z", "c"))
    in_specs = (
        P("x", TOK, None),
        P(),
        P(),
        P("x", None, TOK),
        P("x", None, TOK),
        P("x", TOK, None),
    )
    out_specs = (P("x", TOK, None), P("x", TOK, None), P(), P())
    return jax.shard_map(body, mesh=fine, in_specs=in_specs, out_specs=out_specs, check_vma=False)
```

```python
import jax
import jax.numpy as jnp
from jax import lax
from jax.experimental import pallas as pl
from jax.experimental.pallas import tpu as pltpu
from jax.sharding import Mesh
from jax.sharding import PartitionSpec as P

F32 = jnp.float32
BF16 = jnp.bfloat16
HEADS = 6
HEAD = 64
ROWS = 256
LOCAL = 128
WIDTH = 768
PROJ = 384
UNUSED = 65536.0
PLANE = ("y", "c")
TOK = ("y", "zh", "zl", "c")
STEPS = [(dy, dc) for dy in range(4) for dc in range(2)]
COLUMNS = 96
PIECE = 36
SLOT = 40


def iota(shape, dim):
    return lax.broadcasted_iota(jnp.int32, shape, dim)


def dot(a, b, dims=((1,), (0,))):
    return lax.dot_general(a, b, (dims, ((), ())), preferred_element_type=F32)


def send_kernel(*refs):
    sources, (out_ref, dest_ref), targets, sems = refs[:5], refs[5:7], refs[7:12], refs[12]
    copies = [
        pltpu.make_async_copy(source, target, sems.at[n])
        for n, (source, target) in enumerate(zip(sources, targets))
    ]
    for copy in copies:
        copy.start()
    tok_ref, ws_ref, wv_ref, cluster_ref, cot_ref = targets
    for copy in copies:
        copy.wait()
    tokens = tok_ref[...]
    shared = dot(tokens, ws_ref[...]).astype(BF16)
    value = dot(tokens, wv_ref[...]).astype(BF16)
    cot = cot_ref[...]
    sub = iota((LOCAL, LOCAL), 0)
    lane = iota((LOCAL, LOCAL), 1)
    sub_rows = iota((ROWS, LOCAL), 0)
    lane_rows = iota((ROWS, LOCAL), 1)
    blank = jnp.zeros((LOCAL, HEAD), BF16)
    pending = None
    for h in range(HEADS):
        cluster = cluster_ref[h]
        member = (sub == cluster).astype(BF16)
        same = dot(member, member, ((0,), (0,)))
        order = jnp.sum(jnp.where(sub < lane, same, 0.0), axis=0, keepdims=True)
        dest = cluster * 2 + order.astype(jnp.int32)
        dest_ref[h : h + 1, :] = dest
        hit = sub_rows == dest
        used = jnp.sum(jnp.where(hit, 1.0, 0.0), axis=1, keepdims=True)
        cols = slice(h * HEAD, (h + 1) * HEAD)
        tail = [cot[:, cols], blank] if h % 2 == 0 else [blank, cot[:, cols]]
        packed = jnp.concatenate([shared[:, cols], value[:, cols]] + tail, axis=1)
        moved = dot(hit.astype(BF16), packed)
        mark = (lane_rows == 0) & (used < 0.5)
        out_ref[h] = jnp.where(mark, UNUSED, moved[:, :LOCAL]).astype(BF16)
        if h % 2 == 0:
            pending = moved[:, LOCAL:]
        else:
            out_ref[HEADS + h // 2] = (pending + moved[:, LOCAL:]).astype(BF16)


def attend_kernel(in_ref, out_ref):
    lane_rows = iota((ROWS, LOCAL), 1)
    causal = iota((ROWS, ROWS), 1) <= iota((ROWS, ROWS), 0)
    pending = None
    for h in range(HEADS):
        block = in_ref[h]
        empty = block[:, :1].astype(F32) > 32768.0
        first = lane_rows == 0
        block = jnp.where(empty & first, 0.0, block.astype(F32)).astype(BF16)
        shared = block[:, :HEAD]
        value = block[:, HEAD:]
        pair = in_ref[HEADS + h // 2]
        cot = pair[:, :HEAD] if h % 2 == 0 else pair[:, HEAD:]
        bias_lane = lane_rows == HEAD
        head_lanes = lane_rows < HEAD
        wide = block.astype(F32)
        query = jnp.where(head_lanes, wide, jnp.where(bias_lane, 1.0, 0.0)).astype(BF16)
        key = jnp.where(
            head_lanes, wide, jnp.where(bias_lane & empty, -1e30, 0.0)
        ).astype(BF16)
        scores = dot(query, key, ((1,), (1,))) * 0.125
        scores = jnp.where(causal, scores, -1e30)
        highest = jnp.max(scores, axis=1, keepdims=True)
        weights = jnp.exp(scores - highest)
        probs = (weights / jnp.sum(weights, axis=1, keepdims=True)).astype(BF16)
        out = dot(probs, value)
        d_prob = dot(cot, value, ((1,), (1,)))
        wide_probs = probs.astype(F32)
        delta = jnp.sum(wide_probs * d_prob, axis=1, keepdims=True)
        d_score = (wide_probs * (d_prob - delta)).astype(BF16)
        both = dot(d_score, shared) + dot(d_score, shared, ((0,), (0,)))
        d_shared = (both * 0.125).astype(BF16)
        d_value = dot(probs, cot, ((0,), (0,))).astype(BF16)
        out_ref[h] = jnp.concatenate([d_shared, d_value], axis=1)
        if h % 2 == 0:
            pending = out.astype(BF16)
        else:
            out_ref[HEADS + h // 2] = jnp.concatenate([pending, out.astype(BF16)], axis=1)


def return_kernel(in_ref, dest_ref, ws_ref, wv_ref, att_ref, grad_ref, dt_ref):
    sub_rows = iota((ROWS, LOCAL), 0)
    lane = iota((LOCAL, LOCAL), 1)
    d_shared = []
    d_value = []
    pending = None
    for h in range(HEADS):
        route = (sub_rows == dest_ref[h : h + 1, :]).astype(BF16)
        block = in_ref[h]
        dt_ref[h * LOCAL : (h + 1) * LOCAL, :] = dot(block, route, ((0,), (0,))).astype(BF16)
        rows = dot(route, block, ((0,), (0,))).astype(BF16)
        d_shared.append(rows[:, :HEAD])
        d_value.append(rows[:, HEAD:])
        pair = dot(route, in_ref[HEADS + h // 2], ((0,), (0,)))
        if h % 2 == 0:
            pending = pair
        else:
            k = h // 2
            att_ref[:, k * LOCAL : (k + 1) * LOCAL] = jnp.where(
                lane < HEAD, pending, pair
            ).astype(BF16)
    left = jnp.concatenate(d_shared, axis=1)
    right = jnp.concatenate(d_value, axis=1)
    total = dot(left, ws_ref[...], ((1,), (1,))) + dot(right, wv_ref[...], ((1,), (1,)))
    grad_ref[...] = total.astype(BF16)


def partial_kernel(place_ref, dt_ref, *refs):
    tok_refs, out_ref, scratch = refs[:8], refs[8], refs[9]
    total = None
    for n, (dy, dc) in enumerate(STEPS):
        source = lax.rem(place_ref[0] + 4 - dy, 4) * 2 + lax.rem(place_ref[1] + dc, 2)
        term = dot(dt_ref[source], tok_refs[n][...])
        total = term if total is None else total + term
    for k in range(WIDTH // LOCAL):
        scratch[k * COLUMNS : (k + 1) * COLUMNS, :] = total[:, k * LOCAL : (k + 1) * LOCAL]
    scratch[16 * PIECE :, :] = jnp.zeros((8, LOCAL), F32)
    for i in range(16):
        out_ref[i] = scratch[i * PIECE : i * PIECE + SLOT, :].astype(BF16)


def sum_kernel(in_ref, out_ref):
    total = in_ref[0].astype(F32)
    for i in range(1, in_ref.shape[0]):
        total = total + in_ref[i].astype(F32)
    total = total.astype(BF16)
    for i in range(out_ref.shape[0]):
        out_ref[i] = total


def finish_kernel(place_ref, mine_ref, other_ref, shared_ref, value_ref, scratch):
    here = place_ref[1]
    for y in range(4):
        for i in range(16):
            rows = slice(i * PIECE, (i + 1) * PIECE)
            scratch[here, y, rows, :] = mine_ref[y * 16 + i].astype(F32)[:PIECE]
            scratch[1 - here, y, rows, :] = other_ref[y * 16 + i].astype(F32)[:PIECE]
    for k in range(WIDTH // LOCAL):
        first = k * COLUMNS
        strip = [scratch[j % 2, j // 2, first : first + COLUMNS, :] for j in range(8)]
        strip = jnp.concatenate(strip, axis=0)
        for half, ref in enumerate((shared_ref, value_ref)):
            heads = [
                strip[h * LOCAL + half * HEAD : h * LOCAL + (half + 1) * HEAD]
                for h in range(HEADS)
            ]
            ref[k * LOCAL : (k + 1) * LOCAL, :] = jnp.concatenate(heads, axis=0).T.astype(BF16)


def call(kernel, out, *args, scratch=(), scalars=0, held=False):
    space = pl.ANY if held else pltpu.VMEM
    limit = (60 if held else 48) * 1024 * 1024
    specs = [pl.BlockSpec(memory_space=pltpu.SMEM)] * scalars
    specs += [pl.BlockSpec(memory_space=space)] * (len(args) - scalars)
    return pl.pallas_call(
        kernel,
        out_shape=out,
        in_specs=specs,
        scratch_shapes=scratch,
        compiler_params=pltpu.CompilerParams(vmem_limit_bytes=limit),
    )(*args)


def shape(*dims):
    return jax.ShapeDtypeStruct(dims, BF16)


def swap(rows, axes):
    return lax.all_to_all(rows, axes, split_axis=0, concat_axis=0, tiled=True)


def body(tokens, w_shared, w_value, cluster_ids, slot_index, cotangent):
    rows = tokens[0]
    place = jnp.stack([lax.axis_index("y"), lax.axis_index("c")]).astype(jnp.int32)
    sent, dest = call(
        send_kernel,
        (shape(9, ROWS, LOCAL), jax.ShapeDtypeStruct((HEADS, LOCAL), jnp.int32)),
        rows,
        w_shared,
        w_value,
        cluster_ids.transpose(1, 0, 2),
        cotangent[0],
        scratch=[
            pltpu.VMEM((LOCAL, WIDTH), BF16),
            pltpu.VMEM((WIDTH, PROJ), BF16),
            pltpu.VMEM((WIDTH, PROJ), BF16),
            pltpu.VMEM((HEADS, 1, LOCAL), jnp.int32),
            pltpu.VMEM((LOCAL, PROJ), BF16),
            pltpu.SemaphoreType.DMA((5,)),
        ],
        held=True,
    )

    def route(blocks):
        split = blocks.reshape(9, LOCAL, 2, LOCAL)
        moved = lax.all_to_all(split, TOK, split_axis=1, concat_axis=1, tiled=True)
        return moved.reshape(9, ROWS, LOCAL)

    plane_rows = []
    for dy, dc in STEPS[1:]:
        pairs = [
            (y * 2 + c, (y + dy) % 4 * 2 + (c + dc) % 2) for y in range(4) for c in range(2)
        ]
        plane_rows.append(lax.ppermute(rows, PLANE, pairs))
    worked = call(attend_kernel, shape(9, ROWS, LOCAL), route(sent))
    attention, grad_tokens, turned = call(
        return_kernel,
        (shape(LOCAL, PROJ), shape(LOCAL, WIDTH), shape(WIDTH, LOCAL)),
        route(worked),
        dest,
        w_shared,
        w_value,
    )
    mixed = swap(turned.reshape(8, COLUMNS, LOCAL), PLANE)
    part = call(
        partial_kernel,
        shape(16, SLOT, LOCAL),
        place,
        mixed,
        rows,
        *plane_rows,
        scratch=[pltpu.VMEM((16 * PIECE + 8, LOCAL), F32)],
        scalars=1,
    )
    part = call(sum_kernel, shape(4, SLOT, LOCAL), swap(part, ("x", "zl")))
    block = call(sum_kernel, shape(64, SLOT, LOCAL), swap(part, "zh"))
    block = swap(block, ("y", "x", "zl"))
    other = lax.ppermute(block, "c", [(0, 1), (1, 0)])
    grad_shared, grad_value = call(
        finish_kernel,
        (shape(WIDTH, PROJ), shape(WIDTH, PROJ)),
        place,
        block,
        other,
        scratch=[pltpu.VMEM((2, 4, 16 * PIECE, LOCAL), F32)],
        scalars=1,
    )
    return (attention[None], grad_tokens[None], grad_shared, grad_value)


def solution(mesh):
    fine = Mesh(mesh.devices.reshape(4, 4, 4, 4, 2), ("x", "y", "zh", "zl", "c"))
    in_specs = (
        P("x", TOK, None),
        P(),
        P(),
        P("x", None, TOK),
        P("x", None, TOK),
        P("x", TOK, None),
    )
    out_specs = (P("x", TOK, None), P("x", TOK, None), P(), P())
    return jax.shard_map(body, mesh=fine, in_specs=in_specs, out_specs=out_specs, check_vma=False)
```

```python
import jax
import jax.numpy as jnp
from jax import lax
from jax.experimental import pallas as pl
from jax.experimental.pallas import tpu as pltpu
from jax.sharding import Mesh
from jax.sharding import PartitionSpec as P

F32 = jnp.float32
BF16 = jnp.bfloat16
HEADS = 6
HEAD = 64
ROWS = 256
LOCAL = 128
WIDTH = 768
PROJ = 384
UNUSED = 65536.0
PLANE = ("y", "c")
TOK = ("y", "zh", "zl", "c")
OWNERS = ("y", "c", "zh", "zl")
STEPS = [(dy, dc) for dy in range(4) for dc in range(2)]
COLUMNS = 96
PIECE = 36
SLOT = 40
BLOCK = 16


def iota(shape, dim):
    return lax.broadcasted_iota(jnp.int32, shape, dim)


def dot(a, b, dims=((1,), (0,))):
    return lax.dot_general(a, b, (dims, ((), ())), preferred_element_type=F32)


def send_kernel(*refs):
    sources, (out_ref, ext_ref), targets, sems = refs[:5], refs[5:7], refs[7:12], refs[12]
    copies = [
        pltpu.make_async_copy(source, target, sems.at[n])
        for n, (source, target) in enumerate(zip(sources, targets))
    ]
    for copy in copies:
        copy.start()
    tok_ref, ws_ref, wv_ref, cluster_ref, cot_ref = targets
    for copy in copies:
        copy.wait()
    tokens = tok_ref[...]
    ext_ref[:LOCAL, :] = tokens
    shared = dot(tokens, ws_ref[...]).astype(BF16)
    value = dot(tokens, wv_ref[...]).astype(BF16)
    cot = cot_ref[...]
    sub = iota((LOCAL, LOCAL), 0)
    lane = iota((LOCAL, LOCAL), 1)
    sub_rows = iota((ROWS, LOCAL), 0)
    lane_rows = iota((ROWS, LOCAL), 1)
    blank = jnp.zeros((LOCAL, HEAD), BF16)
    pending = None
    for h in range(HEADS):
        cluster = cluster_ref[h]
        member = (sub == cluster).astype(BF16)
        same = dot(member, member, ((0,), (0,)))
        order = jnp.sum(jnp.where(sub < lane, same, 0.0), axis=0, keepdims=True)
        owner = (cluster & 96) + (cluster & 1) * 16 + ((cluster >> 1) & 15)
        dest = owner * 2 + order.astype(jnp.int32)
        ext_ref[LOCAL:, h * LOCAL : (h + 1) * LOCAL] = jnp.broadcast_to(
            dest.astype(F32), (16, LOCAL)
        ).astype(BF16)
        hit = sub_rows == dest
        used = jnp.sum(jnp.where(hit, 1.0, 0.0), axis=1, keepdims=True)
        cols = slice(h * HEAD, (h + 1) * HEAD)
        tail = [cot[:, cols], blank] if h % 2 == 0 else [blank, cot[:, cols]]
        packed = jnp.concatenate([shared[:, cols], value[:, cols]] + tail, axis=1)
        moved = dot(hit.astype(BF16), packed)
        mark = (lane_rows == 0) & (used < 0.5)
        out_ref[h] = jnp.where(mark, UNUSED, moved[:, :LOCAL]).astype(BF16)
        if h % 2 == 0:
            pending = moved[:, LOCAL:]
        else:
            out_ref[HEADS + h // 2] = (pending + moved[:, LOCAL:]).astype(BF16)


def position(row):
    return (row & 192) + ((row >> 1) & 15) * 4 + ((row >> 5) & 1) * 2 + (row & 1)


def spread(block, slot):
    rows = block.shape[0] // 8
    turned = [block[:rows]]
    for p in range(1, 8):
        turned.append(pltpu.roll(block[p * rows : (p + 1) * rows], BLOCK * p, 1))
    parts = []
    for m in range(8):
        part = turned[-m % 8]
        for q in range(1, 8):
            part = jnp.where(slot == q, turned[(q - m) % 8], part)
        parts.append(part)
    return parts


def attend_kernel(in_ref, out_ref):
    lane_rows = iota((ROWS, LOCAL), 1)
    causal = position(iota((ROWS, ROWS), 1)) <= position(iota((ROWS, ROWS), 0))
    slot = iota((ROWS // 8, LOCAL), 1) >> 4
    pending = None
    for h in range(HEADS):
        block = in_ref[h]
        empty = block[:, :1].astype(F32) > 32768.0
        first = lane_rows == 0
        block = jnp.where(empty & first, 0.0, block.astype(F32)).astype(BF16)
        shared = block[:, :HEAD]
        value = block[:, HEAD:]
        pair = in_ref[HEADS + h // 2]
        cot = pair[:, :HEAD] if h % 2 == 0 else pair[:, HEAD:]
        bias_lane = lane_rows == HEAD
        head_lanes = lane_rows < HEAD
        wide = block.astype(F32)
        query = jnp.where(head_lanes, wide, jnp.where(bias_lane, 1.0, 0.0)).astype(BF16)
        key = jnp.where(
            head_lanes, wide, jnp.where(bias_lane & empty, -1e30, 0.0)
        ).astype(BF16)
        scores = dot(query, key, ((1,), (1,))) * 0.125
        scores = jnp.where(causal, scores, -1e30)
        highest = jnp.max(scores, axis=1, keepdims=True)
        weights = jnp.exp(scores - highest)
        probs = (weights / jnp.sum(weights, axis=1, keepdims=True)).astype(BF16)
        out = dot(probs, value)
        d_prob = dot(cot, value, ((1,), (1,)))
        wide_probs = probs.astype(F32)
        delta = jnp.sum(wide_probs * d_prob, axis=1, keepdims=True)
        d_score = (wide_probs * (d_prob - delta)).astype(BF16)
        both = dot(d_score, shared) + dot(d_score, shared, ((0,), (0,)))
        d_value = dot(probs, cot, ((0,), (0,)))
        for m, part in enumerate(spread(jnp.concatenate([both * 0.125, d_value], axis=1), slot)):
            n = h * 8 + m
            out_ref[n // 6 * 9 + n % 6] = part.astype(BF16)
        if h % 2 == 0:
            pending = out
        else:
            for m, part in enumerate(spread(jnp.concatenate([pending, out], axis=1), slot)):
                n = h // 2 * 8 + m
                out_ref[n // 3 * 9 + 6 + n % 3] = part.astype(BF16)


def index_of(place_ref, dy, dc):
    return lax.rem(place_ref[0] + dy, 4) * 2 + lax.rem(place_ref[1] + dc, 2)


def gather_columns(place_ref, in_ref, base, count, turn, exts, dests, out_ref, first):
    j = place_ref[0] * 2 + place_ref[1]
    head = (j * 3 // 4, (j * 6 + 5) // 8)
    lane_slot = iota((ROWS, LOCAL), 1) >> 4
    sub_rows = iota((ROWS, LOCAL), 0).astype(F32)
    for n, (dy, dc) in enumerate(STEPS):
        source = index_of(place_ref, 4 - dy, dc)
        for i in range(2):
            lanes = pl.ds(pl.multiple_of(head[i] * LOCAL, LOCAL), LOCAL)
            dests[i, source] = exts[n][LOCAL:, lanes].astype(F32)[:8]
    shift = lax.rem(j * turn, 8) * BLOCK
    turned = [pltpu.roll(in_ref[base + b].astype(F32), shift, 1) for b in range(count)]
    limit = lax.rem(j, 4)
    limit = jnp.where(limit == 1, 1, jnp.where(limit == 2, 2, 3)) * count
    for p in range(8):
        rows = turned[0]
        for b in range(1, count):
            rows = jnp.where(lane_slot == (b + p) % 8, turned[b], rows)
        rows = rows.astype(BF16)
        found = [
            dot(rows, (sub_rows == dests[i, p, :1]).astype(BF16), ((0,), (0,))) for i in range(2)
        ]
        blocks = []
        for b in range(count):
            cut = slice((b + p) % 8 * BLOCK, ((b + p) % 8 + 1) * BLOCK)
            blocks.append(jnp.where(b * 3 < limit, found[0][cut], found[1][cut]))
        out_ref[p, first : first + count * BLOCK, :] = jnp.concatenate(blocks, axis=0).astype(BF16)


def partial_kernel(place_ref, in_ref, *refs):
    exts, (out_ref, cols_ref), (dests, scratch) = refs[:8], refs[8:10], refs[10:]
    gather_columns(place_ref, in_ref, 0, 6, 2, exts, dests, cols_ref, 0)
    total = None
    for n, (dy, dc) in enumerate(STEPS):
        source = index_of(place_ref, 4 - dy, dc)
        term = dot(cols_ref[source], exts[n][:LOCAL, :])
        total = term if total is None else total + term
    for k in range(WIDTH // LOCAL):
        scratch[k * COLUMNS : (k + 1) * COLUMNS, :] = total[:, k * LOCAL : (k + 1) * LOCAL]
    scratch[16 * PIECE :, :] = jnp.zeros((8, LOCAL), F32)
    for i in range(16):
        out_ref[i] = scratch[i * PIECE : i * PIECE + SLOT, :].astype(BF16)


def forward_kernel(place_ref, in_ref, cols_ref, *refs):
    exts, outs, (dests, scratch) = refs[:8], refs[8:16], refs[16:]
    gather_columns(place_ref, in_ref, 6, 3, 5, exts, dests, scratch, 0)
    for n, (dy, dc) in enumerate(STEPS):
        target = index_of(place_ref, dy, dc)
        outs[n][:COLUMNS, :] = cols_ref[target]
        outs[n][COLUMNS:, :] = scratch[target]


def return_kernel(place_ref, *refs):
    parts, (ws_ref, wv_ref), (att_ref, grad_ref), held = refs[:8], refs[8:10], refs[10:12], refs[12]
    for n, (dy, dc) in enumerate(STEPS):
        held[index_of(place_ref, 4 - dy, dc)] = parts[n][...]

    def columns(blocks, per, first):
        rows = [
            held[n // per, first + n % per * BLOCK : first + (n % per + 1) * BLOCK, :]
            for n in blocks
        ]
        return jnp.concatenate(rows, axis=0).astype(F32).T.astype(BF16)

    left = columns([h * 8 + m for h in range(HEADS) for m in range(4)], 6, 0)
    right = columns([h * 8 + 4 + m for h in range(HEADS) for m in range(4)], 6, 0)
    att_ref[...] = columns(range(24), 3, COLUMNS)
    total = dot(left, ws_ref[...], ((1,), (1,))) + dot(right, wv_ref[...], ((1,), (1,)))
    grad_ref[...] = total.astype(BF16)


def sum_kernel(in_ref, out_ref):
    total = in_ref[0].astype(F32)
    for i in range(1, in_ref.shape[0]):
        total = total + in_ref[i].astype(F32)
    total = total.astype(BF16)
    for i in range(out_ref.shape[0]):
        out_ref[i] = total


def finish_kernel(place_ref, mine_ref, other_ref, shared_ref, value_ref, scratch):
    here = place_ref[1]
    for y in range(4):
        for i in range(16):
            rows = slice(i * PIECE, (i + 1) * PIECE)
            scratch[here, y, rows, :] = mine_ref[y * 16 + i].astype(F32)[:PIECE]
            scratch[1 - here, y, rows, :] = other_ref[y * 16 + i].astype(F32)[:PIECE]
    for k in range(WIDTH // LOCAL):
        first = k * COLUMNS
        strip = [scratch[j % 2, j // 2, first : first + COLUMNS, :] for j in range(8)]
        strip = jnp.concatenate(strip, axis=0)
        for half, ref in enumerate((shared_ref, value_ref)):
            heads = [
                strip[h * LOCAL + half * HEAD : h * LOCAL + (half + 1) * HEAD]
                for h in range(HEADS)
            ]
            ref[k * LOCAL : (k + 1) * LOCAL, :] = jnp.concatenate(heads, axis=0).T.astype(BF16)


def call(kernel, out, *args, scratch=(), scalars=0, held=False):
    space = pl.ANY if held else pltpu.VMEM
    limit = (60 if held else 48) * 1024 * 1024
    specs = [pl.BlockSpec(memory_space=pltpu.SMEM)] * scalars
    specs += [pl.BlockSpec(memory_space=space)] * (len(args) - scalars)
    return pl.pallas_call(
        kernel,
        out_shape=out,
        in_specs=specs,
        scratch_shapes=scratch,
        compiler_params=pltpu.CompilerParams(vmem_limit_bytes=limit),
    )(*args)


def shape(*dims):
    return jax.ShapeDtypeStruct(dims, BF16)


def swap(rows, axes):
    return lax.all_to_all(rows, axes, split_axis=0, concat_axis=0, tiled=True)


def body(tokens, w_shared, w_value, cluster_ids, slot_index, cotangent):
    rows = tokens[0]
    place = jnp.stack([lax.axis_index("y"), lax.axis_index("c")]).astype(jnp.int32)
    sent, ext = call(
        send_kernel,
        (shape(9, ROWS, LOCAL), shape(LOCAL + 16, WIDTH)),
        rows,
        w_shared,
        w_value,
        cluster_ids.transpose(1, 0, 2),
        cotangent[0],
        scratch=[
            pltpu.VMEM((LOCAL, WIDTH), BF16),
            pltpu.VMEM((WIDTH, PROJ), BF16),
            pltpu.VMEM((WIDTH, PROJ), BF16),
            pltpu.VMEM((HEADS, 1, LOCAL), jnp.int32),
            pltpu.VMEM((LOCAL, PROJ), BF16),
            pltpu.SemaphoreType.DMA((5,)),
        ],
        held=True,
    )

    def exchange(mine):
        parts = []
        for part, (dy, dc) in zip(mine, STEPS):
            pairs = [
                (y * 2 + c, (y + dy) % 4 * 2 + (c + dc) % 2) for y in range(4) for c in range(2)
            ]
            parts.append(lax.ppermute(part, PLANE, pairs) if dy or dc else part)
        return parts

    arrived = swap(sent.reshape(9, LOCAL, 2, LOCAL).transpose(1, 0, 2, 3), OWNERS)
    arrived = arrived.transpose(1, 0, 2, 3)
    worked = call(attend_kernel, shape(72, 32, LOCAL), arrived.reshape(9, ROWS, LOCAL))
    worked = worked.reshape(8, 9, 16, 2, LOCAL).transpose(0, 2, 1, 3, 4)
    back = swap(worked.reshape(LOCAL, 9, 2, LOCAL), OWNERS)
    back = back.transpose(1, 0, 2, 3).reshape(9, ROWS, LOCAL)
    exts = exchange([ext] * 8)
    part, cols = call(
        partial_kernel,
        (shape(16, SLOT, LOCAL), shape(8, COLUMNS, LOCAL)),
        place,
        back,
        *exts,
        scratch=[pltpu.VMEM((2, 8, 8, LOCAL), F32), pltpu.VMEM((16 * PIECE + 8, LOCAL), F32)],
        scalars=1,
    )
    parts = call(
        forward_kernel,
        tuple(shape(COLUMNS * 3 // 2, LOCAL) for _ in STEPS),
        place,
        back,
        cols,
        *exts,
        scratch=[pltpu.VMEM((2, 8, 8, LOCAL), F32), pltpu.VMEM((8, COLUMNS // 2, LOCAL), BF16)],
        scalars=1,
    )
    part = call(sum_kernel, shape(4, SLOT, LOCAL), swap(part, ("x", "zl")))
    part, parts = lax.optimization_barrier((part, parts))
    block = call(sum_kernel, shape(64, SLOT, LOCAL), swap(part, "zh"))
    block, parts = lax.optimization_barrier((block, exchange(parts)))
    attention, grad_tokens = call(
        return_kernel,
        (shape(LOCAL, PROJ), shape(LOCAL, WIDTH)),
        place,
        *parts,
        w_shared,
        w_value,
        scratch=[pltpu.VMEM((8, COLUMNS * 3 // 2, LOCAL), BF16)],
        scalars=1,
    )
    block = swap(block, ("y", "x", "zl"))
    block, attention, grad_tokens = lax.optimization_barrier((block, attention, grad_tokens))
    other = lax.ppermute(block, "c", [(0, 1), (1, 0)])
    grad_shared, grad_value = call(
        finish_kernel,
        (shape(WIDTH, PROJ), shape(WIDTH, PROJ)),
        place,
        block,
        other,
        scratch=[pltpu.VMEM((2, 4, 16 * PIECE, LOCAL), F32)],
        scalars=1,
    )
    return (attention[None], grad_tokens[None], grad_shared, grad_value)


def solution(mesh):
    fine = Mesh(mesh.devices.reshape(4, 4, 4, 4, 2), ("x", "y", "zh", "zl", "c"))
    in_specs = (
        P("x", TOK, None),
        P(),
        P(),
        P("x", None, TOK),
        P("x", None, TOK),
        P("x", TOK, None),
    )
    out_specs = (P("x", TOK, None), P("x", TOK, None), P(), P())
    return jax.shard_map(body, mesh=fine, in_specs=in_specs, out_specs=out_specs, check_vma=False)
```

```python
import jax
import jax.numpy as jnp
from jax import lax
from jax.experimental import pallas as pl
from jax.experimental.pallas import tpu as pltpu
from jax.sharding import Mesh
from jax.sharding import PartitionSpec as P

F32 = jnp.float32
BF16 = jnp.bfloat16
HEADS = 6
HEAD = 64
ROWS = 256
LOCAL = 128
WIDTH = 768
PROJ = 384
UNUSED = 65536.0
PLANE = ("y", "c")
TOK = ("y", "zh", "zl", "c")
OWNERS = ("y", "c", "zh", "zl")
STEPS = [(dy, dc) for dy in range(4) for dc in range(2)]
COLUMNS = 96
PIECE = 36
SLOT = 40
BLOCK = 16
WHOLE = 576
MESSAGE = 144


def iota(shape, dim):
    return lax.broadcasted_iota(jnp.int32, shape, dim)


def dot(a, b, dims=((1,), (0,))):
    return lax.dot_general(a, b, (dims, ((), ())), preferred_element_type=F32)


def send_kernel(*refs):
    sources, (out_ref, ext_ref), targets, sems = refs[:5], refs[5:7], refs[7:12], refs[12]
    copies = [
        pltpu.make_async_copy(source, target, sems.at[n])
        for n, (source, target) in enumerate(zip(sources, targets))
    ]
    for copy in copies:
        copy.start()
    tok_ref, ws_ref, wv_ref, cluster_ref, cot_ref = targets
    for copy in copies:
        copy.wait()
    tokens = tok_ref[...]
    ext_ref[:LOCAL, :] = tokens
    shared = dot(tokens, ws_ref[...]).astype(BF16)
    value = dot(tokens, wv_ref[...]).astype(BF16)
    cot = cot_ref[...]
    sub = iota((LOCAL, LOCAL), 0)
    lane = iota((LOCAL, LOCAL), 1)
    sub_rows = iota((ROWS, LOCAL), 0)
    lane_rows = iota((ROWS, LOCAL), 1)
    blank = jnp.zeros((LOCAL, HEAD), BF16)
    pending = None
    for h in range(HEADS):
        cluster = cluster_ref[h]
        member = (sub == cluster).astype(BF16)
        same = dot(member, member, ((0,), (0,)))
        order = jnp.sum(jnp.where(sub < lane, same, 0.0), axis=0, keepdims=True)
        owner = (cluster & 96) + (cluster & 1) * 16 + ((cluster >> 1) & 15)
        dest = owner * 2 + order.astype(jnp.int32)
        ext_ref[LOCAL:, h * LOCAL : (h + 1) * LOCAL] = jnp.broadcast_to(
            dest.astype(F32), (16, LOCAL)
        ).astype(BF16)
        hit = sub_rows == dest
        used = jnp.sum(jnp.where(hit, 1.0, 0.0), axis=1, keepdims=True)
        cols = slice(h * HEAD, (h + 1) * HEAD)
        tail = [cot[:, cols], blank] if h % 2 == 0 else [blank, cot[:, cols]]
        packed = jnp.concatenate([shared[:, cols], value[:, cols]] + tail, axis=1)
        moved = dot(hit.astype(BF16), packed)
        mark = (lane_rows == 0) & (used < 0.5)
        out_ref[h] = jnp.where(mark, UNUSED, moved[:, :LOCAL]).astype(BF16)
        if h % 2 == 0:
            pending = moved[:, LOCAL:]
        else:
            out_ref[HEADS + h // 2] = (pending + moved[:, LOCAL:]).astype(BF16)


def position(row):
    return (row & 192) + ((row >> 1) & 15) * 4 + ((row >> 5) & 1) * 2 + (row & 1)


def spread(block, slot):
    rows = block.shape[0] // 8
    turned = [block[:rows]]
    for p in range(1, 8):
        turned.append(pltpu.roll(block[p * rows : (p + 1) * rows], BLOCK * p, 1))
    parts = []
    for m in range(8):
        part = turned[-m % 8]
        for q in range(1, 8):
            part = jnp.where(slot == q, turned[(q - m) % 8], part)
        parts.append(part)
    return parts


def attend_kernel(in_ref, out_ref):
    lane_rows = iota((ROWS, LOCAL), 1)
    causal = position(iota((ROWS, ROWS), 1)) <= position(iota((ROWS, ROWS), 0))
    slot = iota((ROWS // 8, LOCAL), 1) >> 4
    pending = None
    for h in range(HEADS):
        block = in_ref[h]
        empty = block[:, :1].astype(F32) > 32768.0
        first = lane_rows == 0
        block = jnp.where(empty & first, 0.0, block.astype(F32)).astype(BF16)
        shared = block[:, :HEAD]
        value = block[:, HEAD:]
        pair = in_ref[HEADS + h // 2]
        cot = pair[:, :HEAD] if h % 2 == 0 else pair[:, HEAD:]
        bias_lane = lane_rows == HEAD
        head_lanes = lane_rows < HEAD
        wide = block.astype(F32)
        query = jnp.where(head_lanes, wide, jnp.where(bias_lane, 1.0, 0.0)).astype(BF16)
        key = jnp.where(
            head_lanes, wide, jnp.where(bias_lane & empty, -1e30, 0.0)
        ).astype(BF16)
        scores = dot(query, key, ((1,), (1,))) * 0.125
        scores = jnp.where(causal, scores, -1e30)
        highest = jnp.max(scores, axis=1, keepdims=True)
        weights = jnp.exp(scores - highest)
        probs = (weights / jnp.sum(weights, axis=1, keepdims=True)).astype(BF16)
        out = dot(probs, value)
        d_prob = dot(cot, value, ((1,), (1,)))
        wide_probs = probs.astype(F32)
        delta = jnp.sum(wide_probs * d_prob, axis=1, keepdims=True)
        d_score = (wide_probs * (d_prob - delta)).astype(BF16)
        both = dot(d_score, shared) + dot(d_score, shared, ((0,), (0,)))
        d_value = dot(probs, cot, ((0,), (0,)))
        for m, part in enumerate(spread(jnp.concatenate([both * 0.125, d_value], axis=1), slot)):
            n = h * 8 + m
            out_ref[n // 6 * 9 + n % 6] = part.astype(BF16)
        if h % 2 == 0:
            pending = out
        else:
            for m, part in enumerate(spread(jnp.concatenate([pending, out], axis=1), slot)):
                n = h // 2 * 8 + m
                out_ref[n // 3 * 9 + 6 + n % 3] = part.astype(BF16)


def index_of(place_ref, dy, dc):
    return lax.rem(place_ref[0] + dy, 4) * 2 + lax.rem(place_ref[1] + dc, 2)


def gather_columns(place_ref, in_ref, base, count, turn, exts, dests, out_ref, first):
    j = place_ref[0] * 2 + place_ref[1]
    head = (j * 3 // 4, (j * 6 + 5) // 8)
    lane_slot = iota((ROWS, LOCAL), 1) >> 4
    sub_rows = iota((ROWS, LOCAL), 0).astype(F32)
    for n, (dy, dc) in enumerate(STEPS):
        source = index_of(place_ref, 4 - dy, dc)
        for i in range(2):
            lanes = pl.ds(pl.multiple_of(head[i] * LOCAL, LOCAL), LOCAL)
            dests[i, source] = exts[n][LOCAL:, lanes].astype(F32)[:8]
    shift = lax.rem(j * turn, 8) * BLOCK
    turned = [pltpu.roll(in_ref[base + b].astype(F32), shift, 1) for b in range(count)]
    limit = lax.rem(j, 4)
    limit = jnp.where(limit == 1, 1, jnp.where(limit == 2, 2, 3)) * count
    for p in range(8):
        rows = turned[0]
        for b in range(1, count):
            rows = jnp.where(lane_slot == (b + p) % 8, turned[b], rows)
        rows = rows.astype(BF16)
        found = [
            dot(rows, (sub_rows == dests[i, p, :1]).astype(BF16), ((0,), (0,))) for i in range(2)
        ]
        blocks = []
        for b in range(count):
            cut = slice((b + p) % 8 * BLOCK, ((b + p) % 8 + 1) * BLOCK)
            blocks.append(jnp.where(b * 3 < limit, found[0][cut], found[1][cut]))
        out_ref[p, first : first + count * BLOCK, :] = jnp.concatenate(blocks, axis=0).astype(BF16)


def partial_kernel(place_ref, in_ref, *refs):
    exts, (out_ref, cols_ref), (dests, scratch) = refs[:8], refs[8:10], refs[10:]
    gather_columns(place_ref, in_ref, 0, 6, 2, exts, dests, cols_ref, 0)
    total = None
    for n, (dy, dc) in enumerate(STEPS):
        source = index_of(place_ref, 4 - dy, dc)
        term = dot(cols_ref[source], exts[n][:LOCAL, :])
        total = term if total is None else total + term
    for k in range(WIDTH // LOCAL):
        scratch[k * COLUMNS : (k + 1) * COLUMNS, :] = total[:, k * LOCAL : (k + 1) * LOCAL]
    scratch[16 * PIECE :, :] = jnp.zeros((8, LOCAL), F32)
    for i in range(16):
        out_ref[i] = scratch[i * PIECE : i * PIECE + SLOT, :].astype(BF16)


def forward_kernel(place_ref, in_ref, cols_ref, *refs):
    exts, (keep_ref, give_ref), (dests, scratch) = refs[:8], refs[8:10], refs[10:]
    gather_columns(place_ref, in_ref, 6, 3, 5, exts, dests, scratch, 0)
    here = place_ref[1]
    for y in range(4):
        for ref, c in ((keep_ref, here), (give_ref, 1 - here)):
            ref[y, :COLUMNS, :] = cols_ref[y * 2 + c]
            ref[y, COLUMNS:, :] = scratch[y * 2 + c]


def pack_kernel(block_ref, keep_ref, got_ref, out_ref, scratch):
    for i in range(16):
        scratch[i * PIECE : (i + 1) * PIECE, :] = block_ref[i].astype(F32)[:PIECE]
    block = scratch[...].astype(BF16)
    for y in range(4):
        out_ref[y, :WHOLE, :] = block
        out_ref[y, WHOLE : WHOLE + MESSAGE, :] = keep_ref[y]
        out_ref[y, WHOLE + MESSAGE :, :] = got_ref[y]


def return_kernel(place_ref, all_ref, ws_ref, wv_ref, att_ref, grad_ref, held):
    here = place_ref[1]
    for y in range(4):
        held[y * 2 + here] = all_ref[y, WHOLE : WHOLE + MESSAGE, :]
        held[y * 2 + 1 - here] = all_ref[y, WHOLE + MESSAGE :, :]

    def columns(blocks, per, first):
        rows = [
            held[n // per, first + n % per * BLOCK : first + (n % per + 1) * BLOCK, :]
            for n in blocks
        ]
        return jnp.concatenate(rows, axis=0).astype(F32).T.astype(BF16)

    left = columns([h * 8 + m for h in range(HEADS) for m in range(4)], 6, 0)
    right = columns([h * 8 + 4 + m for h in range(HEADS) for m in range(4)], 6, 0)
    att_ref[...] = columns(range(24), 3, COLUMNS)
    total = dot(left, ws_ref[...], ((1,), (1,))) + dot(right, wv_ref[...], ((1,), (1,)))
    grad_ref[...] = total.astype(BF16)


def sum_kernel(in_ref, out_ref):
    total = in_ref[0].astype(F32)
    for i in range(1, in_ref.shape[0]):
        total = total + in_ref[i].astype(F32)
    total = total.astype(BF16)
    for i in range(out_ref.shape[0]):
        out_ref[i] = total


def finish_kernel(place_ref, mine_ref, other_ref, shared_ref, value_ref):
    first = place_ref[1] == 0
    for k in range(WIDTH // LOCAL):
        rows = slice(k * COLUMNS, (k + 1) * COLUMNS)
        strip = []
        for y in range(4):
            mine = mine_ref[y, rows, :].astype(F32)
            other = other_ref[y, rows, :].astype(F32)
            strip += [jnp.where(first, mine, other), jnp.where(first, other, mine)]
        strip = jnp.concatenate(strip, axis=0)
        for half, ref in enumerate((shared_ref, value_ref)):
            heads = [
                strip[h * LOCAL + half * HEAD : h * LOCAL + (half + 1) * HEAD]
                for h in range(HEADS)
            ]
            ref[k * LOCAL : (k + 1) * LOCAL, :] = jnp.concatenate(heads, axis=0).T.astype(BF16)


def call(kernel, out, *args, scratch=(), scalars=0, held=False):
    space = pl.ANY if held else pltpu.VMEM
    limit = (60 if held else 48) * 1024 * 1024
    specs = [pl.BlockSpec(memory_space=pltpu.SMEM)] * scalars
    specs += [pl.BlockSpec(memory_space=space)] * (len(args) - scalars)
    return pl.pallas_call(
        kernel,
        out_shape=out,
        in_specs=specs,
        scratch_shapes=scratch,
        compiler_params=pltpu.CompilerParams(vmem_limit_bytes=limit),
    )(*args)


def shape(*dims):
    return jax.ShapeDtypeStruct(dims, BF16)


def swap(rows, axes):
    return lax.all_to_all(rows, axes, split_axis=0, concat_axis=0, tiled=True)


def body(tokens, w_shared, w_value, cluster_ids, slot_index, cotangent):
    rows = tokens[0]
    place = jnp.stack([lax.axis_index("y"), lax.axis_index("c")]).astype(jnp.int32)
    sent, ext = call(
        send_kernel,
        (shape(9, ROWS, LOCAL), shape(LOCAL + 16, WIDTH)),
        rows,
        w_shared,
        w_value,
        cluster_ids.transpose(1, 0, 2),
        cotangent[0],
        scratch=[
            pltpu.VMEM((LOCAL, WIDTH), BF16),
            pltpu.VMEM((WIDTH, PROJ), BF16),
            pltpu.VMEM((WIDTH, PROJ), BF16),
            pltpu.VMEM((HEADS, 1, LOCAL), jnp.int32),
            pltpu.VMEM((LOCAL, PROJ), BF16),
            pltpu.SemaphoreType.DMA((5,)),
        ],
        held=True,
    )

    def shift(part, dy, dc):
        pairs = [(y * 2 + c, (y + dy) % 4 * 2 + (c + dc) % 2) for y in range(4) for c in range(2)]
        return lax.ppermute(part, PLANE, pairs) if dy or dc else part

    arrived = swap(sent.reshape(9, LOCAL, 2, LOCAL).transpose(1, 0, 2, 3), OWNERS)
    early = [shift(ext, dy, dc) for dy, dc in STEPS[:5]]
    arrived, ext, early = lax.optimization_barrier((arrived, ext, early))
    exts = early + [shift(ext, dy, dc) for dy, dc in STEPS[5:]]
    arrived = arrived.transpose(1, 0, 2, 3)
    worked = call(attend_kernel, shape(72, 32, LOCAL), arrived.reshape(9, ROWS, LOCAL))
    worked = worked.reshape(8, 9, 16, 2, LOCAL).transpose(0, 2, 1, 3, 4)
    back = swap(worked.reshape(LOCAL, 9, 2, LOCAL), OWNERS)
    back = back.transpose(1, 0, 2, 3).reshape(9, ROWS, LOCAL)
    part, cols = call(
        partial_kernel,
        (shape(16, SLOT, LOCAL), shape(8, COLUMNS, LOCAL)),
        place,
        back,
        *exts,
        scratch=[pltpu.VMEM((2, 8, 8, LOCAL), F32), pltpu.VMEM((16 * PIECE + 8, LOCAL), F32)],
        scalars=1,
    )
    keep, give = call(
        forward_kernel,
        (shape(4, MESSAGE, LOCAL), shape(4, MESSAGE, LOCAL)),
        place,
        back,
        cols,
        *exts,
        scratch=[pltpu.VMEM((2, 8, 8, LOCAL), F32), pltpu.VMEM((8, COLUMNS // 2, LOCAL), BF16)],
        scalars=1,
    )
    got = lax.ppermute(give, "c", [(0, 1), (1, 0)])
    part = swap(part, ("x", "zl"))
    part, keep, got = lax.optimization_barrier((part, keep, got))
    part = call(sum_kernel, shape(4, SLOT, LOCAL), part)
    block = call(sum_kernel, shape(16, SLOT, LOCAL), swap(part, "zh"))
    block = swap(block, ("x", "zl"))
    block = call(
        pack_kernel,
        shape(4, WHOLE + 2 * MESSAGE, LOCAL),
        block,
        keep,
        got,
        scratch=[pltpu.VMEM((WHOLE, LOCAL), F32)],
    )
    block = swap(block, "y")
    other = lax.ppermute(block, "c", [(0, 1), (1, 0)])
    attention, grad_tokens = call(
        return_kernel,
        (shape(LOCAL, PROJ), shape(LOCAL, WIDTH)),
        place,
        block,
        w_shared,
        w_value,
        scratch=[pltpu.VMEM((8, MESSAGE, LOCAL), BF16)],
        scalars=1,
    )
    grad_shared, grad_value = call(
        finish_kernel,
        (shape(WIDTH, PROJ), shape(WIDTH, PROJ)),
        place,
        block,
        other,
        scalars=1,
    )
    return (attention[None], grad_tokens[None], grad_shared, grad_value)


def solution(mesh):
    fine = Mesh(mesh.devices.reshape(4, 4, 4, 4, 2), ("x", "y", "zh", "zl", "c"))
    in_specs = (
        P("x", TOK, None),
        P(),
        P(),
        P("x", None, TOK),
        P("x", None, TOK),
        P("x", TOK, None),
    )
    out_specs = (P("x", TOK, None), P("x", TOK, None), P(), P())
    return jax.shard_map(body, mesh=fine, in_specs=in_specs, out_specs=out_specs, check_vma=False)
```

```python
import jax
import jax.numpy as jnp
from jax import lax
from jax.experimental import pallas as pl
from jax.experimental.pallas import tpu as pltpu
from jax.sharding import Mesh
from jax.sharding import PartitionSpec as P

F32 = jnp.float32
BF16 = jnp.bfloat16
HEADS = 6
HEAD = 64
ROWS = 256
LOCAL = 128
WIDTH = 768
PROJ = 384
UNUSED = 65536.0
PLANE = ("y", "c")
TOK = ("y", "zh", "zl", "c")
OWNERS = ("y", "c", "zh", "zl")
STEPS = [(dy, dc) for dy in range(4) for dc in range(2)]
COLUMNS = 96
PIECE = 36
SLOT = 40
BLOCK = 16
MESSAGE = 144


def iota(shape, dim):
    return lax.broadcasted_iota(jnp.int32, shape, dim)


def dot(a, b, dims=((1,), (0,))):
    return lax.dot_general(a, b, (dims, ((), ())), preferred_element_type=F32)


def send_kernel(*refs):
    sources, (out_ref, ext_ref), targets, sems = refs[:5], refs[5:7], refs[7:12], refs[12]
    copies = [
        pltpu.make_async_copy(source, target, sems.at[n])
        for n, (source, target) in enumerate(zip(sources, targets))
    ]
    for copy in copies:
        copy.start()
    cluster_ref, tok_ref, ws_ref, wv_ref, cot_ref = targets
    sub = iota((LOCAL, LOCAL), 0)
    lane = iota((LOCAL, LOCAL), 1)
    sub_rows = iota((ROWS, LOCAL), 0)
    lane_rows = iota((ROWS, LOCAL), 1)
    copies[0].wait()
    hits = []
    marks = []
    for h in range(HEADS):
        cluster = cluster_ref[h]
        member = (sub == cluster).astype(BF16)
        same = dot(member, member, ((0,), (0,)))
        order = jnp.sum(jnp.where(sub < lane, same, 0.0), axis=0, keepdims=True)
        owner = (cluster & 96) + (cluster & 1) * 16 + ((cluster >> 1) & 15)
        dest = owner * 2 + order.astype(jnp.int32)
        ext_ref[LOCAL:, h * LOCAL : (h + 1) * LOCAL] = jnp.broadcast_to(
            dest.astype(F32), (16, LOCAL)
        ).astype(BF16)
        hit = sub_rows == dest
        used = jnp.sum(jnp.where(hit, 1.0, 0.0), axis=1, keepdims=True)
        hits.append(hit.astype(BF16))
        marks.append(jnp.where((lane_rows == 0) & (used < 0.5), UNUSED, 0.0))
    for copy in copies[1:]:
        copy.wait()
    tokens = tok_ref[...]
    ext_ref[:LOCAL, :] = tokens
    shared = dot(tokens, ws_ref[...]).astype(BF16)
    value = dot(tokens, wv_ref[...]).astype(BF16)
    cot = cot_ref[...]
    blank = jnp.zeros((LOCAL, HEAD), BF16)
    pending = None
    for h in range(HEADS):
        cols = slice(h * HEAD, (h + 1) * HEAD)
        tail = [cot[:, cols], blank] if h % 2 == 0 else [blank, cot[:, cols]]
        packed = jnp.concatenate([shared[:, cols], value[:, cols]] + tail, axis=1)
        moved = dot(hits[h], packed)
        out_ref[h] = (moved[:, :LOCAL] + marks[h]).astype(BF16)
        if h % 2 == 0:
            pending = moved[:, LOCAL:]
        else:
            out_ref[HEADS + h // 2] = (pending + moved[:, LOCAL:]).astype(BF16)


def position(row):
    return (row & 192) + ((row >> 1) & 15) * 4 + ((row >> 5) & 1) * 2 + (row & 1)


def spread(block, slot):
    rows = block.shape[0] // 8
    turned = [block[:rows]]
    for p in range(1, 8):
        turned.append(pltpu.roll(block[p * rows : (p + 1) * rows], BLOCK * p, 1))
    parts = []
    for m in range(8):
        part = turned[-m % 8]
        for q in range(1, 8):
            part = jnp.where(slot == q, turned[(q - m) % 8], part)
        parts.append(part)
    return parts


def attend_kernel(in_ref, out_ref):
    lane_rows = iota((ROWS, LOCAL), 1)
    causal = position(iota((ROWS, ROWS), 1)) <= position(iota((ROWS, ROWS), 0))
    slot = iota((ROWS // 8, LOCAL), 1) >> 4
    pending = None
    for h in range(HEADS):
        block = in_ref[h]
        empty = block[:, :1].astype(F32) > 32768.0
        first = lane_rows == 0
        block = jnp.where(empty & first, 0.0, block.astype(F32)).astype(BF16)
        shared = block[:, :HEAD]
        value = block[:, HEAD:]
        pair = in_ref[HEADS + h // 2]
        cot = pair[:, :HEAD] if h % 2 == 0 else pair[:, HEAD:]
        bias_lane = lane_rows == HEAD
        head_lanes = lane_rows < HEAD
        wide = block.astype(F32)
        query = jnp.where(head_lanes, wide, jnp.where(bias_lane, 1.0, 0.0)).astype(BF16)
        key = jnp.where(
            head_lanes, wide, jnp.where(bias_lane & empty, -1e30, 0.0)
        ).astype(BF16)
        scores = dot(query, key, ((1,), (1,))) * 0.125
        scores = jnp.where(causal, scores, -1e30)
        highest = jnp.max(scores, axis=1, keepdims=True)
        weights = jnp.exp(scores - highest)
        probs = (weights / jnp.sum(weights, axis=1, keepdims=True)).astype(BF16)
        out = dot(probs, value)
        d_prob = dot(cot, value, ((1,), (1,)))
        wide_probs = probs.astype(F32)
        delta = jnp.sum(wide_probs * d_prob, axis=1, keepdims=True)
        d_score = (wide_probs * (d_prob - delta)).astype(BF16)
        both = dot(d_score, shared) + dot(d_score, shared, ((0,), (0,)))
        d_value = dot(probs, cot, ((0,), (0,)))
        for m, part in enumerate(spread(jnp.concatenate([both * 0.125, d_value], axis=1), slot)):
            n = h * 8 + m
            out_ref[n // 6 * 9 + n % 6] = part.astype(BF16)
        if h % 2 == 0:
            pending = out
        else:
            for m, part in enumerate(spread(jnp.concatenate([pending, out], axis=1), slot)):
                n = h // 2 * 8 + m
                out_ref[n // 3 * 9 + 6 + n % 3] = part.astype(BF16)


def index_of(place_ref, dy, dc):
    return lax.rem(place_ref[0] + dy, 4) * 2 + lax.rem(place_ref[1] + dc, 2)


def gather_columns(place_ref, in_ref, base, count, turn, exts, dests, out_ref, first):
    j = place_ref[0] * 2 + place_ref[1]
    head = (j * 3 // 4, (j * 6 + 5) // 8)
    lane_slot = iota((ROWS, LOCAL), 1) >> 4
    sub_rows = iota((ROWS, LOCAL), 0).astype(F32)
    for n, (dy, dc) in enumerate(STEPS):
        source = index_of(place_ref, 4 - dy, dc)
        for i in range(2):
            lanes = pl.ds(pl.multiple_of(head[i] * LOCAL, LOCAL), LOCAL)
            dests[i, source] = exts[n // 2][n % 2, LOCAL:, lanes].astype(F32)[:8]
    shift = lax.rem(j * turn, 8) * BLOCK
    turned = [pltpu.roll(in_ref[base + b].astype(F32), shift, 1) for b in range(count)]
    limit = lax.rem(j, 4)
    limit = jnp.where(limit == 1, 1, jnp.where(limit == 2, 2, 3)) * count
    for p in range(8):
        rows = turned[0]
        for b in range(1, count):
            rows = jnp.where(lane_slot == (b + p) % 8, turned[b], rows)
        rows = rows.astype(BF16)
        found = [
            dot(rows, (sub_rows == dests[i, p, :1]).astype(BF16), ((0,), (0,))) for i in range(2)
        ]
        blocks = []
        for b in range(count):
            cut = slice((b + p) % 8 * BLOCK, ((b + p) % 8 + 1) * BLOCK)
            blocks.append(jnp.where(b * 3 < limit, found[0][cut], found[1][cut]))
        out_ref[p, first : first + count * BLOCK, :] = jnp.concatenate(blocks, axis=0).astype(BF16)


def partial_kernel(place_ref, in_ref, *refs):
    exts, (out_ref, cols_ref), (dests, scratch) = refs[:4], refs[4:6], refs[6:]
    gather_columns(place_ref, in_ref, 0, 6, 2, exts, dests, cols_ref, 0)
    total = None
    for n, (dy, dc) in enumerate(STEPS):
        source = index_of(place_ref, 4 - dy, dc)
        term = dot(cols_ref[source], exts[n // 2][n % 2, :LOCAL, :])
        total = term if total is None else total + term
    for k in range(WIDTH // LOCAL):
        scratch[k * COLUMNS : (k + 1) * COLUMNS, :] = total[:, k * LOCAL : (k + 1) * LOCAL]
    scratch[16 * PIECE :, :] = jnp.zeros((8, LOCAL), F32)
    for i in range(16):
        out_ref[i] = scratch[i * PIECE : i * PIECE + SLOT, :].astype(BF16)


def forward_kernel(place_ref, in_ref, cols_ref, *refs):
    exts, (keep_ref, give_ref), (dests, scratch) = refs[:4], refs[4:6], refs[6:]
    gather_columns(place_ref, in_ref, 6, 3, 5, exts, dests, scratch, 0)
    here = place_ref[1]
    for y in range(4):
        for ref, c in ((keep_ref, here), (give_ref, 1 - here)):
            ref[y, :COLUMNS, :] = cols_ref[y * 2 + c]
            ref[y, COLUMNS:, :] = scratch[y * 2 + c]


def pack_kernel(in_ref, keep_ref, give_ref, out_ref):
    total = in_ref[0].astype(F32)
    for i in range(1, 4):
        total = total + in_ref[i].astype(F32)
    total = jnp.concatenate([total, jnp.zeros((8, LOCAL), F32)], axis=0).astype(BF16)
    for y in range(4):
        out_ref[y, :MESSAGE, :] = keep_ref[y]
        out_ref[y, MESSAGE : 2 * MESSAGE, :] = give_ref[y]
        out_ref[y, 2 * MESSAGE :, :] = total


def repeat_kernel(all_ref, out_ref, keep_ref, give_ref, scratch):
    for y in range(4):
        keep_ref[y] = all_ref[y, :MESSAGE, :]
        give_ref[y] = all_ref[y, MESSAGE : 2 * MESSAGE, :]
        piece = all_ref[y, 2 * MESSAGE :, :].astype(F32)
        scratch[y * PIECE : (y + 1) * PIECE, :] = piece[:PIECE]
    block = scratch[...].astype(BF16)
    for i in range(16):
        out_ref[i] = block


def return_kernel(place_ref, keep_ref, got_ref, ws_ref, wv_ref, att_ref, grad_ref, held):
    here = place_ref[1]
    for y in range(4):
        held[y * 2 + here] = keep_ref[y]
        held[y * 2 + 1 - here] = got_ref[y]

    def columns(blocks, per, first):
        rows = [
            held[n // per, first + n % per * BLOCK : first + (n % per + 1) * BLOCK, :]
            for n in blocks
        ]
        return jnp.concatenate(rows, axis=0).astype(F32).T.astype(BF16)

    left = columns([h * 8 + m for h in range(HEADS) for m in range(4)], 6, 0)
    right = columns([h * 8 + 4 + m for h in range(HEADS) for m in range(4)], 6, 0)
    att_ref[...] = columns(range(24), 3, COLUMNS)
    total = dot(left, ws_ref[...], ((1,), (1,))) + dot(right, wv_ref[...], ((1,), (1,)))
    grad_ref[...] = total.astype(BF16)


def sum_kernel(in_ref, out_ref):
    total = in_ref[0].astype(F32)
    for i in range(1, in_ref.shape[0]):
        total = total + in_ref[i].astype(F32)
    total = total.astype(BF16)
    for i in range(out_ref.shape[0]):
        out_ref[i] = total


def finish_kernel(place_ref, mine_ref, other_ref, shared_ref, value_ref, wide, scratch):
    here = place_ref[1]
    for i in range(16):
        wide[0, i] = mine_ref[i].astype(F32)
        wide[1, i] = other_ref[i].astype(F32)
    for y in range(4):
        for i in range(16):
            rows = slice(i * PIECE, (i + 1) * PIECE)
            scratch[here, y, rows, :] = wide[0, i, y * PIECE : (y + 1) * PIECE, :]
            scratch[1 - here, y, rows, :] = wide[1, i, y * PIECE : (y + 1) * PIECE, :]
    for k in range(WIDTH // LOCAL):
        first = k * COLUMNS
        strip = [scratch[j % 2, j // 2, first : first + COLUMNS, :] for j in range(8)]
        strip = jnp.concatenate(strip, axis=0)
        for half, ref in enumerate((shared_ref, value_ref)):
            heads = [
                strip[h * LOCAL + half * HEAD : h * LOCAL + (half + 1) * HEAD]
                for h in range(HEADS)
            ]
            ref[k * LOCAL : (k + 1) * LOCAL, :] = jnp.concatenate(heads, axis=0).T.astype(BF16)


def call(kernel, out, *args, scratch=(), scalars=0, held=False):
    space = pl.ANY if held else pltpu.VMEM
    if held:
        args = [pltpu.with_memory_space_constraint(arg, pltpu.HBM) for arg in args]
    specs = [pl.BlockSpec(memory_space=pltpu.SMEM)] * scalars
    specs += [pl.BlockSpec(memory_space=space)] * (len(args) - scalars)
    return pl.pallas_call(
        kernel,
        out_shape=out,
        in_specs=specs,
        scratch_shapes=scratch,
        compiler_params=pltpu.CompilerParams(vmem_limit_bytes=48 * 1024 * 1024),
    )(*args)


def shape(*dims):
    return jax.ShapeDtypeStruct(dims, BF16)


def swap(rows, axes):
    return lax.all_to_all(rows, axes, split_axis=0, concat_axis=0, tiled=True)


def body(tokens, w_shared, w_value, cluster_ids, slot_index, cotangent):
    rows = tokens[0]
    place = jnp.stack([lax.axis_index("y"), lax.axis_index("c")]).astype(jnp.int32)
    sent, ext = call(
        send_kernel,
        (shape(9, ROWS, LOCAL), shape(LOCAL + 16, WIDTH)),
        cluster_ids.transpose(1, 0, 2),
        rows,
        w_shared,
        w_value,
        cotangent[0],
        scratch=[
            pltpu.VMEM((HEADS, 1, LOCAL), jnp.int32),
            pltpu.VMEM((LOCAL, WIDTH), BF16),
            pltpu.VMEM((WIDTH, PROJ), BF16),
            pltpu.VMEM((WIDTH, PROJ), BF16),
            pltpu.VMEM((LOCAL, PROJ), BF16),
            pltpu.SemaphoreType.DMA((5,)),
        ],
        held=True,
    )

    def shift(pair, dy):
        return lax.ppermute(pair, "y", [(y, (y + dy) % 4) for y in range(4)])

    def flip(part):
        return lax.ppermute(part, "c", [(0, 1), (1, 0)])

    arrived = swap(sent.reshape(9, LOCAL, 2, LOCAL).transpose(1, 0, 2, 3), OWNERS)
    pair = jnp.stack([ext, flip(ext)])
    exts = [pair] + [shift(pair, dy) for dy in range(1, 4)]
    arrived, exts, place = lax.optimization_barrier((arrived, exts, place))
    arrived = arrived.transpose(1, 0, 2, 3)
    worked = call(attend_kernel, shape(72, 32, LOCAL), arrived.reshape(9, ROWS, LOCAL))
    worked = worked.reshape(8, 9, 16, 2, LOCAL).transpose(0, 2, 1, 3, 4)
    back = swap(worked.reshape(LOCAL, 9, 2, LOCAL), OWNERS)
    back = back.transpose(1, 0, 2, 3).reshape(9, ROWS, LOCAL)
    part, cols = call(
        partial_kernel,
        (shape(16, SLOT, LOCAL), shape(8, COLUMNS, LOCAL)),
        place,
        back,
        *exts,
        scratch=[pltpu.VMEM((2, 8, 8, LOCAL), F32), pltpu.VMEM((16 * PIECE + 8, LOCAL), F32)],
        scalars=1,
    )
    keep, give = call(
        forward_kernel,
        (shape(4, MESSAGE, LOCAL), shape(4, MESSAGE, LOCAL)),
        place,
        back,
        cols,
        *exts,
        scratch=[pltpu.VMEM((2, 8, 8, LOCAL), F32), pltpu.VMEM((8, COLUMNS // 2, LOCAL), BF16)],
        scalars=1,
    )
    part, keep, give = lax.optimization_barrier((swap(part, ("x", "zl")), keep, give))
    part = swap(call(sum_kernel, shape(4, SLOT, LOCAL), part), "zh")
    block = swap(call(pack_kernel, shape(4, 2 * MESSAGE + 48, LOCAL), part, keep, give), "y")
    pieces, keep, give = call(
        repeat_kernel,
        (shape(16, 4 * PIECE, LOCAL), shape(4, MESSAGE, LOCAL), shape(4, MESSAGE, LOCAL)),
        block,
        scratch=[pltpu.VMEM((4 * PIECE, LOCAL), F32)],
    )
    attention, grad_tokens = call(
        return_kernel,
        (shape(LOCAL, PROJ), shape(LOCAL, WIDTH)),
        place,
        keep,
        flip(give),
        w_shared,
        w_value,
        scratch=[pltpu.VMEM((8, MESSAGE, LOCAL), BF16)],
        scalars=1,
    )
    pieces = swap(pieces, ("x", "zl"))
    pieces, attention, grad_tokens = lax.optimization_barrier((pieces, attention, grad_tokens))
    grad_shared, grad_value = call(
        finish_kernel,
        (shape(WIDTH, PROJ), shape(WIDTH, PROJ)),
        place,
        pieces,
        flip(pieces),
        scratch=[
            pltpu.VMEM((2, 16, 4 * PIECE, LOCAL), F32),
            pltpu.VMEM((2, 4, 16 * PIECE, LOCAL), F32),
        ],
        scalars=1,
    )
    return (attention[None], grad_tokens[None], grad_shared, grad_value)


def solution(mesh):
    fine = Mesh(mesh.devices.reshape(4, 4, 4, 4, 2), ("x", "y", "zh", "zl", "c"))
    in_specs = (
        P("x", TOK, None),
        P(),
        P(),
        P("x", None, TOK),
        P("x", None, TOK),
        P("x", TOK, None),
    )
    out_specs = (P("x", TOK, None), P("x", TOK, None), P(), P())
    return jax.shard_map(body, mesh=fine, in_specs=in_specs, out_specs=out_specs, check_vma=False)
```

```python
import jax
import jax.numpy as jnp
from jax import lax
from jax.experimental import pallas as pl
from jax.experimental.pallas import tpu as pltpu
from jax.sharding import Mesh
from jax.sharding import PartitionSpec as P

F32 = jnp.float32
BF16 = jnp.bfloat16
HEADS = 6
HEAD = 64
ROWS = 256
LOCAL = 128
WIDTH = 768
PROJ = 384
UNUSED = 65536.0
PLANE = ("y", "c")
TOK = ("y", "zh", "zl", "c")
OWNERS = ("y", "c", "zh", "zl")
STEPS = [(dy, dc) for dy in range(4) for dc in range(2)]
COLUMNS = 96
PIECE = 36
SLOT = 40
BLOCK = 16
WHOLE = 576
MESSAGE = 144


def iota(shape, dim):
    return lax.broadcasted_iota(jnp.int32, shape, dim)


def dot(a, b, dims=((1,), (0,))):
    return lax.dot_general(a, b, (dims, ((), ())), preferred_element_type=F32)


def send_kernel(*refs):
    sources, (out_ref, ext_ref), targets, sems = refs[:5], refs[5:7], refs[7:12], refs[12]
    copies = [
        pltpu.make_async_copy(source, target, sems.at[n])
        for n, (source, target) in enumerate(zip(sources, targets))
    ]
    for copy in copies:
        copy.start()
    cluster_ref, tok_ref, ws_ref, wv_ref, cot_ref = targets
    sub = iota((LOCAL, LOCAL), 0)
    lane = iota((LOCAL, LOCAL), 1)
    sub_rows = iota((ROWS, LOCAL), 0)
    lane_rows = iota((ROWS, LOCAL), 1)
    copies[0].wait()
    hits = []
    marks = []
    for h in range(HEADS):
        cluster = cluster_ref[h]
        member = (sub == cluster).astype(BF16)
        same = dot(member, member, ((0,), (0,)))
        order = jnp.sum(jnp.where(sub < lane, same, 0.0), axis=0, keepdims=True)
        owner = (cluster & 96) + (cluster & 1) * 16 + ((cluster >> 1) & 15)
        dest = owner * 2 + order.astype(jnp.int32)
        ext_ref[LOCAL:, h * LOCAL : (h + 1) * LOCAL] = jnp.broadcast_to(
            dest.astype(F32), (16, LOCAL)
        ).astype(BF16)
        hit = sub_rows == dest
        used = jnp.sum(jnp.where(hit, 1.0, 0.0), axis=1, keepdims=True)
        hits.append(hit.astype(BF16))
        marks.append(jnp.where((lane_rows == 0) & (used < 0.5), UNUSED, 0.0))
    for copy in copies[1:]:
        copy.wait()
    tokens = tok_ref[...]
    ext_ref[:LOCAL, :] = tokens
    shared = dot(tokens, ws_ref[...]).astype(BF16)
    value = dot(tokens, wv_ref[...]).astype(BF16)
    cot = cot_ref[...]
    blank = jnp.zeros((LOCAL, HEAD), BF16)
    pending = None
    for h in range(HEADS):
        cols = slice(h * HEAD, (h + 1) * HEAD)
        tail = [cot[:, cols], blank] if h % 2 == 0 else [blank, cot[:, cols]]
        packed = jnp.concatenate([shared[:, cols], value[:, cols]] + tail, axis=1)
        moved = dot(hits[h], packed)
        out_ref[h] = (moved[:, :LOCAL] + marks[h]).astype(BF16)
        if h % 2 == 0:
            pending = moved[:, LOCAL:]
        else:
            out_ref[HEADS + h // 2] = (pending + moved[:, LOCAL:]).astype(BF16)


def position(row):
    return (row & 192) + ((row >> 1) & 15) * 4 + ((row >> 5) & 1) * 2 + (row & 1)


def spread(block, slot):
    rows = block.shape[0] // 8
    turned = [block[:rows]]
    for p in range(1, 8):
        turned.append(pltpu.roll(block[p * rows : (p + 1) * rows], BLOCK * p, 1))
    parts = []
    for m in range(8):
        part = turned[-m % 8]
        for q in range(1, 8):
            part = jnp.where(slot == q, turned[(q - m) % 8], part)
        parts.append(part)
    return parts


def attend_kernel(in_ref, out_ref):
    lane_rows = iota((ROWS, LOCAL), 1)
    causal = position(iota((ROWS, ROWS), 1)) <= position(iota((ROWS, ROWS), 0))
    slot = iota((ROWS // 8, LOCAL), 1) >> 4
    pending = None
    for h in range(HEADS):
        block = in_ref[h]
        empty = block[:, :1].astype(F32) > 32768.0
        first = lane_rows == 0
        block = jnp.where(empty & first, 0.0, block.astype(F32)).astype(BF16)
        shared = block[:, :HEAD]
        value = block[:, HEAD:]
        pair = in_ref[HEADS + h // 2]
        cot = pair[:, :HEAD] if h % 2 == 0 else pair[:, HEAD:]
        bias_lane = lane_rows == HEAD
        head_lanes = lane_rows < HEAD
        wide = block.astype(F32)
        query = jnp.where(head_lanes, wide, jnp.where(bias_lane, 1.0, 0.0)).astype(BF16)
        key = jnp.where(
            head_lanes, wide, jnp.where(bias_lane & empty, -1e30, 0.0)
        ).astype(BF16)
        scores = dot(query, key, ((1,), (1,))) * 0.125
        scores = jnp.where(causal, scores, -1e30)
        highest = jnp.max(scores, axis=1, keepdims=True)
        weights = jnp.exp(scores - highest)
        probs = (weights / jnp.sum(weights, axis=1, keepdims=True)).astype(BF16)
        out = dot(probs, value)
        d_prob = dot(cot, value, ((1,), (1,)))
        wide_probs = probs.astype(F32)
        delta = jnp.sum(wide_probs * d_prob, axis=1, keepdims=True)
        d_score = (wide_probs * (d_prob - delta)).astype(BF16)
        both = dot(d_score, shared) + dot(d_score, shared, ((0,), (0,)))
        d_value = dot(probs, cot, ((0,), (0,)))
        for m, part in enumerate(spread(jnp.concatenate([both * 0.125, d_value], axis=1), slot)):
            n = h * 8 + m
            out_ref[n // 6 * 9 + n % 6] = part.astype(BF16)
        if h % 2 == 0:
            pending = out
        else:
            for m, part in enumerate(spread(jnp.concatenate([pending, out], axis=1), slot)):
                n = h // 2 * 8 + m
                out_ref[n // 3 * 9 + 6 + n % 3] = part.astype(BF16)


def index_of(place_ref, dy, dc):
    return lax.rem(place_ref[0] + dy, 4) * 2 + lax.rem(place_ref[1] + dc, 2)


def gather_columns(place_ref, in_ref, base, count, turn, exts, dests, out_ref, first):
    j = place_ref[0] * 2 + place_ref[1]
    head = (j * 3 // 4, (j * 6 + 5) // 8)
    lane_slot = iota((ROWS, LOCAL), 1) >> 4
    sub_rows = iota((ROWS, LOCAL), 0).astype(F32)
    for n, (dy, dc) in enumerate(STEPS):
        source = index_of(place_ref, 4 - dy, dc)
        for i in range(2):
            lanes = pl.ds(pl.multiple_of(head[i] * LOCAL, LOCAL), LOCAL)
            dests[i, source] = exts[n // 2][n % 2, LOCAL:, lanes].astype(F32)[:8]
    shift = lax.rem(j * turn, 8) * BLOCK
    turned = [pltpu.roll(in_ref[base + b].astype(F32), shift, 1) for b in range(count)]
    limit = lax.rem(j, 4)
    limit = jnp.where(limit == 1, 1, jnp.where(limit == 2, 2, 3)) * count
    for p in range(8):
        rows = turned[0]
        for b in range(1, count):
            rows = jnp.where(lane_slot == (b + p) % 8, turned[b], rows)
        rows = rows.astype(BF16)
        found = [
            dot(rows, (sub_rows == dests[i, p, :1]).astype(BF16), ((0,), (0,))) for i in range(2)
        ]
        blocks = []
        for b in range(count):
            cut = slice((b + p) % 8 * BLOCK, ((b + p) % 8 + 1) * BLOCK)
            blocks.append(jnp.where(b * 3 < limit, found[0][cut], found[1][cut]))
        out_ref[p, first : first + count * BLOCK, :] = jnp.concatenate(blocks, axis=0).astype(BF16)


def partial_kernel(place_ref, in_ref, *refs):
    exts, (out_ref, cols_ref), (dests, scratch) = refs[:4], refs[4:6], refs[6:]
    gather_columns(place_ref, in_ref, 0, 6, 2, exts, dests, cols_ref, 0)
    total = None
    for n, (dy, dc) in enumerate(STEPS):
        source = index_of(place_ref, 4 - dy, dc)
        term = dot(cols_ref[source], exts[n // 2][n % 2, :LOCAL, :])
        total = term if total is None else total + term
    for k in range(WIDTH // LOCAL):
        scratch[k * COLUMNS : (k + 1) * COLUMNS, :] = total[:, k * LOCAL : (k + 1) * LOCAL]
    scratch[16 * PIECE :, :] = jnp.zeros((8, LOCAL), F32)
    for i in range(16):
        out_ref[i] = scratch[i * PIECE : i * PIECE + SLOT, :].astype(BF16)


def forward_kernel(place_ref, in_ref, cols_ref, *refs):
    exts, (keep_ref, give_ref), (dests, scratch) = refs[:4], refs[4:6], refs[6:]
    gather_columns(place_ref, in_ref, 6, 3, 5, exts, dests, scratch, 0)
    here = place_ref[1]
    for y in range(4):
        for ref, c in ((keep_ref, here), (give_ref, 1 - here)):
            ref[y, :COLUMNS, :] = cols_ref[y * 2 + c]
            ref[y, COLUMNS:, :] = scratch[y * 2 + c]


def pack_kernel(block_ref, keep_ref, got_ref, out_ref, scratch):
    for i in range(16):
        scratch[i * PIECE : (i + 1) * PIECE, :] = block_ref[i].astype(F32)[:PIECE]
    block = scratch[...].astype(BF16)
    for y in range(4):
        out_ref[y, :WHOLE, :] = block
        out_ref[y, WHOLE : WHOLE + MESSAGE, :] = keep_ref[y]
        out_ref[y, WHOLE + MESSAGE :, :] = got_ref[y]


def return_kernel(place_ref, all_ref, ws_ref, wv_ref, att_ref, grad_ref, held):
    here = place_ref[1]
    for y in range(4):
        held[y * 2 + here] = all_ref[y, WHOLE : WHOLE + MESSAGE, :]
        held[y * 2 + 1 - here] = all_ref[y, WHOLE + MESSAGE :, :]

    def columns(blocks, per, first):
        rows = [
            held[n // per, first + n % per * BLOCK : first + (n % per + 1) * BLOCK, :]
            for n in blocks
        ]
        return jnp.concatenate(rows, axis=0).astype(F32).T.astype(BF16)

    left = columns([h * 8 + m for h in range(HEADS) for m in range(4)], 6, 0)
    right = columns([h * 8 + 4 + m for h in range(HEADS) for m in range(4)], 6, 0)
    att_ref[...] = columns(range(24), 3, COLUMNS)
    total = dot(left, ws_ref[...], ((1,), (1,))) + dot(right, wv_ref[...], ((1,), (1,)))
    grad_ref[...] = total.astype(BF16)


def sum_kernel(in_ref, out_ref):
    total = in_ref[0].astype(F32)
    for i in range(1, in_ref.shape[0]):
        total = total + in_ref[i].astype(F32)
    total = total.astype(BF16)
    for i in range(out_ref.shape[0]):
        out_ref[i] = total


def finish_kernel(place_ref, mine_ref, other_ref, shared_ref, value_ref):
    first = place_ref[1] == 0
    for k in range(WIDTH // LOCAL):
        rows = slice(k * COLUMNS, (k + 1) * COLUMNS)
        strip = []
        for y in range(4):
            mine = mine_ref[y, rows, :].astype(F32)
            other = other_ref[y, rows, :].astype(F32)
            strip += [jnp.where(first, mine, other), jnp.where(first, other, mine)]
        strip = jnp.concatenate(strip, axis=0)
        for half, ref in enumerate((shared_ref, value_ref)):
            heads = [
                strip[h * LOCAL + half * HEAD : h * LOCAL + (half + 1) * HEAD]
                for h in range(HEADS)
            ]
            ref[k * LOCAL : (k + 1) * LOCAL, :] = jnp.concatenate(heads, axis=0).T.astype(BF16)


def call(kernel, out, *args, scratch=(), scalars=0, held=False):
    space = pl.ANY if held else pltpu.VMEM
    if held:
        args = [pltpu.with_memory_space_constraint(arg, pltpu.HBM) for arg in args]
    specs = [pl.BlockSpec(memory_space=pltpu.SMEM)] * scalars
    specs += [pl.BlockSpec(memory_space=space)] * (len(args) - scalars)
    return pl.pallas_call(
        kernel,
        out_shape=out,
        in_specs=specs,
        scratch_shapes=scratch,
        compiler_params=pltpu.CompilerParams(vmem_limit_bytes=48 * 1024 * 1024),
    )(*args)


def shape(*dims):
    return jax.ShapeDtypeStruct(dims, BF16)


def swap(rows, axes):
    return lax.all_to_all(rows, axes, split_axis=0, concat_axis=0, tiled=True)


def body(tokens, w_shared, w_value, cluster_ids, slot_index, cotangent):
    rows = tokens[0]
    place = jnp.stack([lax.axis_index("y"), lax.axis_index("c")]).astype(jnp.int32)
    sent, ext = call(
        send_kernel,
        (shape(9, ROWS, LOCAL), shape(LOCAL + 16, WIDTH)),
        cluster_ids.transpose(1, 0, 2),
        rows,
        w_shared,
        w_value,
        cotangent[0],
        scratch=[
            pltpu.VMEM((HEADS, 1, LOCAL), jnp.int32),
            pltpu.VMEM((LOCAL, WIDTH), BF16),
            pltpu.VMEM((WIDTH, PROJ), BF16),
            pltpu.VMEM((WIDTH, PROJ), BF16),
            pltpu.VMEM((LOCAL, PROJ), BF16),
            pltpu.SemaphoreType.DMA((5,)),
        ],
        held=True,
    )

    def shift(pair, dy):
        return lax.ppermute(pair, "y", [(y, (y + dy) % 4) for y in range(4)])

    def flip(part):
        return lax.ppermute(part, "c", [(0, 1), (1, 0)])

    arrived = swap(sent.reshape(9, LOCAL, 2, LOCAL).transpose(1, 0, 2, 3), OWNERS)
    pair = jnp.stack([ext, flip(ext)])
    near = (shift(pair, 1), shift(pair, 3))
    arrived, pair, near, place = lax.optimization_barrier((arrived, pair, near, place))
    exts = [pair, near[0], shift(pair, 2), near[1]]
    arrived = arrived.transpose(1, 0, 2, 3)
    worked = call(attend_kernel, shape(72, 32, LOCAL), arrived.reshape(9, ROWS, LOCAL))
    worked = worked.reshape(8, 9, 16, 2, LOCAL).transpose(0, 2, 1, 3, 4)
    back = swap(worked.reshape(LOCAL, 9, 2, LOCAL), OWNERS)
    back = back.transpose(1, 0, 2, 3).reshape(9, ROWS, LOCAL)
    part, cols = call(
        partial_kernel,
        (shape(16, SLOT, LOCAL), shape(8, COLUMNS, LOCAL)),
        place,
        back,
        *exts,
        scratch=[pltpu.VMEM((2, 8, 8, LOCAL), F32), pltpu.VMEM((16 * PIECE + 8, LOCAL), F32)],
        scalars=1,
    )
    keep, give = call(
        forward_kernel,
        (shape(4, MESSAGE, LOCAL), shape(4, MESSAGE, LOCAL)),
        place,
        back,
        cols,
        *exts,
        scratch=[pltpu.VMEM((2, 8, 8, LOCAL), F32), pltpu.VMEM((8, COLUMNS // 2, LOCAL), BF16)],
        scalars=1,
    )
    got = flip(give)
    part = swap(part, ("x", "zl"))
    part, keep, got = lax.optimization_barrier((part, keep, got))
    part = call(sum_kernel, shape(4, SLOT, LOCAL), part)
    block = call(sum_kernel, shape(16, SLOT, LOCAL), swap(part, "zh"))
    block = swap(block, ("x", "zl"))
    block = call(
        pack_kernel,
        shape(4, WHOLE + 2 * MESSAGE, LOCAL),
        block,
        keep,
        got,
        scratch=[pltpu.VMEM((WHOLE, LOCAL), F32)],
    )
    block = swap(block, "y")
    other = flip(block)
    attention, grad_tokens = call(
        return_kernel,
        (shape(LOCAL, PROJ), shape(LOCAL, WIDTH)),
        place,
        block,
        w_shared,
        w_value,
        scratch=[pltpu.VMEM((8, MESSAGE, LOCAL), BF16)],
        scalars=1,
    )
    grad_shared, grad_value = call(
        finish_kernel,
        (shape(WIDTH, PROJ), shape(WIDTH, PROJ)),
        place,
        block,
        other,
        scalars=1,
    )
    return (attention[None], grad_tokens[None], grad_shared, grad_value)


def solution(mesh):
    fine = Mesh(mesh.devices.reshape(4, 4, 4, 4, 2), ("x", "y", "zh", "zl", "c"))
    in_specs = (
        P("x", TOK, None),
        P(),
        P(),
        P("x", None, TOK),
        P("x", None, TOK),
        P("x", TOK, None),
    )
    out_specs = (P("x", TOK, None), P("x", TOK, None), P(), P())
    return jax.shard_map(body, mesh=fine, in_specs=in_specs, out_specs=out_specs, check_vma=False)
```

```python
import jax
import jax.numpy as jnp
from jax import lax
from jax.experimental import pallas as pl
from jax.experimental.pallas import tpu as pltpu
from jax.sharding import Mesh
from jax.sharding import PartitionSpec as P

F32 = jnp.float32
BF16 = jnp.bfloat16
HEADS = 6
HEAD = 64
ROWS = 256
LOCAL = 128
WIDTH = 768
PROJ = 384
UNUSED = 65536.0
PLANE = ("y", "c")
TOK = ("y", "z", "c")
OWNERS = ("y", "c", "z")
RING = [(3, 4, 9, 14), (2, 7, 8, 13), (1, 6, 11, 12), (0, 5, 10, 15)]
FAR = [list(group) for group in RING]
NEAR = [[x * 16 + RING[n][b] for x in range(4) for n in range(4)] for b in range(4)]
STEPS = [(dy, dc) for dy in range(4) for dc in range(2)]
COLUMNS = 96
PIECE = 36
SLOT = 40
BLOCK = 16
WHOLE = 576
MESSAGE = 144


def iota(shape, dim):
    return lax.broadcasted_iota(jnp.int32, shape, dim)


def dot(a, b, dims=((1,), (0,))):
    return lax.dot_general(a, b, (dims, ((), ())), preferred_element_type=F32)


def send_kernel(*refs):
    sources, (out_ref, ext_ref), targets, sems = refs[:5], refs[5:7], refs[7:12], refs[12]
    copies = [
        pltpu.make_async_copy(source, target, sems.at[n])
        for n, (source, target) in enumerate(zip(sources, targets))
    ]
    for copy in copies:
        copy.start()
    cluster_ref, tok_ref, ws_ref, wv_ref, cot_ref = targets
    sub = iota((LOCAL, LOCAL), 0)
    lane = iota((LOCAL, LOCAL), 1)
    sub_rows = iota((ROWS, LOCAL), 0)
    lane_rows = iota((ROWS, LOCAL), 1)
    copies[0].wait()
    hits = []
    marks = []
    for h in range(HEADS):
        cluster = cluster_ref[h]
        member = (sub == cluster).astype(BF16)
        same = dot(member, member, ((0,), (0,)))
        order = jnp.sum(jnp.where(sub < lane, same, 0.0), axis=0, keepdims=True)
        owner = (cluster & 96) + (cluster & 1) * 16 + ((cluster >> 1) & 15)
        dest = owner * 2 + order.astype(jnp.int32)
        ext_ref[LOCAL:, h * LOCAL : (h + 1) * LOCAL] = jnp.broadcast_to(
            dest.astype(F32), (16, LOCAL)
        ).astype(BF16)
        hit = sub_rows == dest
        used = jnp.sum(jnp.where(hit, 1.0, 0.0), axis=1, keepdims=True)
        hits.append(hit.astype(BF16))
        marks.append(jnp.where((lane_rows == 0) & (used < 0.5), UNUSED, 0.0))
    for copy in copies[1:]:
        copy.wait()
    tokens = tok_ref[...]
    ext_ref[:LOCAL, :] = tokens
    shared = dot(tokens, ws_ref[...]).astype(BF16)
    value = dot(tokens, wv_ref[...]).astype(BF16)
    cot = cot_ref[...]
    blank = jnp.zeros((LOCAL, HEAD), BF16)
    pending = None
    for h in range(HEADS):
        cols = slice(h * HEAD, (h + 1) * HEAD)
        tail = [cot[:, cols], blank] if h % 2 == 0 else [blank, cot[:, cols]]
        packed = jnp.concatenate([shared[:, cols], value[:, cols]] + tail, axis=1)
        moved = dot(hits[h], packed)
        out_ref[h] = (moved[:, :LOCAL] + marks[h]).astype(BF16)
        if h % 2 == 0:
            pending = moved[:, LOCAL:]
        else:
            out_ref[HEADS + h // 2] = (pending + moved[:, LOCAL:]).astype(BF16)


def position(row):
    return (row & 192) + ((row >> 1) & 15) * 4 + ((row >> 5) & 1) * 2 + (row & 1)


def spread(block, slot):
    rows = block.shape[0] // 8
    parts = [block[p * rows : (p + 1) * rows] for p in range(8)]
    for bit in (1, 2, 4):
        odd = (slot & bit) != 0
        after = list(parts)
        for p in range(8):
            if p & bit == 0:
                low, high = parts[p], parts[p + bit]
                after[p] = jnp.where(odd, pltpu.roll(high, BLOCK * bit, 1), low)
                after[p + bit] = jnp.where(odd, high, pltpu.roll(low, LOCAL - BLOCK * bit, 1))
        parts = after
    return parts


def attend_kernel(in_ref, out_ref):
    half = ROWS // 2
    lane_rows = iota((ROWS, LOCAL), 1)
    first = lane_rows == 0
    bias_lane = lane_rows == HEAD
    head_lanes = lane_rows < HEAD
    left_causal = position(iota((half, half), 0)) <= position(iota((half, half), 1))
    right_causal = position(iota((ROWS, half), 0)) <= position(iota((ROWS, half), 1) + half)
    slot = iota((ROWS // 8, LOCAL), 1) >> 4
    hidden = jnp.zeros((half, half), BF16)
    pending = None
    for h in range(HEADS):
        block = in_ref[h].astype(F32)
        empty = block[:, :1] > 32768.0
        block = jnp.where(empty & first, 0.0, block)
        query = jnp.where(head_lanes, block * 0.125, jnp.where(bias_lane, 1.0, 0.0)).astype(BF16)
        key = jnp.where(
            head_lanes, block, jnp.where(bias_lane & empty, -1e30, 0.0)
        ).astype(BF16)
        block = block.astype(BF16)
        shared = block[:, :HEAD]
        value = block[:, HEAD:]
        pair = in_ref[HEADS + h // 2]
        cot = pair[:, :HEAD] if h % 2 == 0 else pair[:, HEAD:]
        probs = []
        d_scores = []
        for rows, cols, causal in (
            (slice(0, half), slice(0, half), left_causal),
            (slice(0, ROWS), slice(half, ROWS), right_causal),
        ):
            scores = dot(key[rows], query[cols], ((1,), (1,)))
            scores = jnp.where(causal, scores, -1e30)
            weights = jnp.exp(scores - jnp.max(scores, axis=0, keepdims=True))
            scale = 1.0 / jnp.sum(weights, axis=0, keepdims=True)
            prob = (weights * scale).astype(BF16)
            d_prob = dot(value[rows], cot[cols], ((1,), (1,)))
            wide = prob.astype(F32)
            delta = jnp.sum(wide * d_prob, axis=0, keepdims=True)
            probs.append(prob)
            d_scores.append((wide * (d_prob - delta)).astype(BF16))
        probs = jnp.concatenate([jnp.concatenate([probs[0], hidden], axis=0), probs[1]], axis=1)
        d_scores = jnp.concatenate(
            [jnp.concatenate([d_scores[0], hidden], axis=0), d_scores[1]], axis=1
        )
        turned = block.T
        above = dot(turned[:HEAD], d_scores)
        out = dot(turned[HEAD:], probs)
        both = jnp.concatenate([above, out], axis=0).T
        d_shared = (dot(d_scores, shared) + both[:, :HEAD]) * 0.125
        d_value = dot(probs, cot)
        for m, part in enumerate(spread(jnp.concatenate([d_shared, d_value], axis=1), slot)):
            n = h * 8 + m
            out_ref[n // 6 * 9 + n % 6] = part.astype(BF16)
        if h % 2 == 0:
            pending = both
        else:
            lane = iota((ROWS, LOCAL), 1) < HEAD
            joined = jnp.where(lane, pltpu.roll(pending, HEAD, 1), both)
            for m, part in enumerate(spread(joined, slot)):
                n = h // 2 * 8 + m
                out_ref[n // 3 * 9 + 6 + n % 3] = part.astype(BF16)


def index_of(place_ref, dy, dc):
    return lax.rem(place_ref[0] + dy, 4) * 2 + lax.rem(place_ref[1] + dc, 2)


def gather_columns(place_ref, in_ref, base, count, exts, dests, out_ref, first):
    j = place_ref[0] * 2 + place_ref[1]
    head = (j * 3 // 4, (j * 6 + 5) // 8)
    lane_slot = iota((ROWS, LOCAL), 1) >> 4
    sub_rows = iota((ROWS, LOCAL), 0).astype(F32)
    for n, (dy, dc) in enumerate(STEPS):
        source = index_of(place_ref, 4 - dy, dc)
        for i in range(2):
            lanes = pl.ds(pl.multiple_of(head[i] * LOCAL, LOCAL), LOCAL)
            dests[i, source] = exts[n // 2][n % 2, LOCAL:, lanes].astype(F32)[:8]
    turned = [in_ref[base + b].astype(F32) for b in range(count)]
    turned = [pltpu.roll(rows, BLOCK * b, 1) if b else rows for b, rows in enumerate(turned)]
    limit = lax.rem(j, 4)
    limit = jnp.where(limit == 1, 1, jnp.where(limit == 2, 2, 3)) * count
    for p in range(8):
        rows = turned[0]
        for b in range(1, count):
            rows = jnp.where(lane_slot == (b + p) % 8, turned[b], rows)
        rows = rows.astype(BF16)
        routes = [(sub_rows == dests[i, p, :1]).astype(BF16) for i in range(2)]
        found = dot(rows, jnp.concatenate(routes, axis=1), ((0,), (0,)))
        found = [found[:, :LOCAL], found[:, LOCAL:]]
        blocks = []
        for b in range(count):
            cut = slice((b + p) % 8 * BLOCK, ((b + p) % 8 + 1) * BLOCK)
            blocks.append(jnp.where(b * 3 < limit, found[0][cut], found[1][cut]))
        out_ref[p, first : first + count * BLOCK, :] = jnp.concatenate(blocks, axis=0).astype(BF16)


def partial_kernel(place_ref, in_ref, *refs):
    exts, (out_ref, cols_ref), (dests, scratch) = refs[:4], refs[4:6], refs[6:]
    gather_columns(place_ref, in_ref, 0, 6, exts, dests, cols_ref, 0)
    total = None
    for n, (dy, dc) in enumerate(STEPS):
        source = index_of(place_ref, 4 - dy, dc)
        term = dot(cols_ref[source], exts[n // 2][n % 2, :LOCAL, :])
        total = term if total is None else total + term
    for k in range(WIDTH // LOCAL):
        scratch[k * COLUMNS : (k + 1) * COLUMNS, :] = total[:, k * LOCAL : (k + 1) * LOCAL]
    scratch[16 * PIECE :, :] = jnp.zeros((8, LOCAL), F32)
    for i in range(16):
        out_ref[i] = scratch[i * PIECE : i * PIECE + SLOT, :].astype(BF16)


def forward_kernel(place_ref, in_ref, cols_ref, *refs):
    exts, (keep_ref, give_ref), (dests, scratch) = refs[:4], refs[4:6], refs[6:]
    gather_columns(place_ref, in_ref, 6, 3, exts, dests, scratch, 0)
    here = place_ref[1]
    for y in range(4):
        for ref, c in ((keep_ref, here), (give_ref, 1 - here)):
            ref[y, :COLUMNS, :] = cols_ref[y * 2 + c]
            ref[y, COLUMNS:, :] = scratch[y * 2 + c]


def pack_kernel(block_ref, keep_ref, got_ref, out_ref, scratch):
    for i in range(16):
        scratch[i * PIECE : (i + 1) * PIECE, :] = block_ref[i].astype(F32)[:PIECE]
    block = scratch[...].astype(BF16)
    for y in range(4):
        out_ref[y, :WHOLE, :] = block
        out_ref[y, WHOLE : WHOLE + MESSAGE, :] = keep_ref[y]
        out_ref[y, WHOLE + MESSAGE :, :] = got_ref[y]


def return_kernel(place_ref, all_ref, ws_ref, wv_ref, att_ref, grad_ref, held):
    here = place_ref[1]
    for y in range(4):
        held[y * 2 + here] = all_ref[y, WHOLE : WHOLE + MESSAGE, :]
        held[y * 2 + 1 - here] = all_ref[y, WHOLE + MESSAGE :, :]

    def columns(blocks, per, first):
        rows = [
            held[n // per, first + n % per * BLOCK : first + (n % per + 1) * BLOCK, :]
            for n in blocks
        ]
        return jnp.concatenate(rows, axis=0).astype(F32).T.astype(BF16)

    left = columns([h * 8 + m for h in range(HEADS) for m in range(4)], 6, 0)
    right = columns([h * 8 + 4 + m for h in range(HEADS) for m in range(4)], 6, 0)
    att_ref[...] = columns(range(24), 3, COLUMNS)
    total = dot(left, ws_ref[...], ((1,), (1,))) + dot(right, wv_ref[...], ((1,), (1,)))
    grad_ref[...] = total.astype(BF16)


def sum_kernel(in_ref, out_ref):
    total = in_ref[0].astype(F32)
    for i in range(1, in_ref.shape[0]):
        total = total + in_ref[i].astype(F32)
    total = total.astype(BF16)
    for i in range(out_ref.shape[0]):
        out_ref[i] = total


def finish_kernel(place_ref, mine_ref, other_ref, shared_ref, value_ref, held, sems):
    first = place_ref[1] == 0
    copies = []
    for k in range(WIDTH // LOCAL):
        rows = slice(k * COLUMNS, (k + 1) * COLUMNS)
        strip = []
        for y in range(4):
            mine = mine_ref[y, rows, :].astype(F32)
            other = other_ref[y, rows, :].astype(F32)
            strip += [jnp.where(first, mine, other), jnp.where(first, other, mine)]
        strip = jnp.concatenate(strip, axis=0)
        lines = slice(k * LOCAL, (k + 1) * LOCAL)
        for half, ref in enumerate((shared_ref, value_ref)):
            heads = [
                strip[h * LOCAL + half * HEAD : h * LOCAL + (half + 1) * HEAD]
                for h in range(HEADS)
            ]
            held[half, lines, :] = jnp.concatenate(heads, axis=0).T.astype(BF16)
            copies.append(
                pltpu.make_async_copy(held.at[half, lines], ref.at[lines], sems.at[half, k])
            )
            copies[-1].start()
    for copy in copies:
        copy.wait()


def call(kernel, out, *args, scratch=(), scalars=0, held=False, far=False):
    space = pl.ANY if held else pltpu.VMEM
    if held:
        args = [pltpu.with_memory_space_constraint(arg, pltpu.HBM) for arg in args]
    specs = [pl.BlockSpec(memory_space=pltpu.SMEM)] * scalars
    specs += [pl.BlockSpec(memory_space=space)] * (len(args) - scalars)
    return pl.pallas_call(
        kernel,
        out_shape=out,
        in_specs=specs,
        out_specs=jax.tree.map(lambda _: pl.BlockSpec(memory_space=pl.ANY if far else pltpu.VMEM), out),
        scratch_shapes=scratch,
        compiler_params=pltpu.CompilerParams(vmem_limit_bytes=48 * 1024 * 1024),
    )(*args)


def shape(*dims):
    return jax.ShapeDtypeStruct(dims, BF16)


def swap(rows, axes, groups=None):
    return lax.all_to_all(
        rows, axes, split_axis=0, concat_axis=0, tiled=True, axis_index_groups=groups
    )


def body(tokens, w_shared, w_value, cluster_ids, slot_index, cotangent):
    rows = tokens[0]
    place = jnp.stack([lax.axis_index("y"), lax.axis_index("c")]).astype(jnp.int32)
    sent, ext = call(
        send_kernel,
        (shape(9, ROWS, LOCAL), shape(LOCAL + 16, WIDTH)),
        cluster_ids.transpose(1, 0, 2),
        rows,
        w_shared,
        w_value,
        cotangent[0],
        scratch=[
            pltpu.VMEM((HEADS, 1, LOCAL), jnp.int32),
            pltpu.VMEM((LOCAL, WIDTH), BF16),
            pltpu.VMEM((WIDTH, PROJ), BF16),
            pltpu.VMEM((WIDTH, PROJ), BF16),
            pltpu.VMEM((LOCAL, PROJ), BF16),
            pltpu.SemaphoreType.DMA((5,)),
        ],
        held=True,
    )

    def shift(pair, dy):
        return lax.ppermute(pair, "y", [(y, (y + dy) % 4) for y in range(4)])

    def flip(part):
        return lax.ppermute(part, "c", [(0, 1), (1, 0)])

    arrived = swap(sent.reshape(9, LOCAL, 2, LOCAL).transpose(1, 0, 2, 3), OWNERS)
    pair = jnp.stack([ext, flip(ext)])
    near = (shift(pair, 1), shift(pair, 3))
    arrived, pair, near, place = lax.optimization_barrier((arrived, pair, near, place))
    exts = [pair, near[0], shift(pair, 2), near[1]]
    arrived = arrived.transpose(1, 0, 2, 3)
    worked = call(attend_kernel, shape(72, 32, LOCAL), arrived.reshape(9, ROWS, LOCAL))
    worked = worked.reshape(8, 9, 16, 2, LOCAL).transpose(0, 2, 1, 3, 4)
    back = swap(worked.reshape(LOCAL, 9, 2, LOCAL), OWNERS)
    back = back.transpose(1, 0, 2, 3).reshape(9, ROWS, LOCAL)
    part, cols = call(
        partial_kernel,
        (shape(16, SLOT, LOCAL), shape(8, COLUMNS, LOCAL)),
        place,
        back,
        *exts,
        scratch=[pltpu.VMEM((2, 8, 8, LOCAL), F32), pltpu.VMEM((16 * PIECE + 8, LOCAL), F32)],
        scalars=1,
    )
    keep, give = call(
        forward_kernel,
        (shape(4, MESSAGE, LOCAL), shape(4, MESSAGE, LOCAL)),
        place,
        back,
        cols,
        *exts,
        scratch=[pltpu.VMEM((2, 8, 8, LOCAL), F32), pltpu.VMEM((8, COLUMNS // 2, LOCAL), BF16)],
        scalars=1,
    )
    got = flip(give)
    part = swap(part, ("x", "z"), NEAR)
    part, keep, got = lax.optimization_barrier((part, keep, got))
    part = call(sum_kernel, shape(4, SLOT, LOCAL), part)
    block = call(sum_kernel, shape(16, SLOT, LOCAL), swap(part, "z", FAR))
    block = swap(block, ("x", "z"), NEAR)
    block = call(
        pack_kernel,
        shape(4, WHOLE + 2 * MESSAGE, LOCAL),
        block,
        keep,
        got,
        scratch=[pltpu.VMEM((WHOLE, LOCAL), F32)],
    )
    block = swap(block, "y")
    other = flip(block)
    attention, grad_tokens = call(
        return_kernel,
        (shape(LOCAL, PROJ), shape(LOCAL, WIDTH)),
        place,
        block,
        w_shared,
        w_value,
        scratch=[pltpu.VMEM((8, MESSAGE, LOCAL), BF16)],
        scalars=1,
    )
    grad_shared, grad_value = call(
        finish_kernel,
        (shape(WIDTH, PROJ), shape(WIDTH, PROJ)),
        place,
        block,
        other,
        scratch=[
            pltpu.VMEM((2, WIDTH, PROJ), BF16),
            pltpu.SemaphoreType.DMA((2, WIDTH // LOCAL)),
        ],
        scalars=1,
        far=True,
    )
    return (attention[None], grad_tokens[None], grad_shared, grad_value)


def solution(mesh):
    fine = Mesh(mesh.devices.reshape(4, 4, 16, 2), ("x", "y", "z", "c"))
    in_specs = (
        P("x", TOK, None),
        P(),
        P(),
        P("x", None, TOK),
        P("x", None, TOK),
        P("x", TOK, None),
    )
    out_specs = (P("x", TOK, None), P("x", TOK, None), P(), P())
    return jax.shard_map(body, mesh=fine, in_specs=in_specs, out_specs=out_specs, check_vma=False)
```

```python
import jax
import jax.numpy as jnp
from jax import lax
from jax.experimental import pallas as pl
from jax.experimental.pallas import tpu as pltpu
from jax.sharding import Mesh
from jax.sharding import PartitionSpec as P

F32 = jnp.float32
BF16 = jnp.bfloat16
HEADS = 6
HEAD = 64
ROWS = 256
LOCAL = 128
WIDTH = 768
PROJ = 384
UNUSED = 65536.0
PLANE = ("y", "c")
TOK = ("y", "z", "c")
OWNERS = ("y", "c", "z")
RING = [(3, 4, 9, 14), (2, 7, 8, 13), (1, 6, 11, 12), (0, 5, 10, 15)]
FAR = [list(group) for group in RING]
NEAR = [[x * 16 + RING[n][b] for x in range(4) for n in range(4)] for b in range(4)]
STEPS = [(dy, dc) for dy in range(4) for dc in range(2)]
COLUMNS = 96
PIECE = 36
SLOT = 40
BLOCK = 16
WHOLE = 576
MESSAGE = 144


def iota(shape, dim):
    return lax.broadcasted_iota(jnp.int32, shape, dim)


def dot(a, b, dims=((1,), (0,))):
    return lax.dot_general(a, b, (dims, ((), ())), preferred_element_type=F32)


def send_kernel(*refs):
    sources, (out_ref, ext_ref), targets, sems = refs[:5], refs[5:7], refs[7:12], refs[12]
    copies = [
        pltpu.make_async_copy(source, target, sems.at[n])
        for n, (source, target) in enumerate(zip(sources, targets))
    ]
    for copy in copies:
        copy.start()
    cluster_ref, tok_ref, ws_ref, wv_ref, cot_ref = targets
    sub = iota((LOCAL, LOCAL), 0)
    lane = iota((LOCAL, LOCAL), 1)
    sub_rows = iota((ROWS, LOCAL), 0)
    lane_rows = iota((ROWS, LOCAL), 1)
    copies[0].wait()
    hits = []
    marks = []
    for h in range(HEADS):
        cluster = cluster_ref[h]
        member = (sub == cluster).astype(BF16)
        same = dot(member, member, ((0,), (0,)))
        order = jnp.sum(jnp.where(sub < lane, same, 0.0), axis=0, keepdims=True)
        owner = (cluster & 96) + (cluster & 1) * 16 + ((cluster >> 1) & 15)
        dest = owner * 2 + order.astype(jnp.int32)
        ext_ref[LOCAL:, h * LOCAL : (h + 1) * LOCAL] = jnp.broadcast_to(
            dest.astype(F32), (16, LOCAL)
        ).astype(BF16)
        hit = sub_rows == dest
        used = jnp.sum(jnp.where(hit, 1.0, 0.0), axis=1, keepdims=True)
        hits.append(hit.astype(BF16))
        marks.append(jnp.where((lane_rows == 0) & (used < 0.5), UNUSED, 0.0))
    for copy in copies[1:]:
        copy.wait()
    tokens = tok_ref[...]
    ext_ref[:LOCAL, :] = tokens
    shared = dot(tokens, ws_ref[...]).astype(BF16)
    value = dot(tokens, wv_ref[...]).astype(BF16)
    cot = cot_ref[...]
    blank = jnp.zeros((LOCAL, HEAD), BF16)
    pending = None
    for h in range(HEADS):
        cols = slice(h * HEAD, (h + 1) * HEAD)
        tail = [cot[:, cols], blank] if h % 2 == 0 else [blank, cot[:, cols]]
        packed = jnp.concatenate([shared[:, cols], value[:, cols]] + tail, axis=1)
        moved = dot(hits[h], packed)
        out_ref[:, h] = (moved[:, :LOCAL] + marks[h]).astype(BF16).reshape(LOCAL, 2, LOCAL)
        if h % 2 == 0:
            pending = moved[:, LOCAL:]
        else:
            packed = (pending + moved[:, LOCAL:]).astype(BF16)
            out_ref[:, HEADS + h // 2] = packed.reshape(LOCAL, 2, LOCAL)


def position(row):
    return (row & 192) + ((row >> 1) & 15) * 4 + ((row >> 5) & 1) * 2 + (row & 1)


def spread(block, slot):
    rows = block.shape[0] // 8
    parts = [block[p * rows : (p + 1) * rows] for p in range(8)]
    for bit in (1, 2, 4):
        odd = (slot & bit) != 0
        after = list(parts)
        for p in range(8):
            if p & bit == 0:
                low, high = parts[p], parts[p + bit]
                after[p] = jnp.where(odd, pltpu.roll(high, BLOCK * bit, 1), low)
                after[p + bit] = jnp.where(odd, high, pltpu.roll(low, LOCAL - BLOCK * bit, 1))
        parts = after
    return parts


def attend_kernel(in_ref, out_ref):
    half = ROWS // 2
    lane_rows = iota((ROWS, LOCAL), 1)
    first = lane_rows == 0
    bias_lane = lane_rows == HEAD
    head_lanes = lane_rows < HEAD
    left_causal = position(iota((half, half), 0)) <= position(iota((half, half), 1))
    right_causal = position(iota((ROWS, half), 0)) <= position(iota((ROWS, half), 1) + half)
    slot = iota((ROWS // 8, LOCAL), 1) >> 4
    hidden = jnp.zeros((half, half), BF16)
    pending = None
    for h in range(HEADS):
        block = in_ref[h].astype(F32)
        empty = block[:, :1] > 32768.0
        block = jnp.where(empty & first, 0.0, block)
        query = jnp.where(head_lanes, block * 0.125, jnp.where(bias_lane, 1.0, 0.0)).astype(BF16)
        key = jnp.where(
            head_lanes, block, jnp.where(bias_lane & empty, -1e30, 0.0)
        ).astype(BF16)
        block = block.astype(BF16)
        shared = block[:, :HEAD]
        value = block[:, HEAD:]
        pair = in_ref[HEADS + h // 2]
        cot = pair[:, :HEAD] if h % 2 == 0 else pair[:, HEAD:]
        probs = []
        d_scores = []
        for rows, cols, causal in (
            (slice(0, half), slice(0, half), left_causal),
            (slice(0, ROWS), slice(half, ROWS), right_causal),
        ):
            scores = dot(key[rows], query[cols], ((1,), (1,)))
            scores = jnp.where(causal, scores, -1e30)
            weights = jnp.exp(scores - jnp.max(scores, axis=0, keepdims=True))
            scale = 1.0 / jnp.sum(weights, axis=0, keepdims=True)
            prob = (weights * scale).astype(BF16)
            d_prob = dot(value[rows], cot[cols], ((1,), (1,)))
            wide = prob.astype(F32)
            delta = jnp.sum(wide * d_prob, axis=0, keepdims=True)
            probs.append(prob)
            d_scores.append((wide * (d_prob - delta)).astype(BF16))
        probs = jnp.concatenate([jnp.concatenate([probs[0], hidden], axis=0), probs[1]], axis=1)
        d_scores = jnp.concatenate(
            [jnp.concatenate([d_scores[0], hidden], axis=0), d_scores[1]], axis=1
        )
        turned = block.T
        above = dot(turned[:HEAD], d_scores)
        out = dot(turned[HEAD:], probs)
        both = jnp.concatenate([above, out], axis=0).T
        d_shared = (dot(d_scores, shared) + both[:, :HEAD]) * 0.125
        d_value = dot(probs, cot)
        for m, part in enumerate(spread(jnp.concatenate([d_shared, d_value], axis=1), slot)):
            n = h * 8 + m
            out_ref[n // 6 * 16 : (n // 6 + 1) * 16, n % 6] = part.astype(BF16).reshape(16, 2, LOCAL)
        if h % 2 == 0:
            pending = both
        else:
            lane = iota((ROWS, LOCAL), 1) < HEAD
            joined = jnp.where(lane, pltpu.roll(pending, HEAD, 1), both)
            for m, part in enumerate(spread(joined, slot)):
                n = h // 2 * 8 + m
                out_ref[n // 3 * 16 : (n // 3 + 1) * 16, 6 + n % 3] = part.astype(BF16).reshape(16, 2, LOCAL)


def index_of(place_ref, dy, dc):
    return lax.rem(place_ref[0] + dy, 4) * 2 + lax.rem(place_ref[1] + dc, 2)


def gather_columns(place_ref, in_ref, base, count, exts, dests, out_ref, first):
    j = place_ref[0] * 2 + place_ref[1]
    head = (j * 3 // 4, (j * 6 + 5) // 8)
    lane_slot = iota((ROWS, LOCAL), 1) >> 4
    sub_rows = iota((ROWS, LOCAL), 0).astype(F32)
    for n, (dy, dc) in enumerate(STEPS):
        source = index_of(place_ref, 4 - dy, dc)
        for i in range(2):
            lanes = pl.ds(pl.multiple_of(head[i] * LOCAL, LOCAL), LOCAL)
            dests[i, source] = exts[n // 2][n % 2, LOCAL:, lanes].astype(F32)[:8]
    turned = [in_ref[:, base + b].reshape(ROWS, LOCAL).astype(F32) for b in range(count)]
    turned = [pltpu.roll(rows, BLOCK * b, 1) if b else rows for b, rows in enumerate(turned)]
    limit = lax.rem(j, 4)
    limit = jnp.where(limit == 1, 1, jnp.where(limit == 2, 2, 3)) * count
    for p in range(8):
        rows = turned[0]
        for b in range(1, count):
            rows = jnp.where(lane_slot == (b + p) % 8, turned[b], rows)
        rows = rows.astype(BF16)
        routes = [(sub_rows == dests[i, p, :1]).astype(BF16) for i in range(2)]
        found = dot(rows, jnp.concatenate(routes, axis=1), ((0,), (0,)))
        found = [found[:, :LOCAL], found[:, LOCAL:]]
        blocks = []
        for b in range(count):
            cut = slice((b + p) % 8 * BLOCK, ((b + p) % 8 + 1) * BLOCK)
            blocks.append(jnp.where(b * 3 < limit, found[0][cut], found[1][cut]))
        out_ref[p, first : first + count * BLOCK, :] = jnp.concatenate(blocks, axis=0).astype(BF16)


def partial_kernel(place_ref, in_ref, *refs):
    exts, (out_ref, cols_ref), (dests, scratch) = refs[:4], refs[4:6], refs[6:]
    gather_columns(place_ref, in_ref, 0, 6, exts, dests, cols_ref, 0)
    total = None
    for n, (dy, dc) in enumerate(STEPS):
        source = index_of(place_ref, 4 - dy, dc)
        term = dot(cols_ref[source], exts[n // 2][n % 2, :LOCAL, :])
        total = term if total is None else total + term
    for k in range(WIDTH // LOCAL):
        scratch[k * COLUMNS : (k + 1) * COLUMNS, :] = total[:, k * LOCAL : (k + 1) * LOCAL]
    scratch[16 * PIECE :, :] = jnp.zeros((8, LOCAL), F32)
    for i in range(16):
        out_ref[i] = scratch[i * PIECE : i * PIECE + SLOT, :].astype(BF16)


def forward_kernel(place_ref, in_ref, cols_ref, *refs):
    exts, (keep_ref, give_ref), (dests, scratch) = refs[:4], refs[4:6], refs[6:]
    gather_columns(place_ref, in_ref, 6, 3, exts, dests, scratch, 0)
    here = place_ref[1]
    for y in range(4):
        for ref, c in ((keep_ref, here), (give_ref, 1 - here)):
            ref[y, :COLUMNS, :] = cols_ref[y * 2 + c]
            ref[y, COLUMNS:, :] = scratch[y * 2 + c]


def pack_kernel(block_ref, keep_ref, got_ref, out_ref, scratch):
    for i in range(16):
        scratch[i * PIECE : (i + 1) * PIECE, :] = block_ref[i].astype(F32)[:PIECE]
    block = scratch[...].astype(BF16)
    for y in range(4):
        out_ref[y, :WHOLE, :] = block
        out_ref[y, WHOLE : WHOLE + MESSAGE, :] = keep_ref[y]
        out_ref[y, WHOLE + MESSAGE :, :] = got_ref[y]


def return_kernel(place_ref, all_ref, ws_ref, wv_ref, att_ref, grad_ref, held):
    here = place_ref[1]
    for y in range(4):
        held[y * 2 + here] = all_ref[y, WHOLE : WHOLE + MESSAGE, :]
        held[y * 2 + 1 - here] = all_ref[y, WHOLE + MESSAGE :, :]

    def columns(blocks, per, first):
        rows = [
            held[n // per, first + n % per * BLOCK : first + (n % per + 1) * BLOCK, :]
            for n in blocks
        ]
        return jnp.concatenate(rows, axis=0).astype(F32).T.astype(BF16)

    left = columns([h * 8 + m for h in range(HEADS) for m in range(4)], 6, 0)
    right = columns([h * 8 + 4 + m for h in range(HEADS) for m in range(4)], 6, 0)
    att_ref[...] = columns(range(24), 3, COLUMNS)
    total = dot(left, ws_ref[...], ((1,), (1,))) + dot(right, wv_ref[...], ((1,), (1,)))
    grad_ref[...] = total.astype(BF16)


def sum_kernel(in_ref, out_ref):
    total = in_ref[0].astype(F32)
    for i in range(1, in_ref.shape[0]):
        total = total + in_ref[i].astype(F32)
    total = total.astype(BF16)
    for i in range(out_ref.shape[0]):
        out_ref[i] = total


def finish_kernel(place_ref, mine_ref, other_ref, shared_ref, value_ref, held, sems):
    first = place_ref[1] == 0
    copies = []
    for k in range(WIDTH // LOCAL):
        rows = slice(k * COLUMNS, (k + 1) * COLUMNS)
        strip = []
        for y in range(4):
            mine = mine_ref[y, rows, :]
            other = other_ref[y, rows, :]
            strip += [jnp.where(first, mine, other), jnp.where(first, other, mine)]
        strip = jnp.concatenate(strip, axis=0)
        lines = slice(k * LOCAL, (k + 1) * LOCAL)
        for half, ref in enumerate((shared_ref, value_ref)):
            heads = [
                strip[h * LOCAL + half * HEAD : h * LOCAL + (half + 1) * HEAD]
                for h in range(HEADS)
            ]
            held[half, lines, :] = jnp.concatenate(heads, axis=0).T
            copies.append(
                pltpu.make_async_copy(held.at[half, lines], ref.at[lines], sems.at[half, k])
            )
            copies[-1].start()
    for copy in copies:
        copy.wait()


def call(kernel, out, *args, scratch=(), scalars=0, held=False, far=False):
    space = pl.ANY if held else pltpu.VMEM
    if held:
        args = [pltpu.with_memory_space_constraint(arg, pltpu.HBM) for arg in args]
    specs = [pl.BlockSpec(memory_space=pltpu.SMEM)] * scalars
    specs += [pl.BlockSpec(memory_space=space)] * (len(args) - scalars)
    return pl.pallas_call(
        kernel,
        out_shape=out,
        in_specs=specs,
        out_specs=jax.tree.map(lambda _: pl.BlockSpec(memory_space=pl.ANY if far else pltpu.VMEM), out),
        scratch_shapes=scratch,
        compiler_params=pltpu.CompilerParams(vmem_limit_bytes=48 * 1024 * 1024),
    )(*args)


def shape(*dims):
    return jax.ShapeDtypeStruct(dims, BF16)


def swap(rows, axes, groups=None):
    return lax.all_to_all(
        rows, axes, split_axis=0, concat_axis=0, tiled=True, axis_index_groups=groups
    )


def body(tokens, w_shared, w_value, cluster_ids, slot_index, cotangent):
    rows = tokens[0]
    place = jnp.stack([lax.axis_index("y"), lax.axis_index("c")]).astype(jnp.int32)
    sent, ext = call(
        send_kernel,
        (shape(LOCAL, 9, 2, LOCAL), shape(LOCAL + 16, WIDTH)),
        cluster_ids.transpose(1, 0, 2),
        rows,
        w_shared,
        w_value,
        cotangent[0],
        scratch=[
            pltpu.VMEM((HEADS, 1, LOCAL), jnp.int32),
            pltpu.VMEM((LOCAL, WIDTH), BF16),
            pltpu.VMEM((WIDTH, PROJ), BF16),
            pltpu.VMEM((WIDTH, PROJ), BF16),
            pltpu.VMEM((LOCAL, PROJ), BF16),
            pltpu.SemaphoreType.DMA((5,)),
        ],
        held=True,
    )

    def shift(pair, dy):
        return lax.ppermute(pair, "y", [(y, (y + dy) % 4) for y in range(4)])

    def flip(part):
        return lax.ppermute(part, "c", [(0, 1), (1, 0)])

    arrived = swap(sent, OWNERS)
    pair = jnp.stack([ext, flip(ext)])
    near = (shift(pair, 1), shift(pair, 3))
    arrived, pair, near, place = lax.optimization_barrier((arrived, pair, near, place))
    exts = [pair, near[0], shift(pair, 2), near[1]]
    arrived = arrived.transpose(1, 0, 2, 3).reshape(9, ROWS, LOCAL)
    worked = call(attend_kernel, shape(LOCAL, 9, 2, LOCAL), arrived)
    back = swap(worked, OWNERS)
    part, cols = call(
        partial_kernel,
        (shape(16, SLOT, LOCAL), shape(8, COLUMNS, LOCAL)),
        place,
        back,
        *exts,
        scratch=[pltpu.VMEM((2, 8, 8, LOCAL), F32), pltpu.VMEM((16 * PIECE + 8, LOCAL), F32)],
        scalars=1,
    )
    keep, give = call(
        forward_kernel,
        (shape(4, MESSAGE, LOCAL), shape(4, MESSAGE, LOCAL)),
        place,
        back,
        cols,
        *exts,
        scratch=[pltpu.VMEM((2, 8, 8, LOCAL), F32), pltpu.VMEM((8, COLUMNS // 2, LOCAL), BF16)],
        scalars=1,
    )
    got = flip(give)
    part = swap(part, ("x", "z"), NEAR)
    part, keep, got = lax.optimization_barrier((part, keep, got))
    part = call(sum_kernel, shape(4, SLOT, LOCAL), part)
    block = call(sum_kernel, shape(16, SLOT, LOCAL), swap(part, "z", FAR))
    block = swap(block, ("x", "z"), NEAR)
    block = call(
        pack_kernel,
        shape(4, WHOLE + 2 * MESSAGE, LOCAL),
        block,
        keep,
        got,
        scratch=[pltpu.VMEM((WHOLE, LOCAL), F32)],
    )
    block = swap(block, "y")
    other = flip(block)
    attention, grad_tokens = call(
        return_kernel,
        (shape(LOCAL, PROJ), shape(LOCAL, WIDTH)),
        place,
        block,
        w_shared,
        w_value,
        scratch=[pltpu.VMEM((8, MESSAGE, LOCAL), BF16)],
        scalars=1,
    )
    grad_shared, grad_value = call(
        finish_kernel,
        (shape(WIDTH, PROJ), shape(WIDTH, PROJ)),
        place,
        block,
        other,
        scratch=[
            pltpu.VMEM((2, WIDTH, PROJ), BF16),
            pltpu.SemaphoreType.DMA((2, WIDTH // LOCAL)),
        ],
        scalars=1,
        far=True,
    )
    return (attention[None], grad_tokens[None], grad_shared, grad_value)


def solution(mesh):
    fine = Mesh(mesh.devices.reshape(4, 4, 16, 2), ("x", "y", "z", "c"))
    in_specs = (
        P("x", TOK, None),
        P(),
        P(),
        P("x", None, TOK),
        P("x", None, TOK),
        P("x", TOK, None),
    )
    out_specs = (P("x", TOK, None), P("x", TOK, None), P(), P())
    return jax.shard_map(body, mesh=fine, in_specs=in_specs, out_specs=out_specs, check_vma=False)
```

```python
import jax
import jax.numpy as jnp
from jax import lax
from jax.experimental import pallas as pl
from jax.experimental.pallas import tpu as pltpu
from jax.sharding import Mesh
from jax.sharding import PartitionSpec as P

F32 = jnp.float32
BF16 = jnp.bfloat16
HEADS = 6
HEAD = 64
ROWS = 256
LOCAL = 128
WIDTH = 768
PROJ = 384
UNUSED = 65536.0
PLANE = ("y", "c")
TOK = ("y", "z", "c")
OWNERS = ("y", "c", "z")
RING = [(3, 4, 9, 14), (2, 7, 8, 13), (1, 6, 11, 12), (0, 5, 10, 15)]
FAR = [list(group) for group in RING]
NEAR = [[x * 16 + RING[n][b] for x in range(4) for n in range(4)] for b in range(4)]
STEPS = [(dy, dc) for dy in range(4) for dc in range(2)]
COLUMNS = 96
PIECE = 36
SLOT = 40
BLOCK = 16
WHOLE = 576
MESSAGE = 96


def iota(shape, dim):
    return lax.broadcasted_iota(jnp.int32, shape, dim)


def dot(a, b, dims=((1,), (0,))):
    return lax.dot_general(a, b, (dims, ((), ())), preferred_element_type=F32)


def send_kernel(*refs):
    sources, (out_ref, ext_ref), targets, sems = refs[:5], refs[5:7], refs[7:12], refs[12]
    copies = [
        pltpu.make_async_copy(source, target, sems.at[n])
        for n, (source, target) in enumerate(zip(sources, targets))
    ]
    for copy in copies:
        copy.start()
    cluster_ref, tok_ref, ws_ref, wv_ref, cot_ref = targets
    sub = iota((LOCAL, LOCAL), 0)
    lane = iota((LOCAL, LOCAL), 1)
    sub_rows = iota((ROWS, LOCAL), 0)
    lane_rows = iota((ROWS, LOCAL), 1)
    copies[0].wait()
    hits = []
    marks = []
    for h in range(HEADS):
        cluster = cluster_ref[h]
        member = (sub == cluster).astype(BF16)
        same = dot(member, member, ((0,), (0,)))
        order = jnp.sum(jnp.where(sub < lane, same, 0.0), axis=0, keepdims=True)
        owner = (cluster & 96) + (cluster & 1) * 16 + ((cluster >> 1) & 15)
        dest = owner * 2 + order.astype(jnp.int32)
        ext_ref[LOCAL:, h * LOCAL : (h + 1) * LOCAL] = jnp.broadcast_to(
            dest.astype(F32), (16, LOCAL)
        ).astype(BF16)
        hit = sub_rows == dest
        used = jnp.sum(jnp.where(hit, 1.0, 0.0), axis=1, keepdims=True)
        hits.append(hit.astype(BF16))
        marks.append(jnp.where((lane_rows == 0) & (used < 0.5), UNUSED, 0.0))
    for copy in copies[1:]:
        copy.wait()
    tokens = tok_ref[...]
    ext_ref[:LOCAL, :] = tokens
    shared = dot(tokens, ws_ref[...]).astype(BF16)
    value = dot(tokens, wv_ref[...]).astype(BF16)
    cot = cot_ref[...]
    blank = jnp.zeros((LOCAL, HEAD), BF16)
    pending = None
    for h in range(HEADS):
        cols = slice(h * HEAD, (h + 1) * HEAD)
        tail = [cot[:, cols], blank] if h % 2 == 0 else [blank, cot[:, cols]]
        packed = jnp.concatenate([shared[:, cols], value[:, cols]] + tail, axis=1)
        moved = dot(hits[h], packed)
        out_ref[:, h] = (moved[:, :LOCAL] + marks[h]).astype(BF16).reshape(LOCAL, 2, LOCAL)
        if h % 2 == 0:
            pending = moved[:, LOCAL:]
        else:
            packed = (pending + moved[:, LOCAL:]).astype(BF16)
            out_ref[:, HEADS + h // 2] = packed.reshape(LOCAL, 2, LOCAL)


def position(row):
    return (row & 192) + ((row >> 1) & 15) * 4 + ((row >> 5) & 1) * 2 + (row & 1)


def spread(block, slot):
    rows = block.shape[0] // 8
    parts = [block[p * rows : (p + 1) * rows] for p in range(8)]
    for bit in (1, 2, 4):
        odd = (slot & bit) != 0
        after = list(parts)
        for p in range(8):
            if p & bit == 0:
                low, high = parts[p], parts[p + bit]
                after[p] = jnp.where(odd, pltpu.roll(high, BLOCK * bit, 1), low)
                after[p + bit] = jnp.where(odd, high, pltpu.roll(low, LOCAL - BLOCK * bit, 1))
        parts = after
    return parts


def attend_kernel(in_ref, out_ref):
    half = ROWS // 2
    lane_rows = iota((ROWS, LOCAL), 1)
    first = lane_rows == 0
    bias_lane = lane_rows == HEAD
    head_lanes = lane_rows < HEAD
    left_causal = position(iota((half, half), 0)) <= position(iota((half, half), 1))
    right_causal = position(iota((ROWS, half), 0)) <= position(iota((ROWS, half), 1) + half)
    slot = iota((ROWS // 8, LOCAL), 1) >> 4
    hidden = jnp.zeros((half, half), BF16)
    pending = None
    for h in range(HEADS):
        block = in_ref[h].astype(F32)
        empty = block[:, :1] > 32768.0
        block = jnp.where(empty & first, 0.0, block)
        query = jnp.where(head_lanes, block * 0.125, jnp.where(bias_lane, 1.0, 0.0)).astype(BF16)
        key = jnp.where(
            head_lanes, block, jnp.where(bias_lane & empty, -1e30, 0.0)
        ).astype(BF16)
        block = block.astype(BF16)
        shared = block[:, :HEAD]
        value = block[:, HEAD:]
        pair = in_ref[HEADS + h // 2]
        cot = pair[:, :HEAD] if h % 2 == 0 else pair[:, HEAD:]
        probs = []
        d_scores = []
        for rows, cols, causal in (
            (slice(0, half), slice(0, half), left_causal),
            (slice(0, ROWS), slice(half, ROWS), right_causal),
        ):
            scores = dot(key[rows], query[cols], ((1,), (1,)))
            scores = jnp.where(causal, scores, -1e30)
            weights = jnp.exp(scores - jnp.max(scores, axis=0, keepdims=True))
            scale = 1.0 / jnp.sum(weights, axis=0, keepdims=True)
            prob = (weights * scale).astype(BF16)
            d_prob = dot(value[rows], cot[cols], ((1,), (1,)))
            wide = prob.astype(F32)
            delta = jnp.sum(wide * d_prob, axis=0, keepdims=True)
            probs.append(prob)
            d_scores.append((wide * (d_prob - delta)).astype(BF16))
        probs = jnp.concatenate([jnp.concatenate([probs[0], hidden], axis=0), probs[1]], axis=1)
        d_scores = jnp.concatenate(
            [jnp.concatenate([d_scores[0], hidden], axis=0), d_scores[1]], axis=1
        )
        turned = block.T
        above = dot(turned[:HEAD], d_scores)
        out = dot(turned[HEAD:], probs)
        both = jnp.concatenate([above, out], axis=0).T
        d_shared = (dot(d_scores, shared) + both[:, :HEAD]) * 0.125
        d_value = dot(probs, cot)
        for m, part in enumerate(spread(jnp.concatenate([d_shared, d_value], axis=1), slot)):
            n = h * 8 + m
            out_ref[n // 6 * 16 : (n // 6 + 1) * 16, n % 6] = part.astype(BF16).reshape(16, 2, LOCAL)
        if h % 2 == 0:
            pending = both
        else:
            k = HEADS + h // 2
            joined = jnp.where(head_lanes, pltpu.roll(pending, HEAD, 1), both).astype(BF16)
            out_ref[:, k] = joined.reshape(LOCAL, 2, LOCAL)


def index_of(place_ref, dy, dc):
    return lax.rem(place_ref[0] + dy, 4) * 2 + lax.rem(place_ref[1] + dc, 2)


def partial_kernel(place_ref, in_ref, *refs):
    exts, (out_ref, keep_ref, give_ref), (dests, cols, scratch) = refs[:4], refs[4:7], refs[7:]
    here = place_ref[1]
    j = place_ref[0] * 2 + here
    head = (j * 3 // 4, (j * 6 + 5) // 8)
    lane_slot = iota((ROWS, LOCAL), 1) >> 4
    sub_rows = iota((ROWS, LOCAL), 0).astype(F32)
    for n, (dy, dc) in enumerate(STEPS):
        source = index_of(place_ref, 4 - dy, dc)
        for i in range(2):
            lanes = pl.ds(pl.multiple_of(head[i] * LOCAL, LOCAL), LOCAL)
            dests[i, source] = exts[n // 2][n % 2, LOCAL:, lanes].astype(F32)[:8]
    turned = [in_ref[:, b].reshape(ROWS, LOCAL).astype(F32) for b in range(6)]
    turned = [pltpu.roll(rows, BLOCK * b, 1) if b else rows for b, rows in enumerate(turned)]
    limit = lax.rem(j, 4)
    limit = jnp.where(limit == 1, 2, jnp.where(limit == 2, 4, 6))
    for p in range(8):
        rows = turned[0]
        for b in range(1, 6):
            rows = jnp.where(lane_slot == (b + p) % 8, turned[b], rows)
        routes = [(sub_rows == dests[i, p, :1]).astype(BF16) for i in range(2)]
        found = dot(rows.astype(BF16), jnp.concatenate(routes, axis=1), ((0,), (0,)))
        blocks = []
        for b in range(6):
            cut = slice((b + p) % 8 * BLOCK, ((b + p) % 8 + 1) * BLOCK)
            blocks.append(jnp.where(b < limit, found[cut, :LOCAL], found[cut, LOCAL:]))
        cols[p] = jnp.concatenate(blocks, axis=0).astype(BF16)
    total = None
    for n, (dy, dc) in enumerate(STEPS):
        source = index_of(place_ref, 4 - dy, dc)
        term = dot(cols[source], exts[n // 2][n % 2, :LOCAL, :])
        total = term if total is None else total + term
    for k in range(WIDTH // LOCAL):
        scratch[k * COLUMNS : (k + 1) * COLUMNS, :] = total[:, k * LOCAL : (k + 1) * LOCAL]
    scratch[16 * PIECE :, :] = jnp.zeros((8, LOCAL), F32)
    for i in range(16):
        out_ref[i] = scratch[i * PIECE : i * PIECE + SLOT, :].astype(BF16)
    for y in range(4):
        keep_ref[y] = cols[y * 2 + here]
        give_ref[y] = cols[y * 2 + 1 - here]


def output_kernel(in_ref, ext_ref, att_ref):
    sub_rows = iota((ROWS, LOCAL), 0).astype(F32)
    head_lanes = iota((LOCAL, LOCAL), 1) < HEAD
    dests = ext_ref[0, LOCAL:, :].astype(F32)[:1]
    for k in range(HEADS // 2):
        rows = in_ref[:, HEADS + k].reshape(ROWS, LOCAL)
        found = []
        for h in (2 * k, 2 * k + 1):
            route = (sub_rows == dests[:, h * LOCAL : (h + 1) * LOCAL]).astype(BF16)
            found.append(dot(route, rows, ((0,), (0,))))
        both = jnp.where(head_lanes, found[0], found[1])
        att_ref[:, k * LOCAL : (k + 1) * LOCAL] = both.astype(BF16)


def pack_kernel(block_ref, keep_ref, got_ref, out_ref, scratch):
    for i in range(16):
        scratch[i * PIECE : (i + 1) * PIECE, :] = block_ref[i].astype(F32)[:PIECE]
    block = scratch[...].astype(BF16)
    for y in range(4):
        out_ref[y, :WHOLE, :] = block
        out_ref[y, WHOLE : WHOLE + MESSAGE, :] = keep_ref[y]
        out_ref[y, WHOLE + MESSAGE :, :] = got_ref[y]


def return_kernel(place_ref, all_ref, ws_ref, wv_ref, grad_ref, held):
    here = place_ref[1]
    for y in range(4):
        held[y * 2 + here] = all_ref[y, WHOLE : WHOLE + MESSAGE, :]
        held[y * 2 + 1 - here] = all_ref[y, WHOLE + MESSAGE :, :]

    def columns(first):
        rows = [
            held[n // 6, n % 6 * BLOCK : (n % 6 + 1) * BLOCK, :]
            for h in range(HEADS)
            for n in range(h * 8 + first, h * 8 + first + 4)
        ]
        return jnp.concatenate(rows, axis=0).astype(F32).T.astype(BF16)

    left = columns(0)
    right = columns(4)
    total = dot(left, ws_ref[...], ((1,), (1,))) + dot(right, wv_ref[...], ((1,), (1,)))
    grad_ref[...] = total.astype(BF16)


def sum_kernel(in_ref, out_ref):
    total = in_ref[0].astype(F32)
    for i in range(1, in_ref.shape[0]):
        total = total + in_ref[i].astype(F32)
    total = total.astype(BF16)
    for i in range(out_ref.shape[0]):
        out_ref[i] = total


def finish_kernel(place_ref, mine_ref, other_ref, shared_ref, value_ref, held, sems):
    first = place_ref[1] == 0
    copies = []
    for k in range(WIDTH // LOCAL):
        rows = slice(k * COLUMNS, (k + 1) * COLUMNS)
        strip = []
        for y in range(4):
            mine = mine_ref[y, rows, :]
            other = other_ref[y, rows, :]
            strip += [jnp.where(first, mine, other), jnp.where(first, other, mine)]
        strip = jnp.concatenate(strip, axis=0)
        lines = slice(k * LOCAL, (k + 1) * LOCAL)
        for half, ref in enumerate((shared_ref, value_ref)):
            heads = [
                strip[h * LOCAL + half * HEAD : h * LOCAL + (half + 1) * HEAD]
                for h in range(HEADS)
            ]
            held[half, lines, :] = jnp.concatenate(heads, axis=0).T
            copies.append(
                pltpu.make_async_copy(held.at[half, lines], ref.at[lines], sems.at[half, k])
            )
            copies[-1].start()
    for copy in copies:
        copy.wait()


def call(kernel, out, *args, scratch=(), scalars=0, held=False, far=()):
    if held:
        args = [pltpu.with_memory_space_constraint(arg, pltpu.HBM) for arg in args]
    specs = [pl.BlockSpec(memory_space=pltpu.SMEM)] * scalars
    specs += [pl.BlockSpec(memory_space=pl.ANY if held else pltpu.VMEM)] * (len(args) - scalars)
    outs = [
        pl.BlockSpec(memory_space=pl.ANY if n in far else pltpu.VMEM) for n in range(len(out))
    ]
    return pl.pallas_call(
        kernel,
        out_shape=out,
        in_specs=specs,
        out_specs=outs,
        scratch_shapes=scratch,
        compiler_params=pltpu.CompilerParams(vmem_limit_bytes=48 * 1024 * 1024),
    )(*args)


def shape(*dims):
    return jax.ShapeDtypeStruct(dims, BF16)


def swap(rows, axes, groups=None):
    return lax.all_to_all(
        rows, axes, split_axis=0, concat_axis=0, tiled=True, axis_index_groups=groups
    )


def body(tokens, w_shared, w_value, cluster_ids, slot_index, cotangent):
    rows = tokens[0]
    place = jnp.stack([lax.axis_index("y"), lax.axis_index("c")]).astype(jnp.int32)
    sent, ext = call(
        send_kernel,
        (shape(LOCAL, 9, 2, LOCAL), shape(LOCAL + 16, WIDTH)),
        cluster_ids.transpose(1, 0, 2),
        rows,
        w_shared,
        w_value,
        cotangent[0],
        scratch=[
            pltpu.VMEM((HEADS, 1, LOCAL), jnp.int32),
            pltpu.VMEM((LOCAL, WIDTH), BF16),
            pltpu.VMEM((WIDTH, PROJ), BF16),
            pltpu.VMEM((WIDTH, PROJ), BF16),
            pltpu.VMEM((LOCAL, PROJ), BF16),
            pltpu.SemaphoreType.DMA((5,)),
        ],
        held=True,
    )

    def shift(pair, dy):
        return lax.ppermute(pair, "y", [(y, (y + dy) % 4) for y in range(4)])

    def flip(part):
        return lax.ppermute(part, "c", [(0, 1), (1, 0)])

    arrived = swap(sent, OWNERS)
    pair = jnp.stack([ext, flip(ext)])
    near = (shift(pair, 1), shift(pair, 3))
    arrived, pair, near, place = lax.optimization_barrier((arrived, pair, near, place))
    exts = [pair, near[0], shift(pair, 2), near[1]]
    arrived = arrived.transpose(1, 0, 2, 3).reshape(9, ROWS, LOCAL)
    (worked,) = call(
        attend_kernel,
        [shape(LOCAL, 9, 2, LOCAL)],
        arrived,
    )
    back = swap(worked, OWNERS)
    part, keep, give = call(
        partial_kernel,
        [shape(16, SLOT, LOCAL), shape(4, MESSAGE, LOCAL), shape(4, MESSAGE, LOCAL)],
        place,
        back,
        *exts,
        scratch=[
            pltpu.VMEM((2, 8, 8, LOCAL), F32),
            pltpu.VMEM((8, COLUMNS, LOCAL), BF16),
            pltpu.VMEM((16 * PIECE + 8, LOCAL), F32),
        ],
        scalars=1,
    )
    (attention,) = call(output_kernel, [shape(LOCAL, PROJ)], back, pair)
    part = swap(part, ("x", "z"), NEAR)
    part, keep, got, attention = lax.optimization_barrier((part, keep, flip(give), attention))
    (part,) = call(sum_kernel, [shape(4, SLOT, LOCAL)], part)
    (block,) = call(sum_kernel, [shape(16, SLOT, LOCAL)], swap(part, "z", FAR))
    (block,) = call(
        pack_kernel,
        [shape(4, WHOLE + 2 * MESSAGE, LOCAL)],
        swap(block, ("x", "z"), NEAR),
        keep,
        got,
        scratch=[pltpu.VMEM((WHOLE, LOCAL), F32)],
    )
    block = swap(block, "y")
    other = flip(block)
    (grad_tokens,) = call(
        return_kernel,
        [shape(LOCAL, WIDTH)],
        place,
        block,
        w_shared,
        w_value,
        scratch=[pltpu.VMEM((8, MESSAGE, LOCAL), BF16)],
        scalars=1,
    )
    grad_shared, grad_value = call(
        finish_kernel,
        (shape(WIDTH, PROJ), shape(WIDTH, PROJ)),
        place,
        block,
        other,
        scratch=[
            pltpu.VMEM((2, WIDTH, PROJ), BF16),
            pltpu.SemaphoreType.DMA((2, WIDTH // LOCAL)),
        ],
        scalars=1,
        far=(0, 1),
    )
    return (attention[None], grad_tokens[None], grad_shared, grad_value)


def solution(mesh):
    fine = Mesh(mesh.devices.reshape(4, 4, 16, 2), ("x", "y", "z", "c"))
    in_specs = (
        P("x", TOK, None),
        P(),
        P(),
        P("x", None, TOK),
        P("x", None, TOK),
        P("x", TOK, None),
    )
    out_specs = (P("x", TOK, None), P("x", TOK, None), P(), P())
    return jax.shard_map(body, mesh=fine, in_specs=in_specs, out_specs=out_specs, check_vma=False)
```

```python
import jax
import jax.numpy as jnp
from jax import lax
from jax.experimental import pallas as pl
from jax.experimental.pallas import tpu as pltpu
from jax.sharding import Mesh
from jax.sharding import PartitionSpec as P

F32 = jnp.float32
BF16 = jnp.bfloat16
HEADS = 6
HEAD = 64
ROWS = 256
LOCAL = 128
WIDTH = 768
PROJ = 384
UNUSED = 65536.0
PLANE = ("y", "c")
TOK = ("y", "z", "c")
OWNERS = ("y", "c", "z")
RING = [(3, 4, 9, 14), (2, 7, 8, 13), (1, 6, 11, 12), (0, 5, 10, 15)]
FAR = [list(group) for group in RING]
NEAR = [[x * 16 + RING[n][b] for x in range(4) for n in range(4)] for b in range(4)]
STEPS = [(dy, dc) for dy in range(4) for dc in range(2)]
COLUMNS = 96
PIECE = 36
SLOT = 40
BLOCK = 16
WHOLE = 576
MESSAGE = 96


def iota(shape, dim):
    return lax.broadcasted_iota(jnp.int32, shape, dim)


def dot(a, b, dims=((1,), (0,))):
    return lax.dot_general(a, b, (dims, ((), ())), preferred_element_type=F32)


def send_kernel(*refs):
    sources, (out_ref, ext_ref), targets, sems = refs[:5], refs[5:7], refs[7:12], refs[12]
    copies = [
        pltpu.make_async_copy(source, target, sems.at[n])
        for n, (source, target) in enumerate(zip(sources, targets))
    ]
    for copy in copies:
        copy.start()
    cluster_ref, tok_ref, ws_ref, wv_ref, cot_ref = targets
    sub = iota((LOCAL, LOCAL), 0)
    lane = iota((LOCAL, LOCAL), 1)
    sub_rows = iota((ROWS, LOCAL), 0)
    lane_rows = iota((ROWS, LOCAL), 1)
    copies[0].wait()
    hits = []
    marks = []
    for h in range(HEADS):
        cluster = cluster_ref[h]
        member = (sub == cluster).astype(BF16)
        same = dot(member, member, ((0,), (0,)))
        order = jnp.sum(jnp.where(sub < lane, same, 0.0), axis=0, keepdims=True)
        owner = (cluster & 96) + (cluster & 1) * 16 + ((cluster >> 1) & 15)
        dest = owner * 2 + order.astype(jnp.int32)
        ext_ref[LOCAL:, h * LOCAL : (h + 1) * LOCAL] = jnp.broadcast_to(
            dest.astype(F32), (16, LOCAL)
        ).astype(BF16)
        hit = sub_rows == dest
        used = jnp.sum(jnp.where(hit, 1.0, 0.0), axis=1, keepdims=True)
        hits.append(hit.astype(BF16))
        marks.append(jnp.where((lane_rows == 0) & (used < 0.5), UNUSED, 0.0))
    for copy in copies[1:]:
        copy.wait()
    tokens = tok_ref[...]
    ext_ref[:LOCAL, :] = tokens
    shared = dot(tokens, ws_ref[...]).astype(BF16)
    value = dot(tokens, wv_ref[...]).astype(BF16)
    cot = cot_ref[...]
    blank = jnp.zeros((LOCAL, HEAD), BF16)
    pending = None
    for h in range(HEADS):
        cols = slice(h * HEAD, (h + 1) * HEAD)
        tail = [cot[:, cols], blank] if h % 2 == 0 else [blank, cot[:, cols]]
        packed = jnp.concatenate([shared[:, cols], value[:, cols]] + tail, axis=1)
        moved = dot(hits[h], packed)
        out_ref[:, h] = (moved[:, :LOCAL] + marks[h]).astype(BF16).reshape(LOCAL, 2, LOCAL)
        if h % 2 == 0:
            pending = moved[:, LOCAL:]
        else:
            packed = (pending + moved[:, LOCAL:]).astype(BF16)
            out_ref[:, HEADS + h // 2] = packed.reshape(LOCAL, 2, LOCAL)


def position(row):
    return (row & 192) + ((row >> 1) & 15) * 4 + ((row >> 5) & 1) * 2 + (row & 1)


def spread(block, slot):
    rows = block.shape[0] // 8
    parts = [block[p * rows : (p + 1) * rows] for p in range(8)]
    for bit in (1, 2, 4):
        odd = (slot & bit) != 0
        after = list(parts)
        for p in range(8):
            if p & bit == 0:
                low, high = parts[p], parts[p + bit]
                after[p] = jnp.where(odd, pltpu.roll(high, BLOCK * bit, 1), low)
                after[p + bit] = jnp.where(odd, high, pltpu.roll(low, LOCAL - BLOCK * bit, 1))
        parts = after
    return parts


def attend_kernel(in_ref, out_ref):
    half = ROWS // 2
    lane_rows = iota((ROWS, LOCAL), 1)
    first = lane_rows == 0
    bias_lane = lane_rows == HEAD
    head_lanes = lane_rows < HEAD
    left_causal = position(iota((half, half), 0)) <= position(iota((half, half), 1))
    right_causal = position(iota((ROWS, half), 0)) <= position(iota((ROWS, half), 1) + half)
    slot = iota((ROWS // 8, LOCAL), 1) >> 4
    hidden = jnp.zeros((half, half), BF16)
    pending = None
    for start in range(0, HEADS, 3):
        group = range(start, start + 3)
        blocks, keys, queries, cots = {}, {}, {}, {}
        for h in group:
            block = in_ref[h].astype(F32)
            empty = block[:, :1] > 32768.0
            block = jnp.where(empty & first, 0.0, block)
            query = jnp.where(head_lanes, block * 0.125, jnp.where(bias_lane, 1.0, 0.0))
            queries[h] = query.astype(BF16)
            keys[h] = jnp.where(
                head_lanes, block, jnp.where(bias_lane & empty, -1e30, 0.0)
            ).astype(BF16)
            blocks[h] = block.astype(BF16)
            pair = in_ref[HEADS + h // 2]
            cots[h] = pair[:, :HEAD] if h % 2 == 0 else pair[:, HEAD:]
        tiles = (
            (slice(0, half), slice(0, half), left_causal),
            (slice(0, ROWS), slice(half, ROWS), right_causal),
        )
        scores, d_probs = {}, {}
        for h in group:
            scores[h] = dot(keys[h], queries[h], ((1,), (1,)))
            d_probs[h] = dot(blocks[h][:, HEAD:], cots[h], ((1,), (1,)))
        probs, d_scores = {}, {}
        for h in group:
            parts = []
            for rows, cols, causal in tiles:
                tile = jnp.where(causal, scores[h][rows, cols], -1e30)
                weights = jnp.exp(tile - jnp.max(tile, axis=0, keepdims=True))
                scale = 1.0 / jnp.sum(weights, axis=0, keepdims=True)
                parts.append((weights * scale).astype(BF16))
            lower = [
                (parts[n].astype(F32), d_probs[h][rows, cols])
                for n, (rows, cols, causal) in enumerate(tiles)
            ]
            slopes = [
                (wide * (d_prob - jnp.sum(wide * d_prob, axis=0, keepdims=True))).astype(BF16)
                for wide, d_prob in lower
            ]
            for held, done in ((probs, parts), (d_scores, slopes)):
                left = jnp.concatenate([done[0], hidden], axis=0)
                held[h] = jnp.concatenate([left, done[1]], axis=1)
        for h in group:
            turned = blocks[h].T
            above = dot(turned[:HEAD], d_scores[h])
            above = above + dot(turned[:HEAD], d_scores[h], ((1,), (1,)))
            out = dot(turned[HEAD:], probs[h])
            d_value = dot(cots[h].T, probs[h], ((1,), (1,)))
            grads = jnp.concatenate([above * 0.125, d_value], axis=0).T
            for m, part in enumerate(spread(grads, slot)):
                n = h * 8 + m
                part = part.astype(BF16).reshape(16, 2, LOCAL)
                out_ref[n // 6 * 16 : (n // 6 + 1) * 16, n % 6] = part
            if h % 2 == 0:
                pending = out
            else:
                k = HEADS + h // 2
                joined = jnp.concatenate([pending, out], axis=0).T.astype(BF16)
                out_ref[:, k] = joined.reshape(LOCAL, 2, LOCAL)


def index_of(place_ref, dy, dc):
    return lax.rem(place_ref[0] + dy, 4) * 2 + lax.rem(place_ref[1] + dc, 2)


def partial_kernel(place_ref, in_ref, *refs):
    exts, (out_ref, keep_ref, give_ref), (dests, cols, scratch) = refs[:4], refs[4:7], refs[7:]
    here = place_ref[1]
    j = place_ref[0] * 2 + here
    head = (j * 3 // 4, (j * 6 + 5) // 8)
    lane_slot = iota((ROWS, LOCAL), 1) >> 4
    sub_rows = iota((ROWS, LOCAL), 0).astype(F32)
    for n, (dy, dc) in enumerate(STEPS):
        source = index_of(place_ref, 4 - dy, dc)
        for i in range(2):
            lanes = pl.ds(pl.multiple_of(head[i] * LOCAL, LOCAL), LOCAL)
            dests[i, source] = exts[n // 2][n % 2, LOCAL:, lanes].astype(F32)[:8]
    turned = [in_ref[:, b].reshape(ROWS, LOCAL) for b in range(6)]
    turned = [pltpu.roll(rows.astype(F32), BLOCK * b, 1).astype(BF16) if b else rows for b, rows in enumerate(turned)]
    limit = lax.rem(j, 4)
    limit = jnp.where(limit == 1, 2, jnp.where(limit == 2, 4, 6))
    for p in range(8):
        rows = turned[0]
        for b in range(1, 6):
            rows = jnp.where(lane_slot == (b + p) % 8, turned[b], rows)
        routes = [(sub_rows == dests[i, p, :1]).astype(BF16) for i in range(2)]
        found = dot(rows, jnp.concatenate(routes, axis=1), ((0,), (0,)))
        blocks = []
        for b in range(6):
            cut = slice((b + p) % 8 * BLOCK, ((b + p) % 8 + 1) * BLOCK)
            blocks.append(jnp.where(b < limit, found[cut, :LOCAL], found[cut, LOCAL:]))
        cols[p] = jnp.concatenate(blocks, axis=0).astype(BF16)
    total = None
    for dy in range(4):
        near = [cols[index_of(place_ref, 4 - dy, dc)] for dc in range(2)]
        rows = exts[dy][:, :LOCAL, :].reshape(2 * LOCAL, WIDTH)
        term = dot(jnp.concatenate(near, axis=1), rows)
        total = term if total is None else total + term
    for k in range(WIDTH // LOCAL):
        scratch[k * COLUMNS : (k + 1) * COLUMNS, :] = total[:, k * LOCAL : (k + 1) * LOCAL]
    scratch[16 * PIECE :, :] = jnp.zeros((8, LOCAL), F32)
    for i in range(16):
        out_ref[i] = scratch[i * PIECE : i * PIECE + SLOT, :].astype(BF16)
    for y in range(4):
        keep_ref[y] = cols[y * 2 + here]
        give_ref[y] = cols[y * 2 + 1 - here]


def output_kernel(in_ref, ext_ref, att_ref):
    sub_rows = iota((ROWS, LOCAL), 0).astype(F32)
    head_lanes = iota((LOCAL, LOCAL), 1) < HEAD
    dests = ext_ref[0, LOCAL:, :].astype(F32)[:1]
    for k in range(HEADS // 2):
        rows = in_ref[:, HEADS + k].reshape(ROWS, LOCAL)
        found = []
        for h in (2 * k, 2 * k + 1):
            route = (sub_rows == dests[:, h * LOCAL : (h + 1) * LOCAL]).astype(BF16)
            found.append(dot(route, rows, ((0,), (0,))))
        both = jnp.where(head_lanes, found[0], found[1])
        att_ref[:, k * LOCAL : (k + 1) * LOCAL] = both.astype(BF16)


def pack_kernel(block_ref, keep_ref, got_ref, out_ref, scratch):
    for i in range(16):
        scratch[i * PIECE : (i + 1) * PIECE, :] = block_ref[i].astype(F32)[:PIECE]
    block = scratch[...].astype(BF16)
    for y in range(4):
        out_ref[y, :WHOLE, :] = block
        out_ref[y, WHOLE : WHOLE + MESSAGE, :] = keep_ref[y]
        out_ref[y, WHOLE + MESSAGE :, :] = got_ref[y]


def return_kernel(place_ref, all_ref, ws_ref, wv_ref, grad_ref, held):
    here = place_ref[1]
    for y in range(4):
        held[y * 2 + here] = all_ref[y, WHOLE : WHOLE + MESSAGE, :]
        held[y * 2 + 1 - here] = all_ref[y, WHOLE + MESSAGE :, :]

    def columns(first):
        rows = [
            held[n // 6, n % 6 * BLOCK : (n % 6 + 1) * BLOCK, :]
            for h in range(HEADS)
            for n in range(h * 8 + first, h * 8 + first + 4)
        ]
        return jnp.concatenate(rows, axis=0).astype(F32).T.astype(BF16)

    left = columns(0)
    right = columns(4)
    total = dot(left, ws_ref[...], ((1,), (1,))) + dot(right, wv_ref[...], ((1,), (1,)))
    grad_ref[...] = total.astype(BF16)


def sum_kernel(in_ref, out_ref):
    total = in_ref[0].astype(F32)
    for i in range(1, in_ref.shape[0]):
        total = total + in_ref[i].astype(F32)
    total = total.astype(BF16)
    for i in range(out_ref.shape[0]):
        out_ref[i] = total


def finish_kernel(place_ref, mine_ref, other_ref, shared_ref, value_ref, held, sems):
    first = place_ref[1] == 0
    copies = []
    for k in range(WIDTH // LOCAL):
        rows = slice(k * COLUMNS, (k + 1) * COLUMNS)
        strip = []
        for y in range(4):
            mine = mine_ref[y, rows, :]
            other = other_ref[y, rows, :]
            strip += [jnp.where(first, mine, other), jnp.where(first, other, mine)]
        strip = jnp.concatenate(strip, axis=0)
        lines = slice(k * LOCAL, (k + 1) * LOCAL)
        for half, ref in enumerate((shared_ref, value_ref)):
            heads = [
                strip[h * LOCAL + half * HEAD : h * LOCAL + (half + 1) * HEAD]
                for h in range(HEADS)
            ]
            held[half, lines, :] = jnp.concatenate(heads, axis=0).T
            copies.append(
                pltpu.make_async_copy(held.at[half, lines], ref.at[lines], sems.at[half, k])
            )
            copies[-1].start()
    for copy in copies:
        copy.wait()


def call(kernel, out, *args, scratch=(), scalars=0, held=False, far=()):
    if held:
        args = [pltpu.with_memory_space_constraint(arg, pltpu.HBM) for arg in args]
    specs = [pl.BlockSpec(memory_space=pltpu.SMEM)] * scalars
    specs += [pl.BlockSpec(memory_space=pl.ANY if held else pltpu.VMEM)] * (len(args) - scalars)
    outs = [
        pl.BlockSpec(memory_space=pl.ANY if n in far else pltpu.VMEM) for n in range(len(out))
    ]
    return pl.pallas_call(
        kernel,
        out_shape=out,
        in_specs=specs,
        out_specs=outs,
        scratch_shapes=scratch,
        compiler_params=pltpu.CompilerParams(vmem_limit_bytes=48 * 1024 * 1024),
    )(*args)


def shape(*dims):
    return jax.ShapeDtypeStruct(dims, BF16)


def swap(rows, axes, groups=None):
    return lax.all_to_all(
        rows, axes, split_axis=0, concat_axis=0, tiled=True, axis_index_groups=groups
    )


def body(tokens, w_shared, w_value, cluster_ids, slot_index, cotangent):
    rows = tokens[0]
    place = jnp.stack([lax.axis_index("y"), lax.axis_index("c")]).astype(jnp.int32)
    sent, ext = call(
        send_kernel,
        (shape(LOCAL, 9, 2, LOCAL), shape(LOCAL + 16, WIDTH)),
        cluster_ids.transpose(1, 0, 2),
        rows,
        w_shared,
        w_value,
        cotangent[0],
        scratch=[
            pltpu.VMEM((HEADS, 1, LOCAL), jnp.int32),
            pltpu.VMEM((LOCAL, WIDTH), BF16),
            pltpu.VMEM((WIDTH, PROJ), BF16),
            pltpu.VMEM((WIDTH, PROJ), BF16),
            pltpu.VMEM((LOCAL, PROJ), BF16),
            pltpu.SemaphoreType.DMA((5,)),
        ],
        held=True,
    )

    def shift(pair, dy):
        return lax.ppermute(pair, "y", [(y, (y + dy) % 4) for y in range(4)])

    def flip(part):
        return lax.ppermute(part, "c", [(0, 1), (1, 0)])

    arrived = swap(sent, OWNERS)
    pair = jnp.stack([ext, flip(ext)])
    near = (shift(pair, 1), shift(pair, 3))
    arrived, pair, near, place = lax.optimization_barrier((arrived, pair, near, place))
    exts = [pair, near[0], shift(pair, 2), near[1]]
    arrived = arrived.transpose(1, 0, 2, 3).reshape(9, ROWS, LOCAL)
    (worked,) = call(
        attend_kernel,
        [shape(LOCAL, 9, 2, LOCAL)],
        arrived,
    )
    back = swap(worked, OWNERS)
    part, keep, give = call(
        partial_kernel,
        [shape(16, SLOT, LOCAL), shape(4, MESSAGE, LOCAL), shape(4, MESSAGE, LOCAL)],
        place,
        back,
        *exts,
        scratch=[
            pltpu.VMEM((2, 8, 8, LOCAL), F32),
            pltpu.VMEM((8, COLUMNS, LOCAL), BF16),
            pltpu.VMEM((16 * PIECE + 8, LOCAL), F32),
        ],
        scalars=1,
    )
    (attention,) = call(output_kernel, [shape(LOCAL, PROJ)], back, pair)
    part = swap(part, ("x", "z"), NEAR)
    part, keep, got, attention = lax.optimization_barrier((part, keep, flip(give), attention))
    (part,) = call(sum_kernel, [shape(4, SLOT, LOCAL)], part)
    (block,) = call(sum_kernel, [shape(16, SLOT, LOCAL)], swap(part, "z", FAR))
    (block,) = call(
        pack_kernel,
        [shape(4, WHOLE + 2 * MESSAGE, LOCAL)],
        swap(block, ("x", "z"), NEAR),
        keep,
        got,
        scratch=[pltpu.VMEM((WHOLE, LOCAL), F32)],
    )
    block = swap(block, "y")
    other = flip(block)
    (grad_tokens,) = call(
        return_kernel,
        [shape(LOCAL, WIDTH)],
        place,
        block,
        w_shared,
        w_value,
        scratch=[pltpu.VMEM((8, MESSAGE, LOCAL), BF16)],
        scalars=1,
    )
    grad_shared, grad_value = call(
        finish_kernel,
        (shape(WIDTH, PROJ), shape(WIDTH, PROJ)),
        place,
        block,
        other,
        scratch=[
            pltpu.VMEM((2, WIDTH, PROJ), BF16),
            pltpu.SemaphoreType.DMA((2, WIDTH // LOCAL)),
        ],
        scalars=1,
        far=(0, 1),
    )
    return (attention[None], grad_tokens[None], grad_shared, grad_value)


def solution(mesh):
    fine = Mesh(mesh.devices.reshape(4, 4, 16, 2), ("x", "y", "z", "c"))
    in_specs = (
        P("x", TOK, None),
        P(),
        P(),
        P("x", None, TOK),
        P("x", None, TOK),
        P("x", TOK, None),
    )
    out_specs = (P("x", TOK, None), P("x", TOK, None), P(), P())
    return jax.shard_map(body, mesh=fine, in_specs=in_specs, out_specs=out_specs, check_vma=False)
```

```python
import jax
import jax.numpy as jnp
from jax import lax
from jax.experimental import pallas as pl
from jax.experimental.pallas import tpu as pltpu
from jax.sharding import Mesh
from jax.sharding import PartitionSpec as P

F32 = jnp.float32
BF16 = jnp.bfloat16
HEADS = 6
HEAD = 64
ROWS = 256
LOCAL = 128
WIDTH = 768
PROJ = 384
UNUSED = 65536.0
PLANE = ("y", "c")
TOK = ("y", "z", "c")
OWNERS = ("y", "c", "z")
RING = [(3, 4, 9, 14), (2, 7, 8, 13), (1, 6, 11, 12), (0, 5, 10, 15)]
FAR = [list(group) for group in RING]
QUARTER = [[group[b] for group in RING] for b in range(4)]
NEAR = [[x * 16 + RING[n][b] for x in range(4) for n in range(4)] for b in range(4)]
STEPS = [(dy, dc) for dy in range(4) for dc in range(2)]
COLUMNS = 96
PIECE = 36
SLOT = 40
BLOCK = 16
WHOLE = 576


def iota(shape, dim):
    return lax.broadcasted_iota(jnp.int32, shape, dim)


def dot(a, b, dims=((1,), (0,))):
    return lax.dot_general(a, b, (dims, ((), ())), preferred_element_type=F32)


def send_kernel(*refs):
    sources, (out_ref, ext_ref), targets, sems = refs[:5], refs[5:7], refs[7:12], refs[12]
    copies = [
        pltpu.make_async_copy(source, target, sems.at[n])
        for n, (source, target) in enumerate(zip(sources, targets))
    ]
    for copy in copies:
        copy.start()
    cluster_ref, tok_ref, ws_ref, wv_ref, cot_ref = targets
    sub = iota((LOCAL, LOCAL), 0)
    lane = iota((LOCAL, LOCAL), 1)
    sub_rows = iota((ROWS, LOCAL), 0)
    lane_rows = iota((ROWS, LOCAL), 1)
    copies[0].wait()
    hits = []
    marks = []
    for h in range(HEADS):
        cluster = cluster_ref[h]
        member = (sub == cluster).astype(BF16)
        same = dot(member, member, ((0,), (0,)))
        order = jnp.sum(jnp.where(sub < lane, same, 0.0), axis=0, keepdims=True)
        owner = (cluster & 96) + (cluster & 1) * 16 + ((cluster >> 1) & 15)
        dest = owner * 2 + order.astype(jnp.int32)
        ext_ref[LOCAL:, h * LOCAL : (h + 1) * LOCAL] = jnp.broadcast_to(
            dest.astype(F32), (16, LOCAL)
        ).astype(BF16)
        hit = sub_rows == dest
        used = jnp.sum(jnp.where(hit, 1.0, 0.0), axis=1, keepdims=True)
        hits.append(hit.astype(BF16))
        marks.append(jnp.where((lane_rows == 0) & (used < 0.5), UNUSED, 0.0))
    for copy in copies[1:]:
        copy.wait()
    tokens = tok_ref[...]
    ext_ref[:LOCAL, :] = tokens
    shared = dot(tokens, ws_ref[...]).astype(BF16)
    value = dot(tokens, wv_ref[...]).astype(BF16)
    cot = cot_ref[...]
    blank = jnp.zeros((LOCAL, HEAD), BF16)
    pending = None
    for h in range(HEADS):
        cols = slice(h * HEAD, (h + 1) * HEAD)
        tail = [cot[:, cols], blank] if h % 2 == 0 else [blank, cot[:, cols]]
        packed = jnp.concatenate([shared[:, cols], value[:, cols]] + tail, axis=1)
        moved = dot(hits[h], packed)
        out_ref[:, h] = (moved[:, :LOCAL] + marks[h]).astype(BF16).reshape(LOCAL, 2, LOCAL)
        if h % 2 == 0:
            pending = moved[:, LOCAL:]
        else:
            packed = (pending + moved[:, LOCAL:]).astype(BF16)
            out_ref[:, HEADS + h // 2] = packed.reshape(LOCAL, 2, LOCAL)


def position(row):
    return (row & 192) + ((row >> 1) & 15) * 4 + ((row >> 5) & 1) * 2 + (row & 1)


def spread(block, slot):
    rows = block.shape[0] // 8
    parts = [block[p * rows : (p + 1) * rows] for p in range(8)]
    for bit in (1, 2, 4):
        odd = (slot & bit) != 0
        after = list(parts)
        for p in range(8):
            if p & bit == 0:
                low, high = parts[p], parts[p + bit]
                after[p] = jnp.where(odd, pltpu.roll(high, BLOCK * bit, 1), low)
                after[p + bit] = jnp.where(odd, high, pltpu.roll(low, LOCAL - BLOCK * bit, 1))
        parts = after
    return parts


def attend_kernel(in_ref, out_ref):
    half = ROWS // 2
    lane_rows = iota((ROWS, LOCAL), 1)
    first = lane_rows == 0
    bias_lane = lane_rows == HEAD
    head_lanes = lane_rows < HEAD
    left_causal = position(iota((half, half), 0)) <= position(iota((half, half), 1))
    right_causal = position(iota((ROWS, half), 0)) <= position(iota((ROWS, half), 1) + half)
    slot = iota((ROWS // 8, LOCAL), 1) >> 4
    hidden = jnp.zeros((half, half), BF16)
    pending = None
    for start in range(0, HEADS, 3):
        group = range(start, start + 3)
        blocks, keys, queries, cots = {}, {}, {}, {}
        for h in group:
            block = in_ref[h].astype(F32)
            empty = block[:, :1] > 32768.0
            block = jnp.where(empty & first, 0.0, block)
            query = jnp.where(head_lanes, block * 0.125, jnp.where(bias_lane, 1.0, 0.0))
            queries[h] = query.astype(BF16)
            keys[h] = jnp.where(
                head_lanes, block, jnp.where(bias_lane & empty, -1e30, 0.0)
            ).astype(BF16)
            blocks[h] = block.astype(BF16)
            pair = in_ref[HEADS + h // 2]
            cots[h] = pair[:, :HEAD] if h % 2 == 0 else pair[:, HEAD:]
        tiles = (
            (slice(0, half), slice(0, half), left_causal),
            (slice(0, ROWS), slice(half, ROWS), right_causal),
        )
        scores, d_probs = {}, {}
        for h in group:
            scores[h] = dot(keys[h], queries[h], ((1,), (1,)))
            d_probs[h] = dot(blocks[h][:, HEAD:], cots[h], ((1,), (1,)))
        probs, d_scores = {}, {}
        for h in group:
            parts = []
            for rows, cols, causal in tiles:
                tile = jnp.where(causal, scores[h][rows, cols], -1e30)
                weights = jnp.exp(tile - jnp.max(tile, axis=0, keepdims=True))
                scale = 1.0 / jnp.sum(weights, axis=0, keepdims=True)
                parts.append((weights * scale).astype(BF16))
            lower = [
                (parts[n].astype(F32), d_probs[h][rows, cols])
                for n, (rows, cols, causal) in enumerate(tiles)
            ]
            slopes = [
                (wide * (d_prob - jnp.sum(wide * d_prob, axis=0, keepdims=True))).astype(BF16)
                for wide, d_prob in lower
            ]
            for held, done in ((probs, parts), (d_scores, slopes)):
                left = jnp.concatenate([done[0], hidden], axis=0)
                held[h] = jnp.concatenate([left, done[1]], axis=1)
        for h in group:
            turned = blocks[h].T
            above = dot(turned[:HEAD], d_scores[h])
            above = above + dot(turned[:HEAD], d_scores[h], ((1,), (1,)))
            out = dot(turned[HEAD:], probs[h])
            d_value = dot(cots[h].T, probs[h], ((1,), (1,)))
            grads = jnp.concatenate([above * 0.125, d_value], axis=0).T
            for m, part in enumerate(spread(grads, slot)):
                n = h * 8 + m
                part = part.astype(BF16).reshape(16, 2, LOCAL)
                out_ref[n // 6 * 16 : (n // 6 + 1) * 16, n % 6] = part
            if h % 2 == 0:
                pending = out
            else:
                k = HEADS + h // 2
                joined = jnp.concatenate([pending, out], axis=0).T.astype(BF16)
                out_ref[:, k] = joined.reshape(LOCAL, 2, LOCAL)


def index_of(place_ref, dy, dc):
    return lax.rem(place_ref[0] + dy, 4) * 2 + lax.rem(place_ref[1] + dc, 2)


def partial_kernel(place_ref, in_ref, *refs):
    exts, (out_ref, keep_ref, give_ref), (dests, cols, scratch) = refs[:4], refs[4:7], refs[7:]
    here = place_ref[1]
    j = place_ref[0] * 2 + here
    head = (j * 3 // 4, (j * 6 + 5) // 8)
    lane_slot = iota((ROWS, LOCAL), 1) >> 4
    sub_rows = iota((ROWS, LOCAL), 0).astype(F32)
    for n, (dy, dc) in enumerate(STEPS):
        source = index_of(place_ref, 4 - dy, dc)
        for i in range(2):
            lanes = pl.ds(pl.multiple_of(head[i] * LOCAL, LOCAL), LOCAL)
            dests[i, source] = exts[n // 2][n % 2, LOCAL:, lanes].astype(F32)[:8]
    turned = [in_ref[:, b].reshape(ROWS, LOCAL) for b in range(6)]
    turned = [pltpu.roll(rows.astype(F32), BLOCK * b, 1).astype(BF16) if b else rows for b, rows in enumerate(turned)]
    limit = lax.rem(j, 4)
    limit = jnp.where(limit == 1, 2, jnp.where(limit == 2, 4, 6))
    for p in range(8):
        rows = turned[0]
        for b in range(1, 6):
            rows = jnp.where(lane_slot == (b + p) % 8, turned[b], rows)
        routes = [(sub_rows == dests[i, p, :1]).astype(BF16) for i in range(2)]
        found = dot(rows, jnp.concatenate(routes, axis=1), ((0,), (0,)))
        blocks = []
        for b in range(6):
            cut = slice((b + p) % 8 * BLOCK, ((b + p) % 8 + 1) * BLOCK)
            blocks.append(jnp.where(b < limit, found[cut, :LOCAL], found[cut, LOCAL:]))
        cols[p] = jnp.concatenate(blocks, axis=0).astype(BF16)
    total = None
    for dy in range(4):
        near = [cols[index_of(place_ref, 4 - dy, dc)] for dc in range(2)]
        rows = exts[dy][:, :LOCAL, :].reshape(2 * LOCAL, WIDTH)
        term = dot(jnp.concatenate(near, axis=1), rows)
        total = term if total is None else total + term
    for k in range(WIDTH // LOCAL):
        scratch[k * COLUMNS : (k + 1) * COLUMNS, :] = total[:, k * LOCAL : (k + 1) * LOCAL]
    scratch[16 * PIECE :, :] = jnp.zeros((8, LOCAL), F32)
    for i in range(16):
        out_ref[i] = scratch[i * PIECE : i * PIECE + SLOT, :].astype(BF16)
    for dy in range(4):
        keep_ref[dy] = cols[index_of(place_ref, dy, 0)]
        give_ref[dy] = cols[index_of(place_ref, dy, 1)]


def output_kernel(in_ref, ext_ref, att_ref):
    sub_rows = iota((ROWS, LOCAL), 0).astype(F32)
    head_lanes = iota((LOCAL, LOCAL), 1) < HEAD
    dests = ext_ref[0, LOCAL:, :].astype(F32)[:1]
    for k in range(HEADS // 2):
        rows = in_ref[:, HEADS + k].reshape(ROWS, LOCAL)
        found = []
        for h in (2 * k, 2 * k + 1):
            route = (sub_rows == dests[:, h * LOCAL : (h + 1) * LOCAL]).astype(BF16)
            found.append(dot(route, rows, ((0,), (0,))))
        both = jnp.where(head_lanes, found[0], found[1])
        att_ref[:, k * LOCAL : (k + 1) * LOCAL] = both.astype(BF16)


def message_kernel(keep_ref, got_ref, *outs):
    for dy, out_ref in enumerate(outs):
        out_ref[0] = keep_ref[dy]
        out_ref[1] = got_ref[dy]


def repeat_kernel(in_ref, out_ref, scratch):
    for i in range(4):
        scratch[i * PIECE : (i + 1) * PIECE, :] = in_ref[i].astype(F32)[:PIECE]
    block = scratch[...].astype(BF16)
    for i in range(16):
        out_ref[i] = block


def return_kernel(place_ref, *refs):
    parts, (ws_ref, wv_ref, grad_ref, held) = refs[:4], refs[4:]
    for dy in range(4):
        for dc in range(2):
            held[index_of(place_ref, 4 - dy, dc)] = parts[dy][dc]

    def columns(first):
        rows = [
            held[n // 6, n % 6 * BLOCK : (n % 6 + 1) * BLOCK, :]
            for h in range(HEADS)
            for n in range(h * 8 + first, h * 8 + first + 4)
        ]
        return jnp.concatenate(rows, axis=0).astype(F32).T.astype(BF16)

    left = columns(0)
    right = columns(4)
    total = dot(left, ws_ref[...], ((1,), (1,))) + dot(right, wv_ref[...], ((1,), (1,)))
    grad_ref[...] = total.astype(BF16)


def sum_kernel(in_ref, out_ref):
    total = in_ref[0].astype(F32)
    for i in range(1, in_ref.shape[0]):
        total = total + in_ref[i].astype(F32)
    total = total.astype(BF16)
    for i in range(out_ref.shape[0]):
        out_ref[i] = total


def finish_kernel(place_ref, mine_ref, other_ref, shared_ref, value_ref, held, sems):
    first = place_ref[1] == 0
    copies = []
    for k in range(WIDTH // LOCAL):
        rows = slice(k * COLUMNS, (k + 1) * COLUMNS)
        strip = []
        for y in range(4):
            mine = mine_ref[y, rows, :]
            other = other_ref[y, rows, :]
            strip += [jnp.where(first, mine, other), jnp.where(first, other, mine)]
        strip = jnp.concatenate(strip, axis=0)
        lines = slice(k * LOCAL, (k + 1) * LOCAL)
        for half, ref in enumerate((shared_ref, value_ref)):
            heads = [
                strip[h * LOCAL + half * HEAD : h * LOCAL + (half + 1) * HEAD]
                for h in range(HEADS)
            ]
            held[half, lines, :] = jnp.concatenate(heads, axis=0).T
            copies.append(
                pltpu.make_async_copy(held.at[half, lines], ref.at[lines], sems.at[half, k])
            )
            copies[-1].start()
    for copy in copies:
        copy.wait()


def call(kernel, out, *args, scratch=(), scalars=0, held=False, far=()):
    if held:
        args = [pltpu.with_memory_space_constraint(arg, pltpu.HBM) for arg in args]
    specs = [pl.BlockSpec(memory_space=pltpu.SMEM)] * scalars
    specs += [pl.BlockSpec(memory_space=pl.ANY if held else pltpu.VMEM)] * (len(args) - scalars)
    outs = [
        pl.BlockSpec(memory_space=pl.ANY if n in far else pltpu.VMEM) for n in range(len(out))
    ]
    return pl.pallas_call(
        kernel,
        out_shape=out,
        in_specs=specs,
        out_specs=outs,
        scratch_shapes=scratch,
        compiler_params=pltpu.CompilerParams(vmem_limit_bytes=48 * 1024 * 1024),
    )(*args)


def shape(*dims):
    return jax.ShapeDtypeStruct(dims, BF16)


def swap(rows, axes, groups=None):
    return lax.all_to_all(
        rows, axes, split_axis=0, concat_axis=0, tiled=True, axis_index_groups=groups
    )


def body(tokens, w_shared, w_value, cluster_ids, slot_index, cotangent):
    rows = tokens[0]
    place = jnp.stack([lax.axis_index("y"), lax.axis_index("c")]).astype(jnp.int32)
    sent, ext = call(
        send_kernel,
        (shape(LOCAL, 9, 2, LOCAL), shape(LOCAL + 16, WIDTH)),
        cluster_ids.transpose(1, 0, 2),
        rows,
        w_shared,
        w_value,
        cotangent[0],
        scratch=[
            pltpu.VMEM((HEADS, 1, LOCAL), jnp.int32),
            pltpu.VMEM((LOCAL, WIDTH), BF16),
            pltpu.VMEM((WIDTH, PROJ), BF16),
            pltpu.VMEM((WIDTH, PROJ), BF16),
            pltpu.VMEM((LOCAL, PROJ), BF16),
            pltpu.SemaphoreType.DMA((5,)),
        ],
        held=True,
    )

    def shift(pair, dy):
        return lax.ppermute(pair, "y", [(y, (y + dy) % 4) for y in range(4)])

    def flip(part):
        return lax.ppermute(part, "c", [(0, 1), (1, 0)])

    arrived = swap(sent, OWNERS)
    pair = jnp.stack([ext, flip(ext)])
    near = (shift(pair, 1), shift(pair, 3))
    arrived, pair, near, place = lax.optimization_barrier((arrived, pair, near, place))
    exts = [pair, near[0], shift(pair, 2), near[1]]
    arrived = arrived.transpose(1, 0, 2, 3).reshape(9, ROWS, LOCAL)
    (worked,) = call(
        attend_kernel,
        [shape(LOCAL, 9, 2, LOCAL)],
        arrived,
    )
    back = swap(worked, OWNERS)
    part, keep, give = call(
        partial_kernel,
        [shape(16, SLOT, LOCAL), shape(4, COLUMNS, LOCAL), shape(4, COLUMNS, LOCAL)],
        place,
        back,
        *exts,
        scratch=[
            pltpu.VMEM((2, 8, 8, LOCAL), F32),
            pltpu.VMEM((8, COLUMNS, LOCAL), BF16),
            pltpu.VMEM((16 * PIECE + 8, LOCAL), F32),
        ],
        scalars=1,
    )
    (attention,) = call(output_kernel, [shape(LOCAL, PROJ)], back, pair)
    part = swap(part, ("x", "z"), NEAR)
    part, keep, got, attention = lax.optimization_barrier((part, keep, flip(give), attention))
    parts = call(message_kernel, [shape(2, COLUMNS, LOCAL)] * 4, keep, got)
    (part,) = call(sum_kernel, [shape(4, SLOT, LOCAL)], part)
    part, parts = lax.optimization_barrier((part, parts))
    moved = [shift(parts[dy], dy) for dy in range(1, 4)]
    part, moved = lax.optimization_barrier((swap(part, "z", FAR), moved))
    (block,) = call(sum_kernel, [shape(4, SLOT, LOCAL)], part)
    (block,) = call(
        repeat_kernel,
        [shape(16, 4 * PIECE, LOCAL)],
        swap(block, "z", QUARTER),
        scratch=[pltpu.VMEM((4 * PIECE, LOCAL), F32)],
    )
    (grad_tokens,) = call(
        return_kernel,
        [shape(LOCAL, WIDTH)],
        place,
        parts[0],
        *moved,
        w_shared,
        w_value,
        scratch=[pltpu.VMEM((8, COLUMNS, LOCAL), BF16)],
        scalars=1,
    )
    block = swap(block, ("y", "x"))
    block, grad_tokens = lax.optimization_barrier((block, grad_tokens))
    block = block.reshape(4, WHOLE, LOCAL)
    other = flip(block)
    grad_shared, grad_value = call(
        finish_kernel,
        (shape(WIDTH, PROJ), shape(WIDTH, PROJ)),
        place,
        block,
        other,
        scratch=[
            pltpu.VMEM((2, WIDTH, PROJ), BF16),
            pltpu.SemaphoreType.DMA((2, WIDTH // LOCAL)),
        ],
        scalars=1,
        far=(0, 1),
    )
    return (attention[None], grad_tokens[None], grad_shared, grad_value)


def solution(mesh):
    fine = Mesh(mesh.devices.reshape(4, 4, 16, 2), ("x", "y", "z", "c"))
    in_specs = (
        P("x", TOK, None),
        P(),
        P(),
        P("x", None, TOK),
        P("x", None, TOK),
        P("x", TOK, None),
    )
    out_specs = (P("x", TOK, None), P("x", TOK, None), P(), P())
    return jax.shard_map(body, mesh=fine, in_specs=in_specs, out_specs=out_specs, check_vma=False)
```

```python
import jax
import jax.numpy as jnp
from jax import lax
from jax.experimental import pallas as pl
from jax.experimental.pallas import tpu as pltpu
from jax.sharding import Mesh
from jax.sharding import PartitionSpec as P

F32 = jnp.float32
BF16 = jnp.bfloat16
HEADS = 6
HEAD = 64
ROWS = 256
LOCAL = 128
WIDTH = 768
PROJ = 384
UNUSED = 65536.0
PLANE = ("y", "c")
TOK = ("y", "z", "c")
OWNERS = ("y", "c", "z")
RING = [(3, 4, 9, 14), (2, 7, 8, 13), (1, 6, 11, 12), (0, 5, 10, 15)]
FAR = [list(group) for group in RING]
NEAR = [[x * 16 + RING[n][b] for x in range(4) for n in range(4)] for b in range(4)]
STEPS = [(dy, dc) for dy in range(4) for dc in range(2)]
COLUMNS = 96
PIECE = 36
SLOT = 40
BLOCK = 16
WHOLE = 576
MESSAGE = 96


def iota(shape, dim):
    return lax.broadcasted_iota(jnp.int32, shape, dim)


def dot(a, b, dims=((1,), (0,))):
    return lax.dot_general(a, b, (dims, ((), ())), preferred_element_type=F32)


def send_kernel(*refs):
    sources, (out_ref, ext_ref), targets, sems = refs[:5], refs[5:7], refs[7:12], refs[12]
    copies = [
        pltpu.make_async_copy(source, target, sems.at[n])
        for n, (source, target) in enumerate(zip(sources, targets))
    ]
    for copy in copies:
        copy.start()
    cluster_ref, tok_ref, ws_ref, wv_ref, cot_ref = targets
    sub = iota((LOCAL, LOCAL), 0)
    lane = iota((LOCAL, LOCAL), 1)
    sub_rows = iota((ROWS, LOCAL), 0)
    lane_rows = iota((ROWS, LOCAL), 1)
    copies[0].wait()
    hits = []
    marks = []
    for h in range(HEADS):
        cluster = cluster_ref[h]
        member = (sub == cluster).astype(BF16)
        same = dot(member, member, ((0,), (0,)))
        order = jnp.sum(jnp.where(sub < lane, same, 0.0), axis=0, keepdims=True)
        owner = (cluster & 96) + (cluster & 1) * 16 + ((cluster >> 1) & 15)
        dest = owner * 2 + order.astype(jnp.int32)
        ext_ref[LOCAL:, h * LOCAL : (h + 1) * LOCAL] = jnp.broadcast_to(
            dest.astype(F32), (16, LOCAL)
        ).astype(BF16)
        hit = sub_rows == dest
        used = jnp.sum(jnp.where(hit, 1.0, 0.0), axis=1, keepdims=True)
        hits.append(hit.astype(BF16))
        marks.append(jnp.where((lane_rows == 0) & (used < 0.5), UNUSED, 0.0))
    for copy in copies[1:]:
        copy.wait()
    tokens = tok_ref[...]
    ext_ref[:LOCAL, :] = tokens
    shared = dot(tokens, ws_ref[...]).astype(BF16)
    value = dot(tokens, wv_ref[...]).astype(BF16)
    cot = cot_ref[...]
    blank = jnp.zeros((LOCAL, HEAD), BF16)
    pending = None
    for h in range(HEADS):
        cols = slice(h * HEAD, (h + 1) * HEAD)
        tail = [cot[:, cols], blank] if h % 2 == 0 else [blank, cot[:, cols]]
        packed = jnp.concatenate([shared[:, cols], value[:, cols]] + tail, axis=1)
        moved = dot(hits[h], packed)
        out_ref[:, h] = (moved[:, :LOCAL] + marks[h]).astype(BF16).reshape(LOCAL, 2, LOCAL)
        if h % 2 == 0:
            pending = moved[:, LOCAL:]
        else:
            packed = (pending + moved[:, LOCAL:]).astype(BF16)
            out_ref[:, HEADS + h // 2] = packed.reshape(LOCAL, 2, LOCAL)


def position(row):
    return (row & 192) + ((row >> 1) & 15) * 4 + ((row >> 5) & 1) * 2 + (row & 1)


def spread(block, slot):
    rows = block.shape[0] // 8
    parts = [block[p * rows : (p + 1) * rows] for p in range(8)]
    for bit in (1, 2, 4):
        odd = (slot & bit) != 0
        after = list(parts)
        for p in range(8):
            if p & bit == 0:
                low, high = parts[p], parts[p + bit]
                after[p] = jnp.where(odd, pltpu.roll(high, BLOCK * bit, 1), low)
                after[p + bit] = jnp.where(odd, high, pltpu.roll(low, LOCAL - BLOCK * bit, 1))
        parts = after
    return parts


def attend_kernel(in_ref, out_ref):
    half = ROWS // 2
    lane_rows = iota((ROWS, LOCAL), 1)
    first = lane_rows == 0
    bias_lane = lane_rows == HEAD
    head_lanes = lane_rows < HEAD
    left_causal = position(iota((half, half), 0)) <= position(iota((half, half), 1))
    right_causal = position(iota((ROWS, half), 0)) <= position(iota((ROWS, half), 1) + half)
    slot = iota((ROWS // 8, LOCAL), 1) >> 4
    hidden = jnp.zeros((half, half), BF16)
    pending = None
    for start in range(0, HEADS, 3):
        group = range(start, start + 3)
        blocks, keys, queries, cots = {}, {}, {}, {}
        for h in group:
            block = in_ref[h].astype(F32)
            empty = block[:, :1] > 32768.0
            block = jnp.where(empty & first, 0.0, block)
            query = jnp.where(head_lanes, block * 0.125, jnp.where(bias_lane, 1.0, 0.0))
            queries[h] = query.astype(BF16)
            keys[h] = jnp.where(
                head_lanes, block, jnp.where(bias_lane & empty, -1e30, 0.0)
            ).astype(BF16)
            blocks[h] = block.astype(BF16)
            pair = in_ref[HEADS + h // 2]
            cots[h] = pair[:, :HEAD] if h % 2 == 0 else pair[:, HEAD:]
        tiles = (
            (slice(0, half), slice(0, half), left_causal),
            (slice(0, ROWS), slice(half, ROWS), right_causal),
        )
        scores, d_probs = {}, {}
        for h in group:
            scores[h] = dot(keys[h], queries[h], ((1,), (1,)))
            d_probs[h] = dot(blocks[h][:, HEAD:], cots[h], ((1,), (1,)))
        probs, d_scores = {}, {}
        for h in group:
            parts = []
            for rows, cols, causal in tiles:
                tile = jnp.where(causal, scores[h][rows, cols], -1e30)
                weights = jnp.exp(tile - jnp.max(tile, axis=0, keepdims=True))
                scale = 1.0 / jnp.sum(weights, axis=0, keepdims=True)
                parts.append((weights * scale).astype(BF16))
            lower = [
                (parts[n].astype(F32), d_probs[h][rows, cols])
                for n, (rows, cols, causal) in enumerate(tiles)
            ]
            slopes = [
                (wide * (d_prob - jnp.sum(wide * d_prob, axis=0, keepdims=True))).astype(BF16)
                for wide, d_prob in lower
            ]
            for held, done in ((probs, parts), (d_scores, slopes)):
                left = jnp.concatenate([done[0], hidden], axis=0)
                held[h] = jnp.concatenate([left, done[1]], axis=1)
        for h in group:
            turned = blocks[h].T
            above = dot(turned[:HEAD], d_scores[h])
            above = above + dot(turned[:HEAD], d_scores[h], ((1,), (1,)))
            out = dot(turned[HEAD:], probs[h])
            d_value = dot(cots[h].T, probs[h], ((1,), (1,)))
            grads = jnp.concatenate([above * 0.125, d_value], axis=0).T
            for m, part in enumerate(spread(grads, slot)):
                n = h * 8 + m
                part = part.astype(BF16).reshape(16, 2, LOCAL)
                out_ref[n // 6 * 16 : (n // 6 + 1) * 16, n % 6] = part
            if h % 2 == 0:
                pending = out
            else:
                k = HEADS + h // 2
                joined = jnp.concatenate([pending, out], axis=0).T.astype(BF16)
                out_ref[:, k] = joined.reshape(LOCAL, 2, LOCAL)


def index_of(place_ref, dy, dc):
    return lax.rem(place_ref[0] + dy, 4) * 2 + lax.rem(place_ref[1] + dc, 2)


def partial_kernel(place_ref, in_ref, *refs):
    exts, (out_ref, keep_ref, give_ref), (dests, cols, scratch) = refs[:4], refs[4:7], refs[7:]
    here = place_ref[1]
    j = place_ref[0] * 2 + here
    head = (j * 3 // 4, (j * 6 + 5) // 8)
    lane_slot = iota((ROWS, LOCAL), 1) >> 4
    sub_rows = iota((ROWS, LOCAL), 0).astype(F32)
    for n, (dy, dc) in enumerate(STEPS):
        source = index_of(place_ref, 4 - dy, dc)
        for i in range(2):
            lanes = pl.ds(pl.multiple_of(head[i] * LOCAL, LOCAL), LOCAL)
            dests[i, source] = exts[n // 2][n % 2, LOCAL:, lanes].astype(F32)[:8]
    turned = [in_ref[:, b].reshape(ROWS, LOCAL) for b in range(6)]
    turned = [pltpu.roll(rows.astype(F32), BLOCK * b, 1).astype(BF16) if b else rows for b, rows in enumerate(turned)]
    limit = lax.rem(j, 4)
    limit = jnp.where(limit == 1, 2, jnp.where(limit == 2, 4, 6))
    for p in range(8):
        rows = turned[0]
        for b in range(1, 6):
            rows = jnp.where(lane_slot == (b + p) % 8, turned[b], rows)
        routes = [(sub_rows == dests[i, p, :1]).astype(BF16) for i in range(2)]
        found = dot(rows, jnp.concatenate(routes, axis=1), ((0,), (0,)))
        blocks = []
        for b in range(6):
            cut = slice((b + p) % 8 * BLOCK, ((b + p) % 8 + 1) * BLOCK)
            blocks.append(jnp.where(b < limit, found[cut, :LOCAL], found[cut, LOCAL:]))
        cols[p] = jnp.concatenate(blocks, axis=0).astype(BF16)
    total = None
    for dy in range(4):
        near = [cols[index_of(place_ref, 4 - dy, dc)] for dc in range(2)]
        rows = exts[dy][:, :LOCAL, :].reshape(2 * LOCAL, WIDTH)
        term = dot(jnp.concatenate(near, axis=1), rows)
        total = term if total is None else total + term
    for k in range(WIDTH // LOCAL):
        scratch[k * COLUMNS : (k + 1) * COLUMNS, :] = total[:, k * LOCAL : (k + 1) * LOCAL]
    scratch[16 * PIECE :, :] = jnp.zeros((8, LOCAL), F32)
    for i in range(16):
        out_ref[i] = scratch[i * PIECE : i * PIECE + SLOT, :].astype(BF16)
    for y in range(4):
        keep_ref[y] = cols[y * 2 + here]
        give_ref[y] = cols[y * 2 + 1 - here]


def output_kernel(in_ref, ext_ref, att_ref):
    sub_rows = iota((ROWS, LOCAL), 0).astype(F32)
    head_lanes = iota((LOCAL, LOCAL), 1) < HEAD
    dests = ext_ref[0, LOCAL:, :].astype(F32)[:1]
    for k in range(HEADS // 2):
        rows = in_ref[:, HEADS + k].reshape(ROWS, LOCAL)
        found = []
        for h in (2 * k, 2 * k + 1):
            route = (sub_rows == dests[:, h * LOCAL : (h + 1) * LOCAL]).astype(BF16)
            found.append(dot(route, rows, ((0,), (0,))))
        both = jnp.where(head_lanes, found[0], found[1])
        att_ref[:, k * LOCAL : (k + 1) * LOCAL] = both.astype(BF16)


def pack_kernel(block_ref, keep_ref, got_ref, out_ref, scratch):
    for i in range(16):
        scratch[i * PIECE : (i + 1) * PIECE, :] = block_ref[i].astype(F32)[:PIECE]
    block = scratch[...].astype(BF16)
    for y in range(4):
        out_ref[y, :WHOLE, :] = block
        out_ref[y, WHOLE : WHOLE + MESSAGE, :] = keep_ref[y]
        out_ref[y, WHOLE + MESSAGE :, :] = got_ref[y]


def return_kernel(place_ref, all_ref, ws_ref, wv_ref, grad_ref, held):
    here = place_ref[1]
    for y in range(4):
        held[y * 2 + here] = all_ref[y, WHOLE : WHOLE + MESSAGE, :]
        held[y * 2 + 1 - here] = all_ref[y, WHOLE + MESSAGE :, :]

    def columns(first):
        rows = [
            held[n // 6, n % 6 * BLOCK : (n % 6 + 1) * BLOCK, :]
            for h in range(HEADS)
            for n in range(h * 8 + first, h * 8 + first + 4)
        ]
        return jnp.concatenate(rows, axis=0).astype(F32).T.astype(BF16)

    left = columns(0)
    right = columns(4)
    total = dot(left, ws_ref[...], ((1,), (1,))) + dot(right, wv_ref[...], ((1,), (1,)))
    grad_ref[...] = total.astype(BF16)


def sum_kernel(in_ref, out_ref):
    total = in_ref[0].astype(F32)
    for i in range(1, in_ref.shape[0]):
        total = total + in_ref[i].astype(F32)
    total = total.astype(BF16)
    for i in range(out_ref.shape[0]):
        out_ref[i] = total


def finish_kernel(place_ref, mine_ref, other_ref, shared_ref, value_ref, held, sems):
    first = place_ref[1] == 0
    copies = []
    for k in range(WIDTH // LOCAL):
        rows = slice(k * COLUMNS, (k + 1) * COLUMNS)
        strip = []
        for y in range(4):
            mine = mine_ref[y, rows, :]
            other = other_ref[y, rows, :]
            strip += [jnp.where(first, mine, other), jnp.where(first, other, mine)]
        strip = jnp.concatenate(strip, axis=0)
        lines = slice(k * LOCAL, (k + 1) * LOCAL)
        for half, ref in enumerate((shared_ref, value_ref)):
            heads = [
                strip[h * LOCAL + half * HEAD : h * LOCAL + (half + 1) * HEAD]
                for h in range(HEADS)
            ]
            held[half, lines, :] = jnp.concatenate(heads, axis=0).T
            copies.append(
                pltpu.make_async_copy(held.at[half, lines], ref.at[lines], sems.at[half, k])
            )
            copies[-1].start()
    for copy in copies:
        copy.wait()


def call(kernel, out, *args, scratch=(), scalars=0, held=False, far=()):
    if held:
        args = [pltpu.with_memory_space_constraint(arg, pltpu.HBM) for arg in args]
    specs = [pl.BlockSpec(memory_space=pltpu.SMEM)] * scalars
    specs += [pl.BlockSpec(memory_space=pl.ANY if held else pltpu.VMEM)] * (len(args) - scalars)
    outs = [
        pl.BlockSpec(memory_space=pl.ANY if n in far else pltpu.VMEM) for n in range(len(out))
    ]
    return pl.pallas_call(
        kernel,
        out_shape=out,
        in_specs=specs,
        out_specs=outs,
        scratch_shapes=scratch,
        compiler_params=pltpu.CompilerParams(vmem_limit_bytes=48 * 1024 * 1024),
    )(*args)


def shape(*dims):
    return jax.ShapeDtypeStruct(dims, BF16)


def swap(rows, axes, groups=None):
    return lax.all_to_all(
        rows, axes, split_axis=0, concat_axis=0, tiled=True, axis_index_groups=groups
    )


def body(tokens, w_shared, w_value, cluster_ids, slot_index, cotangent):
    rows = tokens[0]
    place = jnp.stack([lax.axis_index("y"), lax.axis_index("c")]).astype(jnp.int32)
    sent, ext = call(
        send_kernel,
        (shape(LOCAL, 9, 2, LOCAL), shape(LOCAL + 16, WIDTH)),
        cluster_ids.transpose(1, 0, 2),
        rows,
        w_shared,
        w_value,
        cotangent[0],
        scratch=[
            pltpu.VMEM((HEADS, 1, LOCAL), jnp.int32),
            pltpu.VMEM((LOCAL, WIDTH), BF16),
            pltpu.VMEM((WIDTH, PROJ), BF16),
            pltpu.VMEM((WIDTH, PROJ), BF16),
            pltpu.VMEM((LOCAL, PROJ), BF16),
            pltpu.SemaphoreType.DMA((5,)),
        ],
        held=True,
    )

    def shift(pair, dy):
        return lax.ppermute(pair, "y", [(y, (y + dy) % 4) for y in range(4)])

    def flip(part):
        return lax.ppermute(part, "c", [(0, 1), (1, 0)])

    arrived = swap(sent, OWNERS)
    pair = jnp.stack([ext, flip(ext)])
    exts = [pair, shift(pair, 1), shift(pair, 2), shift(pair, 3)]
    arrived = arrived.transpose(1, 0, 2, 3).reshape(9, ROWS, LOCAL)
    (worked,) = call(
        attend_kernel,
        [shape(LOCAL, 9, 2, LOCAL)],
        arrived,
    )
    worked, exts, place = lax.optimization_barrier((worked, exts, place))
    back = swap(worked, OWNERS)
    part, keep, give = call(
        partial_kernel,
        [shape(16, SLOT, LOCAL), shape(4, MESSAGE, LOCAL), shape(4, MESSAGE, LOCAL)],
        place,
        back,
        *exts,
        scratch=[
            pltpu.VMEM((2, 8, 8, LOCAL), F32),
            pltpu.VMEM((8, COLUMNS, LOCAL), BF16),
            pltpu.VMEM((16 * PIECE + 8, LOCAL), F32),
        ],
        scalars=1,
    )
    (attention,) = call(output_kernel, [shape(LOCAL, PROJ)], back, pair)
    part = swap(part, ("x", "z"), NEAR)
    part, keep, got, attention = lax.optimization_barrier((part, keep, flip(give), attention))
    (part,) = call(sum_kernel, [shape(4, SLOT, LOCAL)], part)
    (block,) = call(sum_kernel, [shape(16, SLOT, LOCAL)], swap(part, "z", FAR))
    (block,) = call(
        pack_kernel,
        [shape(4, WHOLE + 2 * MESSAGE, LOCAL)],
        swap(block, ("x", "z"), NEAR),
        keep,
        got,
        scratch=[pltpu.VMEM((WHOLE, LOCAL), F32)],
    )
    block = swap(block, "y")
    other = flip(block)
    (grad_tokens,) = call(
        return_kernel,
        [shape(LOCAL, WIDTH)],
        place,
        block,
        w_shared,
        w_value,
        scratch=[pltpu.VMEM((8, MESSAGE, LOCAL), BF16)],
        scalars=1,
    )
    grad_shared, grad_value = call(
        finish_kernel,
        (shape(WIDTH, PROJ), shape(WIDTH, PROJ)),
        place,
        block,
        other,
        scratch=[
            pltpu.VMEM((2, WIDTH, PROJ), BF16),
            pltpu.SemaphoreType.DMA((2, WIDTH // LOCAL)),
        ],
        scalars=1,
        far=(0, 1),
    )
    return (attention[None], grad_tokens[None], grad_shared, grad_value)


def solution(mesh):
    fine = Mesh(mesh.devices.reshape(4, 4, 16, 2), ("x", "y", "z", "c"))
    in_specs = (
        P("x", TOK, None),
        P(),
        P(),
        P("x", None, TOK),
        P("x", None, TOK),
        P("x", TOK, None),
    )
    out_specs = (P("x", TOK, None), P("x", TOK, None), P(), P())
    return jax.shard_map(body, mesh=fine, in_specs=in_specs, out_specs=out_specs, check_vma=False)
```

```python
import jax
import jax.numpy as jnp
from jax import lax
from jax.experimental import pallas as pl
from jax.experimental.pallas import tpu as pltpu
from jax.sharding import Mesh
from jax.sharding import PartitionSpec as P

F32 = jnp.float32
BF16 = jnp.bfloat16
HEADS = 6
HEAD = 64
ROWS = 256
LOCAL = 128
WIDTH = 768
PROJ = 384
UNUSED = 65536.0
PLANE = ("y", "c")
TOK = ("y", "z", "c")
OWNERS = ("y", "c", "z")
RING = [(3, 4, 9, 14), (2, 7, 8, 13), (1, 6, 11, 12), (0, 5, 10, 15)]
FAR = [list(group) for group in RING]
NEAR = [[x * 16 + RING[n][b] for x in range(4) for n in range(4)] for b in range(4)]
STEPS = [(dy, dc) for dy in range(4) for dc in range(2)]
COLUMNS = 96
PIECE = 36
SLOT = 40
BLOCK = 16
WHOLE = 576
MESSAGE = 96


def iota(shape, dim):
    return lax.broadcasted_iota(jnp.int32, shape, dim)


def dot(a, b, dims=((1,), (0,))):
    return lax.dot_general(a, b, (dims, ((), ())), preferred_element_type=F32)


def send_kernel(*refs):
    sources, (out_ref, ext_ref), targets, sems = refs[:5], refs[5:7], refs[7:12], refs[12]
    copies = [
        pltpu.make_async_copy(source, target, sems.at[n])
        for n, (source, target) in enumerate(zip(sources, targets))
    ]
    for copy in copies:
        copy.start()
    cluster_ref, tok_ref, ws_ref, wv_ref, cot_ref = targets
    sub = iota((LOCAL, LOCAL), 0)
    lane = iota((LOCAL, LOCAL), 1)
    sub_rows = iota((ROWS, LOCAL), 0)
    lane_rows = iota((ROWS, LOCAL), 1)
    copies[0].wait()
    hits = []
    marks = []
    for h in range(HEADS):
        cluster = cluster_ref[h]
        member = (sub == cluster).astype(BF16)
        same = dot(member, member, ((0,), (0,)))
        order = jnp.sum(jnp.where(sub < lane, same, 0.0), axis=0, keepdims=True)
        owner = (cluster & 96) + (cluster & 1) * 16 + ((cluster >> 1) & 15)
        dest = owner * 2 + order.astype(jnp.int32)
        ext_ref[LOCAL:, h * LOCAL : (h + 1) * LOCAL] = jnp.broadcast_to(
            dest.astype(F32), (16, LOCAL)
        ).astype(BF16)
        hit = sub_rows == dest
        used = jnp.sum(jnp.where(hit, 1.0, 0.0), axis=1, keepdims=True)
        hits.append(hit.astype(BF16))
        marks.append(jnp.where((lane_rows == 0) & (used < 0.5), UNUSED, 0.0))
    for copy in copies[1:]:
        copy.wait()
    tokens = tok_ref[...]
    ext_ref[:LOCAL, :] = tokens
    shared = dot(tokens, ws_ref[...]).astype(BF16)
    value = dot(tokens, wv_ref[...]).astype(BF16)
    cot = cot_ref[...]
    blank = jnp.zeros((LOCAL, HEAD), BF16)
    pending = None
    for h in range(HEADS):
        cols = slice(h * HEAD, (h + 1) * HEAD)
        tail = [cot[:, cols], blank] if h % 2 == 0 else [blank, cot[:, cols]]
        packed = jnp.concatenate([shared[:, cols], value[:, cols]] + tail, axis=1)
        moved = dot(hits[h], packed)
        out_ref[:, h] = (moved[:, :LOCAL] + marks[h]).astype(BF16).reshape(LOCAL, 2, LOCAL)
        if h % 2 == 0:
            pending = moved[:, LOCAL:]
        else:
            packed = (pending + moved[:, LOCAL:]).astype(BF16)
            out_ref[:, HEADS + h // 2] = packed.reshape(LOCAL, 2, LOCAL)


def position(row):
    return (row & 192) + ((row >> 1) & 15) * 4 + ((row >> 5) & 1) * 2 + (row & 1)


def spread(block, slot):
    rows = block.shape[0] // 8
    parts = [block[p * rows : (p + 1) * rows] for p in range(8)]
    for bit in (1, 2, 4):
        odd = (slot & bit) != 0
        after = list(parts)
        for p in range(8):
            if p & bit == 0:
                low, high = parts[p], parts[p + bit]
                after[p] = jnp.where(odd, pltpu.roll(high, BLOCK * bit, 1), low)
                after[p + bit] = jnp.where(odd, high, pltpu.roll(low, LOCAL - BLOCK * bit, 1))
        parts = after
    return parts


def attend_kernel(in_ref, out_ref):
    half = ROWS // 2
    lane_rows = iota((ROWS, LOCAL), 1)
    first = lane_rows == 0
    bias_lane = lane_rows == HEAD
    head_lanes = lane_rows < HEAD
    left_causal = position(iota((half, half), 0)) <= position(iota((half, half), 1))
    right_causal = position(iota((ROWS, half), 0)) <= position(iota((ROWS, half), 1) + half)
    slot = iota((ROWS // 8, LOCAL), 1) >> 4
    hidden = jnp.zeros((half, half), BF16)
    pending = None
    for start in range(0, HEADS, 3):
        group = range(start, start + 3)
        blocks, keys, queries, cots = {}, {}, {}, {}
        for h in group:
            block = in_ref[h].astype(F32)
            empty = block[:, :1] > 32768.0
            block = jnp.where(empty & first, 0.0, block)
            query = jnp.where(head_lanes, block * 0.125, jnp.where(bias_lane, 1.0, 0.0))
            queries[h] = query.astype(BF16)
            keys[h] = jnp.where(
                head_lanes, block, jnp.where(bias_lane & empty, -1e30, 0.0)
            ).astype(BF16)
            blocks[h] = block.astype(BF16)
            pair = in_ref[HEADS + h // 2]
            cots[h] = pair[:, :HEAD] if h % 2 == 0 else pair[:, HEAD:]
        tiles = (
            (slice(0, half), slice(0, half), left_causal),
            (slice(0, ROWS), slice(half, ROWS), right_causal),
        )
        scores, d_probs = {}, {}
        for h in group:
            scores[h] = dot(keys[h], queries[h], ((1,), (1,)))
            d_probs[h] = dot(blocks[h][:, HEAD:], cots[h], ((1,), (1,)))
        probs, d_scores = {}, {}
        for h in group:
            parts = []
            for rows, cols, causal in tiles:
                tile = jnp.where(causal, scores[h][rows, cols], -1e30)
                weights = jnp.exp(tile - jnp.max(tile, axis=0, keepdims=True))
                scale = 1.0 / jnp.sum(weights, axis=0, keepdims=True)
                parts.append((weights * scale).astype(BF16))
            lower = [
                (parts[n].astype(F32), d_probs[h][rows, cols])
                for n, (rows, cols, causal) in enumerate(tiles)
            ]
            slopes = [
                (wide * (d_prob - jnp.sum(wide * d_prob, axis=0, keepdims=True))).astype(BF16)
                for wide, d_prob in lower
            ]
            for held, done in ((probs, parts), (d_scores, slopes)):
                left = jnp.concatenate([done[0], hidden], axis=0)
                held[h] = jnp.concatenate([left, done[1]], axis=1)
        for h in group:
            turned = blocks[h].T
            above = dot(turned[:HEAD], d_scores[h])
            above = above + dot(turned[:HEAD], d_scores[h], ((1,), (1,)))
            out = dot(turned[HEAD:], probs[h])
            d_value = dot(cots[h].T, probs[h], ((1,), (1,)))
            grads = jnp.concatenate([above * 0.125, d_value], axis=0).T
            for m, part in enumerate(spread(grads, slot)):
                n = h * 8 + m
                part = part.astype(BF16).reshape(16, 2, LOCAL)
                out_ref[n // 6 * 16 : (n // 6 + 1) * 16, n % 6] = part
            if h % 2 == 0:
                pending = out
            else:
                k = HEADS + h // 2
                joined = jnp.concatenate([pending, out], axis=0).T.astype(BF16)
                out_ref[:, k] = joined.reshape(LOCAL, 2, LOCAL)


def index_of(place_ref, dy, dc):
    return lax.rem(place_ref[0] + dy, 4) * 2 + lax.rem(place_ref[1] + dc, 2)


def partial_kernel(place_ref, in_ref, *refs):
    exts, (out_ref, keep_ref, give_ref), (dests, cols, scratch) = refs[:4], refs[4:7], refs[7:]
    here = place_ref[1]
    j = place_ref[0] * 2 + here
    head = (j * 3 // 4, (j * 6 + 5) // 8)
    lane_slot = iota((ROWS, LOCAL), 1) >> 4
    sub_rows = iota((ROWS, LOCAL), 0).astype(F32)
    for n, (dy, dc) in enumerate(STEPS):
        source = index_of(place_ref, 4 - dy, dc)
        for i in range(2):
            lanes = pl.ds(pl.multiple_of(head[i] * LOCAL, LOCAL), LOCAL)
            dests[i, source] = exts[n // 2][n % 2, LOCAL:, lanes].astype(F32)[:8]
    turned = [in_ref[:, b].reshape(ROWS, LOCAL) for b in range(6)]
    turned = [pltpu.roll(rows.astype(F32), BLOCK * b, 1).astype(BF16) if b else rows for b, rows in enumerate(turned)]
    limit = lax.rem(j, 4)
    limit = jnp.where(limit == 1, 2, jnp.where(limit == 2, 4, 6))
    for p in range(8):
        rows = turned[0]
        for b in range(1, 6):
            rows = jnp.where(lane_slot == (b + p) % 8, turned[b], rows)
        routes = [(sub_rows == dests[i, p, :1]).astype(BF16) for i in range(2)]
        found = dot(rows, jnp.concatenate(routes, axis=1), ((0,), (0,)))
        blocks = []
        for b in range(6):
            cut = slice((b + p) % 8 * BLOCK, ((b + p) % 8 + 1) * BLOCK)
            blocks.append(jnp.where(b < limit, found[cut, :LOCAL], found[cut, LOCAL:]))
        cols[p] = jnp.concatenate(blocks, axis=0).astype(BF16)
    total = None
    for dy in range(4):
        near = [cols[index_of(place_ref, 4 - dy, dc)] for dc in range(2)]
        rows = exts[dy][:, :LOCAL, :].reshape(2 * LOCAL, WIDTH)
        term = dot(jnp.concatenate(near, axis=1), rows)
        total = term if total is None else total + term
    for k in range(WIDTH // LOCAL):
        scratch[k * COLUMNS : (k + 1) * COLUMNS, :] = total[:, k * LOCAL : (k + 1) * LOCAL]
    scratch[16 * PIECE :, :] = jnp.zeros((8, LOCAL), F32)
    for i in range(16):
        out_ref[i] = scratch[i * PIECE : i * PIECE + SLOT, :].astype(BF16)
    for y in range(4):
        keep_ref[y] = cols[y * 2 + here]
        give_ref[y] = cols[y * 2 + 1 - here]


def output_kernel(in_ref, ext_ref, att_ref):
    sub_rows = iota((ROWS, LOCAL), 0).astype(F32)
    head_lanes = iota((LOCAL, LOCAL), 1) < HEAD
    dests = ext_ref[0, LOCAL:, :].astype(F32)[:1]
    for k in range(HEADS // 2):
        rows = in_ref[:, HEADS + k].reshape(ROWS, LOCAL)
        found = []
        for h in (2 * k, 2 * k + 1):
            route = (sub_rows == dests[:, h * LOCAL : (h + 1) * LOCAL]).astype(BF16)
            found.append(dot(route, rows, ((0,), (0,))))
        both = jnp.where(head_lanes, found[0], found[1])
        att_ref[:, k * LOCAL : (k + 1) * LOCAL] = both.astype(BF16)


def pack_kernel(block_ref, keep_ref, got_ref, out_ref, scratch):
    for i in range(16):
        scratch[i * PIECE : (i + 1) * PIECE, :] = block_ref[i].astype(F32)[:PIECE]
    block = scratch[...].astype(BF16)
    for y in range(4):
        out_ref[y, :WHOLE, :] = block
        out_ref[y, WHOLE : WHOLE + MESSAGE, :] = keep_ref[y]
        out_ref[y, WHOLE + MESSAGE :, :] = got_ref[y]


def return_kernel(place_ref, all_ref, ws_ref, wv_ref, grad_ref, held):
    here = place_ref[1]
    for y in range(4):
        held[y * 2 + here] = all_ref[y, WHOLE : WHOLE + MESSAGE, :]
        held[y * 2 + 1 - here] = all_ref[y, WHOLE + MESSAGE :, :]

    def columns(first):
        rows = [
            held[n // 6, n % 6 * BLOCK : (n % 6 + 1) * BLOCK, :]
            for h in range(HEADS)
            for n in range(h * 8 + first, h * 8 + first + 4)
        ]
        return jnp.concatenate(rows, axis=0).astype(F32).T.astype(BF16)

    left = columns(0)
    right = columns(4)
    total = dot(left, ws_ref[...], ((1,), (1,))) + dot(right, wv_ref[...], ((1,), (1,)))
    grad_ref[...] = total.astype(BF16)


def sum_kernel(in_ref, out_ref):
    total = in_ref[0].astype(F32)
    for i in range(1, in_ref.shape[0]):
        total = total + in_ref[i].astype(F32)
    total = total.astype(BF16)
    for i in range(out_ref.shape[0]):
        out_ref[i] = total


def finish_kernel(place_ref, mine_ref, other_ref, shared_ref, value_ref, held, sems):
    first = place_ref[1] == 0
    copies = []
    for k in range(WIDTH // LOCAL):
        rows = slice(k * COLUMNS, (k + 1) * COLUMNS)
        strip = []
        for y in range(4):
            mine = mine_ref[y, rows, :]
            other = other_ref[y, rows, :]
            strip += [jnp.where(first, mine, other), jnp.where(first, other, mine)]
        strip = jnp.concatenate(strip, axis=0)
        lines = slice(k * LOCAL, (k + 1) * LOCAL)
        for half, ref in enumerate((shared_ref, value_ref)):
            heads = [
                strip[h * LOCAL + half * HEAD : h * LOCAL + (half + 1) * HEAD]
                for h in range(HEADS)
            ]
            held[half, lines, :] = jnp.concatenate(heads, axis=0).T
            copies.append(
                pltpu.make_async_copy(held.at[half, lines], ref.at[lines], sems.at[half, k])
            )
            copies[-1].start()
    for copy in copies:
        copy.wait()


def call(kernel, out, *args, scratch=(), scalars=0, held=False, far=()):
    if held:
        args = [pltpu.with_memory_space_constraint(arg, pltpu.HBM) for arg in args]
    specs = [pl.BlockSpec(memory_space=pltpu.SMEM)] * scalars
    specs += [pl.BlockSpec(memory_space=pl.ANY if held else pltpu.VMEM)] * (len(args) - scalars)
    outs = [
        pl.BlockSpec(memory_space=pl.ANY if n in far else pltpu.VMEM) for n in range(len(out))
    ]
    return pl.pallas_call(
        kernel,
        out_shape=out,
        in_specs=specs,
        out_specs=outs,
        scratch_shapes=scratch,
        compiler_params=pltpu.CompilerParams(vmem_limit_bytes=48 * 1024 * 1024),
    )(*args)


def shape(*dims):
    return jax.ShapeDtypeStruct(dims, BF16)


def swap(rows, axes, groups=None):
    return lax.all_to_all(
        rows, axes, split_axis=0, concat_axis=0, tiled=True, axis_index_groups=groups
    )


def body(tokens, w_shared, w_value, cluster_ids, slot_index, cotangent):
    rows = tokens[0]
    place = jnp.stack([lax.axis_index("y"), lax.axis_index("c")]).astype(jnp.int32)
    sent, ext = call(
        send_kernel,
        (shape(LOCAL, 9, 2, LOCAL), shape(LOCAL + 16, WIDTH)),
        cluster_ids.transpose(1, 0, 2),
        rows,
        w_shared,
        w_value,
        cotangent[0],
        scratch=[
            pltpu.VMEM((HEADS, 1, LOCAL), jnp.int32),
            pltpu.VMEM((LOCAL, WIDTH), BF16),
            pltpu.VMEM((WIDTH, PROJ), BF16),
            pltpu.VMEM((WIDTH, PROJ), BF16),
            pltpu.VMEM((LOCAL, PROJ), BF16),
            pltpu.SemaphoreType.DMA((5,)),
        ],
        held=True,
    )

    def shift(pair, dy):
        return lax.ppermute(pair, "y", [(y, (y + dy) % 4) for y in range(4)])

    def flip(part):
        return lax.ppermute(part, "c", [(0, 1), (1, 0)])

    arrived = swap(sent, OWNERS)
    pair = jnp.stack([ext, flip(ext)])
    near = (shift(pair, 1), shift(pair, 3))
    arrived, pair, near, place = lax.optimization_barrier((arrived, pair, near, place))
    exts = [pair, near[0], shift(pair, 2), near[1]]
    arrived = arrived.transpose(1, 0, 2, 3).reshape(9, ROWS, LOCAL)
    (worked,) = call(
        attend_kernel,
        [shape(LOCAL, 9, 2, LOCAL)],
        arrived,
    )
    back = swap(worked, OWNERS)
    part, keep, give = call(
        partial_kernel,
        [shape(16, SLOT, LOCAL), shape(4, MESSAGE, LOCAL), shape(4, MESSAGE, LOCAL)],
        place,
        back,
        *exts,
        scratch=[
            pltpu.VMEM((2, 8, 8, LOCAL), F32),
            pltpu.VMEM((8, COLUMNS, LOCAL), BF16),
            pltpu.VMEM((16 * PIECE + 8, LOCAL), F32),
        ],
        scalars=1,
    )
    part = swap(part, ("x", "z"), NEAR)
    part, back, give = lax.optimization_barrier((part, back, give))
    (attention,) = call(output_kernel, [shape(LOCAL, PROJ)], back, pair)
    (part,) = call(sum_kernel, [shape(4, SLOT, LOCAL)], part)
    part = swap(part, "z", FAR)
    part, got, attention = lax.optimization_barrier((part, flip(give), attention))
    (block,) = call(sum_kernel, [shape(16, SLOT, LOCAL)], part)
    (block,) = call(
        pack_kernel,
        [shape(4, WHOLE + 2 * MESSAGE, LOCAL)],
        swap(block, ("x", "z"), NEAR),
        keep,
        got,
        scratch=[pltpu.VMEM((WHOLE, LOCAL), F32)],
    )
    block = swap(block, "y")
    other = flip(block)
    (grad_tokens,) = call(
        return_kernel,
        [shape(LOCAL, WIDTH)],
        place,
        block,
        w_shared,
        w_value,
        scratch=[pltpu.VMEM((8, MESSAGE, LOCAL), BF16)],
        scalars=1,
    )
    grad_shared, grad_value = call(
        finish_kernel,
        (shape(WIDTH, PROJ), shape(WIDTH, PROJ)),
        place,
        block,
        other,
        scratch=[
            pltpu.VMEM((2, WIDTH, PROJ), BF16),
            pltpu.SemaphoreType.DMA((2, WIDTH // LOCAL)),
        ],
        scalars=1,
        far=(0, 1),
    )
    return (attention[None], grad_tokens[None], grad_shared, grad_value)


def solution(mesh):
    fine = Mesh(mesh.devices.reshape(4, 4, 16, 2), ("x", "y", "z", "c"))
    in_specs = (
        P("x", TOK, None),
        P(),
        P(),
        P("x", None, TOK),
        P("x", None, TOK),
        P("x", TOK, None),
    )
    out_specs = (P("x", TOK, None), P("x", TOK, None), P(), P())
    return jax.shard_map(body, mesh=fine, in_specs=in_specs, out_specs=out_specs, check_vma=False)
```

```python
import jax
import jax.numpy as jnp
from jax import lax
from jax.experimental import pallas as pl
from jax.experimental.pallas import tpu as pltpu
from jax.sharding import Mesh
from jax.sharding import PartitionSpec as P

F32 = jnp.float32
BF16 = jnp.bfloat16
HEADS = 6
HEAD = 64
ROWS = 256
LOCAL = 128
WIDTH = 768
PROJ = 384
UNUSED = 65536.0
PLANE = ("y", "c")
TOK = ("y", "z", "c")
OWNERS = ("y", "c", "z")
RING = [(3, 4, 9, 14), (2, 7, 8, 13), (1, 6, 11, 12), (0, 5, 10, 15)]
FAR = [list(group) for group in RING]
NEAR = [[x * 16 + RING[n][b] for x in range(4) for n in range(4)] for b in range(4)]
STEPS = [(dy, dc) for dy in range(4) for dc in range(2)]
COLUMNS = 96
PIECE = 36
SLOT = 40
BLOCK = 16
WHOLE = 576
MESSAGE = 96


def iota(shape, dim):
    return lax.broadcasted_iota(jnp.int32, shape, dim)


def dot(a, b, dims=((1,), (0,))):
    return lax.dot_general(a, b, (dims, ((), ())), preferred_element_type=F32)


def send_kernel(*refs):
    sources, (out_ref, ext_ref), targets, sems = refs[:5], refs[5:7], refs[7:12], refs[12]
    copies = [
        pltpu.make_async_copy(source, target, sems.at[n])
        for n, (source, target) in enumerate(zip(sources, targets))
    ]
    for copy in copies:
        copy.start()
    cluster_ref, tok_ref, ws_ref, wv_ref, cot_ref = targets
    sub = iota((LOCAL, LOCAL), 0)
    lane = iota((LOCAL, LOCAL), 1)
    sub_rows = iota((ROWS, LOCAL), 0)
    lane_rows = iota((ROWS, LOCAL), 1)
    copies[0].wait()
    hits = []
    marks = []
    for h in range(HEADS):
        cluster = cluster_ref[h]
        member = (sub == cluster).astype(BF16)
        same = dot(member, member, ((0,), (0,)))
        order = jnp.sum(jnp.where(sub < lane, same, 0.0), axis=0, keepdims=True)
        owner = (cluster & 96) + (cluster & 1) * 16 + ((cluster >> 1) & 15)
        dest = owner * 2 + order.astype(jnp.int32)
        ext_ref[LOCAL:, h * LOCAL : (h + 1) * LOCAL] = jnp.broadcast_to(
            dest.astype(F32), (16, LOCAL)
        ).astype(BF16)
        hit = sub_rows == dest
        used = jnp.sum(jnp.where(hit, 1.0, 0.0), axis=1, keepdims=True)
        hits.append(hit.astype(BF16))
        marks.append(jnp.where((lane_rows == 0) & (used < 0.5), UNUSED, 0.0))
    for copy in copies[1:]:
        copy.wait()
    tokens = tok_ref[...]
    ext_ref[:LOCAL, :] = tokens
    shared = dot(tokens, ws_ref[...]).astype(BF16)
    value = dot(tokens, wv_ref[...]).astype(BF16)
    cot = cot_ref[...]
    blank = jnp.zeros((LOCAL, HEAD), BF16)
    pending = None
    for h in range(HEADS):
        cols = slice(h * HEAD, (h + 1) * HEAD)
        tail = [cot[:, cols], blank] if h % 2 == 0 else [blank, cot[:, cols]]
        packed = jnp.concatenate([shared[:, cols], value[:, cols]] + tail, axis=1)
        moved = dot(hits[h], packed)
        out_ref[:, h] = (moved[:, :LOCAL] + marks[h]).astype(BF16).reshape(LOCAL, 2, LOCAL)
        if h % 2 == 0:
            pending = moved[:, LOCAL:]
        else:
            packed = (pending + moved[:, LOCAL:]).astype(BF16)
            out_ref[:, HEADS + h // 2] = packed.reshape(LOCAL, 2, LOCAL)


def position(row):
    return (row & 192) + ((row >> 1) & 15) * 4 + ((row >> 5) & 1) * 2 + (row & 1)


def spread(block, slot):
    rows = block.shape[0] // 8
    parts = [block[p * rows : (p + 1) * rows] for p in range(8)]
    for bit in (1, 2, 4):
        odd = (slot & bit) != 0
        after = list(parts)
        for p in range(8):
            if p & bit == 0:
                low, high = parts[p], parts[p + bit]
                after[p] = jnp.where(odd, pltpu.roll(high, BLOCK * bit, 1), low)
                after[p + bit] = jnp.where(odd, high, pltpu.roll(low, LOCAL - BLOCK * bit, 1))
        parts = after
    return parts


def attend_kernel(in_ref, out_ref):
    half = ROWS // 2
    lane_rows = iota((ROWS, LOCAL), 1)
    first = lane_rows == 0
    bias_lane = lane_rows == HEAD
    head_lanes = lane_rows < HEAD
    left_causal = position(iota((half, half), 0)) <= position(iota((half, half), 1))
    right_causal = position(iota((ROWS, half), 0)) <= position(iota((ROWS, half), 1) + half)
    slot = iota((ROWS // 8, LOCAL), 1) >> 4
    hidden = jnp.zeros((half, half), BF16)
    pending = None
    for start in range(0, HEADS, 3):
        group = range(start, start + 3)
        blocks, keys, queries, cots = {}, {}, {}, {}
        for h in group:
            block = in_ref[h].astype(F32)
            empty = block[:, :1] > 32768.0
            block = jnp.where(empty & first, 0.0, block)
            query = jnp.where(head_lanes, block * 0.125, jnp.where(bias_lane, 1.0, 0.0))
            queries[h] = query.astype(BF16)
            keys[h] = jnp.where(
                head_lanes, block, jnp.where(bias_lane & empty, -1e30, 0.0)
            ).astype(BF16)
            blocks[h] = block.astype(BF16)
            pair = in_ref[HEADS + h // 2]
            cots[h] = pair[:, :HEAD] if h % 2 == 0 else pair[:, HEAD:]
        tiles = (
            (slice(0, half), slice(0, half), left_causal),
            (slice(0, ROWS), slice(half, ROWS), right_causal),
        )
        scores, d_probs = {}, {}
        for h in group:
            scores[h] = dot(keys[h], queries[h], ((1,), (1,)))
            d_probs[h] = dot(blocks[h][:, HEAD:], cots[h], ((1,), (1,)))
        probs, d_scores = {}, {}
        for h in group:
            parts = []
            for rows, cols, causal in tiles:
                tile = jnp.where(causal, scores[h][rows, cols], -1e30)
                weights = jnp.exp(tile - jnp.max(tile, axis=0, keepdims=True))
                scale = 1.0 / jnp.sum(weights, axis=0, keepdims=True)
                parts.append((weights * scale).astype(BF16))
            lower = [
                (parts[n].astype(F32), d_probs[h][rows, cols])
                for n, (rows, cols, causal) in enumerate(tiles)
            ]
            slopes = [
                (wide * (d_prob - jnp.sum(wide * d_prob, axis=0, keepdims=True))).astype(BF16)
                for wide, d_prob in lower
            ]
            for held, done in ((probs, parts), (d_scores, slopes)):
                left = jnp.concatenate([done[0], hidden], axis=0)
                held[h] = jnp.concatenate([left, done[1]], axis=1)
        for h in group:
            turned = blocks[h].T
            above = dot(turned[:HEAD], d_scores[h])
            above = above + dot(turned[:HEAD], d_scores[h], ((1,), (1,)))
            out = dot(turned[HEAD:], probs[h])
            d_value = dot(cots[h].T, probs[h], ((1,), (1,)))
            grads = jnp.concatenate([above * 0.125, d_value], axis=0).T
            for m, part in enumerate(spread(grads, slot)):
                n = h * 8 + m
                part = part.astype(BF16).reshape(16, 2, LOCAL)
                out_ref[n // 6 * 16 : (n // 6 + 1) * 16, n % 6] = part
            if h % 2 == 0:
                pending = out
            else:
                k = HEADS + h // 2
                joined = jnp.concatenate([pending, out], axis=0).T.astype(BF16)
                out_ref[:, k] = joined.reshape(LOCAL, 2, LOCAL)


def index_of(place_ref, dy, dc):
    return lax.rem(place_ref[0] + dy, 4) * 2 + lax.rem(place_ref[1] + dc, 2)


def partial_kernel(place_ref, in_ref, *refs):
    exts, (out_ref, keep_ref, give_ref), (dests, cols, scratch) = refs[:4], refs[4:7], refs[7:]
    here = place_ref[1]
    j = place_ref[0] * 2 + here
    head = (j * 3 // 4, (j * 6 + 5) // 8)
    lane_slot = iota((ROWS, LOCAL), 1) >> 4
    sub_rows = iota((ROWS, LOCAL), 0).astype(F32)
    for n, (dy, dc) in enumerate(STEPS):
        source = index_of(place_ref, 4 - dy, dc)
        for i in range(2):
            lanes = pl.ds(pl.multiple_of(head[i] * LOCAL, LOCAL), LOCAL)
            dests[i, source] = exts[n // 2][n % 2, LOCAL:, lanes].astype(F32)[:8]
    turned = [in_ref[:, b].reshape(ROWS, LOCAL) for b in range(6)]
    turned = [pltpu.roll(rows.astype(F32), BLOCK * b, 1).astype(BF16) if b else rows for b, rows in enumerate(turned)]
    limit = lax.rem(j, 4)
    limit = jnp.where(limit == 1, 2, jnp.where(limit == 2, 4, 6))
    for p in range(8):
        rows = turned[0]
        for b in range(1, 6):
            rows = jnp.where(lane_slot == (b + p) % 8, turned[b], rows)
        routes = [(sub_rows == dests[i, p, :1]).astype(BF16) for i in range(2)]
        found = dot(rows, jnp.concatenate(routes, axis=1), ((0,), (0,)))
        blocks = []
        for b in range(6):
            cut = slice((b + p) % 8 * BLOCK, ((b + p) % 8 + 1) * BLOCK)
            blocks.append(jnp.where(b < limit, found[cut, :LOCAL], found[cut, LOCAL:]))
        cols[p] = jnp.concatenate(blocks, axis=0).astype(BF16)
    total = None
    for dy in range(4):
        near = [cols[index_of(place_ref, 4 - dy, dc)] for dc in range(2)]
        rows = exts[dy][:, :LOCAL, :].reshape(2 * LOCAL, WIDTH)
        term = dot(jnp.concatenate(near, axis=1), rows)
        total = term if total is None else total + term
    for k in range(WIDTH // LOCAL):
        scratch[k * COLUMNS : (k + 1) * COLUMNS, :] = total[:, k * LOCAL : (k + 1) * LOCAL]
    scratch[16 * PIECE :, :] = jnp.zeros((8, LOCAL), F32)
    for i in range(16):
        out_ref[i] = scratch[i * PIECE : i * PIECE + SLOT, :].astype(BF16)
    for y in range(4):
        keep_ref[y] = cols[y * 2 + here]
        give_ref[y] = cols[y * 2 + 1 - here]


def output_kernel(in_ref, ext_ref, att_ref):
    sub_rows = iota((ROWS, LOCAL), 0).astype(F32)
    head_lanes = iota((LOCAL, LOCAL), 1) < HEAD
    dests = ext_ref[0, LOCAL:, :].astype(F32)[:1]
    for k in range(HEADS // 2):
        rows = in_ref[:, HEADS + k].reshape(ROWS, LOCAL)
        found = []
        for h in (2 * k, 2 * k + 1):
            route = (sub_rows == dests[:, h * LOCAL : (h + 1) * LOCAL]).astype(BF16)
            found.append(dot(route, rows, ((0,), (0,))))
        both = jnp.where(head_lanes, found[0], found[1])
        att_ref[:, k * LOCAL : (k + 1) * LOCAL] = both.astype(BF16)


def pack_kernel(block_ref, keep_ref, got_ref, out_ref, scratch):
    for i in range(16):
        scratch[i * PIECE : (i + 1) * PIECE, :] = block_ref[i].astype(F32)[:PIECE]
    block = scratch[...].astype(BF16)
    for y in range(4):
        out_ref[y, :WHOLE, :] = block
        out_ref[y, WHOLE : WHOLE + MESSAGE, :] = keep_ref[y]
        out_ref[y, WHOLE + MESSAGE :, :] = got_ref[y]


def return_kernel(place_ref, all_ref, ws_ref, wv_ref, grad_ref, held):
    here = place_ref[1]
    for y in range(4):
        held[y * 2 + here] = all_ref[y, WHOLE : WHOLE + MESSAGE, :]
        held[y * 2 + 1 - here] = all_ref[y, WHOLE + MESSAGE :, :]

    def columns(first):
        rows = [
            held[n // 6, n % 6 * BLOCK : (n % 6 + 1) * BLOCK, :]
            for h in range(HEADS)
            for n in range(h * 8 + first, h * 8 + first + 4)
        ]
        return jnp.concatenate(rows, axis=0).astype(F32).T.astype(BF16)

    left = columns(0)
    right = columns(4)
    total = dot(left, ws_ref[...], ((1,), (1,))) + dot(right, wv_ref[...], ((1,), (1,)))
    grad_ref[...] = total.astype(BF16)


def sum_kernel(in_ref, out_ref):
    total = in_ref[0].astype(F32)
    for i in range(1, in_ref.shape[0]):
        total = total + in_ref[i].astype(F32)
    total = total.astype(BF16)
    for i in range(out_ref.shape[0]):
        out_ref[i] = total


def finish_kernel(place_ref, mine_ref, other_ref, shared_ref, value_ref, held, sems):
    first = place_ref[1] == 0
    copies = []
    for k in range(WIDTH // LOCAL):
        rows = slice(k * COLUMNS, (k + 1) * COLUMNS)
        strip = []
        for y in range(4):
            mine = mine_ref[y, rows, :]
            other = other_ref[y, rows, :]
            strip += [jnp.where(first, mine, other), jnp.where(first, other, mine)]
        strip = jnp.concatenate(strip, axis=0)
        lines = slice(k * LOCAL, (k + 1) * LOCAL)
        for half, ref in enumerate((shared_ref, value_ref)):
            heads = [
                strip[h * LOCAL + half * HEAD : h * LOCAL + (half + 1) * HEAD]
                for h in range(HEADS)
            ]
            held[half, lines, :] = jnp.concatenate(heads, axis=0).T
            copies.append(
                pltpu.make_async_copy(held.at[half, lines], ref.at[lines], sems.at[half, k])
            )
            copies[-1].start()
    for copy in copies:
        copy.wait()


def call(kernel, out, *args, scratch=(), scalars=0, held=False, far=()):
    if held:
        args = [pltpu.with_memory_space_constraint(arg, pltpu.HBM) for arg in args]
    specs = [pl.BlockSpec(memory_space=pltpu.SMEM)] * scalars
    specs += [pl.BlockSpec(memory_space=pl.ANY if held else pltpu.VMEM)] * (len(args) - scalars)
    outs = [
        pl.BlockSpec(memory_space=pl.ANY if n in far else pltpu.VMEM) for n in range(len(out))
    ]
    return pl.pallas_call(
        kernel,
        out_shape=out,
        in_specs=specs,
        out_specs=outs,
        scratch_shapes=scratch,
        compiler_params=pltpu.CompilerParams(vmem_limit_bytes=48 * 1024 * 1024),
    )(*args)


def shape(*dims):
    return jax.ShapeDtypeStruct(dims, BF16)


def swap(rows, axes, groups=None):
    return lax.all_to_all(
        rows, axes, split_axis=0, concat_axis=0, tiled=True, axis_index_groups=groups
    )


def body(tokens, w_shared, w_value, cluster_ids, slot_index, cotangent):
    rows = tokens[0]
    place = jnp.stack([lax.axis_index("y"), lax.axis_index("c")]).astype(jnp.int32)
    sent, ext = call(
        send_kernel,
        (shape(LOCAL, 9, 2, LOCAL), shape(LOCAL + 16, WIDTH)),
        cluster_ids.transpose(1, 0, 2),
        rows,
        w_shared,
        w_value,
        cotangent[0],
        scratch=[
            pltpu.VMEM((HEADS, 1, LOCAL), jnp.int32),
            pltpu.VMEM((LOCAL, WIDTH), BF16),
            pltpu.VMEM((WIDTH, PROJ), BF16),
            pltpu.VMEM((WIDTH, PROJ), BF16),
            pltpu.VMEM((LOCAL, PROJ), BF16),
            pltpu.SemaphoreType.DMA((5,)),
        ],
        held=True,
    )

    def shift(pair, dy):
        return lax.ppermute(pair, "y", [(y, (y + dy) % 4) for y in range(4)])

    def flip(part):
        return lax.ppermute(part, "c", [(0, 1), (1, 0)])

    arrived = swap(sent, OWNERS)
    arrived, ext = lax.optimization_barrier((arrived, ext))
    pair = jnp.stack([ext, flip(ext)])
    exts = [pair] + [shift(pair, dy) for dy in range(1, 4)]
    arrived = arrived.transpose(1, 0, 2, 3).reshape(9, ROWS, LOCAL)
    (worked,) = call(
        attend_kernel,
        [shape(LOCAL, 9, 2, LOCAL)],
        arrived,
    )
    back = swap(worked, OWNERS)
    part, keep, give = call(
        partial_kernel,
        [shape(16, SLOT, LOCAL), shape(4, MESSAGE, LOCAL), shape(4, MESSAGE, LOCAL)],
        place,
        back,
        *exts,
        scratch=[
            pltpu.VMEM((2, 8, 8, LOCAL), F32),
            pltpu.VMEM((8, COLUMNS, LOCAL), BF16),
            pltpu.VMEM((16 * PIECE + 8, LOCAL), F32),
        ],
        scalars=1,
    )
    part = swap(part, ("x", "z"), NEAR)
    part, back, give = lax.optimization_barrier((part, back, give))
    (attention,) = call(output_kernel, [shape(LOCAL, PROJ)], back, pair)
    (part,) = call(sum_kernel, [shape(4, SLOT, LOCAL)], part)
    part = swap(part, "z", FAR)
    part, got, attention = lax.optimization_barrier((part, flip(give), attention))
    (block,) = call(sum_kernel, [shape(16, SLOT, LOCAL)], part)
    (block,) = call(
        pack_kernel,
        [shape(4, WHOLE + 2 * MESSAGE, LOCAL)],
        swap(block, ("x", "z"), NEAR),
        keep,
        got,
        scratch=[pltpu.VMEM((WHOLE, LOCAL), F32)],
    )
    block = swap(block, "y")
    other = flip(block)
    (grad_tokens,) = call(
        return_kernel,
        [shape(LOCAL, WIDTH)],
        place,
        block,
        w_shared,
        w_value,
        scratch=[pltpu.VMEM((8, MESSAGE, LOCAL), BF16)],
        scalars=1,
    )
    grad_shared, grad_value = call(
        finish_kernel,
        (shape(WIDTH, PROJ), shape(WIDTH, PROJ)),
        place,
        block,
        other,
        scratch=[
            pltpu.VMEM((2, WIDTH, PROJ), BF16),
            pltpu.SemaphoreType.DMA((2, WIDTH // LOCAL)),
        ],
        scalars=1,
        far=(0, 1),
    )
    return (attention[None], grad_tokens[None], grad_shared, grad_value)


def solution(mesh):
    fine = Mesh(mesh.devices.reshape(4, 4, 16, 2), ("x", "y", "z", "c"))
    in_specs = (
        P("x", TOK, None),
        P(),
        P(),
        P("x", None, TOK),
        P("x", None, TOK),
        P("x", TOK, None),
    )
    out_specs = (P("x", TOK, None), P("x", TOK, None), P(), P())
    return jax.shard_map(body, mesh=fine, in_specs=in_specs, out_specs=out_specs, check_vma=False)
```

```python
import jax
import jax.numpy as jnp
from jax import lax
from jax.experimental import pallas as pl
from jax.experimental.pallas import tpu as pltpu
from jax.sharding import Mesh
from jax.sharding import PartitionSpec as P

F32 = jnp.float32
BF16 = jnp.bfloat16
HEADS = 6
HEAD = 64
ROWS = 256
LOCAL = 128
WIDTH = 768
PROJ = 384
UNUSED = 65536.0
PLANE = ("y", "c")
TOK = ("y", "z", "c")
OWNERS = ("y", "c", "z")
RING = [(3, 4, 9, 14), (2, 7, 8, 13), (1, 6, 11, 12), (0, 5, 10, 15)]
FAR = [list(group) for group in RING]
NEAR = [[x * 16 + RING[n][b] for x in range(4) for n in range(4)] for b in range(4)]
STEPS = [(dy, dc) for dy in range(4) for dc in range(2)]
COLUMNS = 96
PIECE = 36
SLOT = 40
BLOCK = 16
WHOLE = 576
MESSAGE = 96


def iota(shape, dim):
    return lax.broadcasted_iota(jnp.int32, shape, dim)


def dot(a, b, dims=((1,), (0,))):
    return lax.dot_general(a, b, (dims, ((), ())), preferred_element_type=F32)


def send_kernel(*refs):
    sources, (out_ref, ext_ref), targets, sems = refs[:5], refs[5:7], refs[7:12], refs[12]
    copies = [
        pltpu.make_async_copy(source, target, sems.at[n])
        for n, (source, target) in enumerate(zip(sources, targets))
    ]
    for copy in copies:
        copy.start()
    cluster_ref, tok_ref, ws_ref, wv_ref, cot_ref = targets
    sub = iota((LOCAL, LOCAL), 0)
    lane = iota((LOCAL, LOCAL), 1)
    sub_rows = iota((ROWS, LOCAL), 0)
    lane_rows = iota((ROWS, LOCAL), 1)
    copies[0].wait()
    hits = []
    marks = []
    for h in range(HEADS):
        cluster = cluster_ref[h]
        member = (sub == cluster).astype(BF16)
        same = dot(member, member, ((0,), (0,)))
        order = jnp.sum(jnp.where(sub < lane, same, 0.0), axis=0, keepdims=True)
        owner = (cluster & 96) + (cluster & 1) * 16 + ((cluster >> 1) & 15)
        dest = owner * 2 + order.astype(jnp.int32)
        ext_ref[LOCAL:, h * LOCAL : (h + 1) * LOCAL] = jnp.broadcast_to(
            dest.astype(F32), (16, LOCAL)
        ).astype(BF16)
        hit = sub_rows == dest
        used = jnp.sum(jnp.where(hit, 1.0, 0.0), axis=1, keepdims=True)
        hits.append(hit.astype(BF16))
        marks.append(jnp.where((lane_rows == 0) & (used < 0.5), UNUSED, 0.0))
    for copy in copies[1:]:
        copy.wait()
    tokens = tok_ref[...]
    ext_ref[:LOCAL, :] = tokens
    shared = dot(tokens, ws_ref[...]).astype(BF16)
    value = dot(tokens, wv_ref[...]).astype(BF16)
    cot = cot_ref[...]
    blank = jnp.zeros((LOCAL, HEAD), BF16)
    pending = None
    for h in range(HEADS):
        cols = slice(h * HEAD, (h + 1) * HEAD)
        tail = [cot[:, cols], blank] if h % 2 == 0 else [blank, cot[:, cols]]
        packed = jnp.concatenate([shared[:, cols], value[:, cols]] + tail, axis=1)
        moved = dot(hits[h], packed)
        out_ref[:, h] = (moved[:, :LOCAL] + marks[h]).astype(BF16).reshape(LOCAL, 2, LOCAL)
        if h % 2 == 0:
            pending = moved[:, LOCAL:]
        else:
            packed = (pending + moved[:, LOCAL:]).astype(BF16)
            out_ref[:, HEADS + h // 2] = packed.reshape(LOCAL, 2, LOCAL)


def position(row):
    return (row & 192) + ((row >> 1) & 15) * 4 + ((row >> 5) & 1) * 2 + (row & 1)


def spread(block, slot):
    rows = block.shape[0] // 8
    parts = [block[p * rows : (p + 1) * rows] for p in range(8)]
    for bit in (1, 2, 4):
        odd = (slot & bit) != 0
        after = list(parts)
        for p in range(8):
            if p & bit == 0:
                low, high = parts[p], parts[p + bit]
                after[p] = jnp.where(odd, pltpu.roll(high, BLOCK * bit, 1), low)
                after[p + bit] = jnp.where(odd, high, pltpu.roll(low, LOCAL - BLOCK * bit, 1))
        parts = after
    return parts


def attend_kernel(in_ref, out_ref):
    half = ROWS // 2
    lane_rows = iota((ROWS, LOCAL), 1)
    first = lane_rows == 0
    bias_lane = lane_rows == HEAD
    head_lanes = lane_rows < HEAD
    left_causal = position(iota((half, half), 0)) <= position(iota((half, half), 1))
    right_causal = position(iota((ROWS, half), 0)) <= position(iota((ROWS, half), 1) + half)
    slot = iota((ROWS // 8, LOCAL), 1) >> 4
    hidden = jnp.zeros((half, half), BF16)
    pending = None
    for start in range(0, HEADS, 3):
        group = range(start, start + 3)
        blocks, keys, queries, cots = {}, {}, {}, {}
        for h in group:
            block = in_ref[h].astype(F32)
            empty = block[:, :1] > 32768.0
            block = jnp.where(empty & first, 0.0, block)
            query = jnp.where(head_lanes, block * 0.125, jnp.where(bias_lane, 1.0, 0.0))
            queries[h] = query.astype(BF16)
            keys[h] = jnp.where(
                head_lanes, block, jnp.where(bias_lane & empty, -1e30, 0.0)
            ).astype(BF16)
            blocks[h] = block.astype(BF16)
            pair = in_ref[HEADS + h // 2]
            cots[h] = pair[:, :HEAD] if h % 2 == 0 else pair[:, HEAD:]
        tiles = (
            (slice(0, half), slice(0, half), left_causal),
            (slice(0, ROWS), slice(half, ROWS), right_causal),
        )
        scores, d_probs = {}, {}
        for h in group:
            scores[h] = dot(keys[h], queries[h], ((1,), (1,)))
            d_probs[h] = dot(blocks[h][:, HEAD:], cots[h], ((1,), (1,)))
        probs, d_scores = {}, {}
        for h in group:
            parts = []
            for rows, cols, causal in tiles:
                tile = jnp.where(causal, scores[h][rows, cols], -1e30)
                weights = jnp.exp(tile - jnp.max(tile, axis=0, keepdims=True))
                scale = 1.0 / jnp.sum(weights, axis=0, keepdims=True)
                parts.append((weights * scale).astype(BF16))
            lower = [
                (parts[n].astype(F32), d_probs[h][rows, cols])
                for n, (rows, cols, causal) in enumerate(tiles)
            ]
            slopes = [
                (wide * (d_prob - jnp.sum(wide * d_prob, axis=0, keepdims=True))).astype(BF16)
                for wide, d_prob in lower
            ]
            for held, done in ((probs, parts), (d_scores, slopes)):
                left = jnp.concatenate([done[0], hidden], axis=0)
                held[h] = jnp.concatenate([left, done[1]], axis=1)
        for h in group:
            turned = blocks[h].T
            above = dot(turned[:HEAD], d_scores[h])
            above = above + dot(turned[:HEAD], d_scores[h], ((1,), (1,)))
            out = dot(turned[HEAD:], probs[h])
            d_value = dot(cots[h].T, probs[h], ((1,), (1,)))
            grads = jnp.concatenate([above * 0.125, d_value], axis=0).T
            for m, part in enumerate(spread(grads, slot)):
                n = h * 8 + m
                part = part.astype(BF16).reshape(16, 2, LOCAL)
                out_ref[n // 6 * 16 : (n // 6 + 1) * 16, n % 6] = part
            if h % 2 == 0:
                pending = out
            else:
                k = HEADS + h // 2
                joined = jnp.concatenate([pending, out], axis=0).T.astype(BF16)
                out_ref[:, k] = joined.reshape(LOCAL, 2, LOCAL)


def index_of(place_ref, dy, dc):
    return lax.rem(place_ref[0] + dy, 4) * 2 + lax.rem(place_ref[1] + dc, 2)


def partial_kernel(place_ref, in_ref, *refs):
    exts, (out_ref, keep_ref, give_ref), (dests, cols, scratch) = refs[:2], refs[2:5], refs[5:]
    here = place_ref[1]
    j = place_ref[0] * 2 + here
    head = (j * 3 // 4, (j * 6 + 5) // 8)
    lane_slot = iota((ROWS, LOCAL), 1) >> 4
    sub_rows = iota((ROWS, LOCAL), 0).astype(F32)
    for n, (dy, dc) in enumerate(STEPS):
        source = index_of(place_ref, 4 - dy, dc)
        for i in range(2):
            lanes = pl.ds(pl.multiple_of(head[i] * LOCAL, LOCAL), LOCAL)
            dests[i, source] = exts[dc][dy, LOCAL:, lanes].astype(F32)[:8]
    turned = [in_ref[:, b].reshape(ROWS, LOCAL) for b in range(6)]
    turned = [pltpu.roll(rows.astype(F32), BLOCK * b, 1).astype(BF16) if b else rows for b, rows in enumerate(turned)]
    limit = lax.rem(j, 4)
    limit = jnp.where(limit == 1, 2, jnp.where(limit == 2, 4, 6))
    for p in range(8):
        rows = turned[0]
        for b in range(1, 6):
            rows = jnp.where(lane_slot == (b + p) % 8, turned[b], rows)
        routes = [(sub_rows == dests[i, p, :1]).astype(BF16) for i in range(2)]
        found = dot(rows, jnp.concatenate(routes, axis=1), ((0,), (0,)))
        blocks = []
        for b in range(6):
            cut = slice((b + p) % 8 * BLOCK, ((b + p) % 8 + 1) * BLOCK)
            blocks.append(jnp.where(b < limit, found[cut, :LOCAL], found[cut, LOCAL:]))
        cols[p] = jnp.concatenate(blocks, axis=0).astype(BF16)
    total = None
    for dy in range(4):
        near = [cols[index_of(place_ref, 4 - dy, dc)] for dc in range(2)]
        rows = jnp.concatenate([exts[dc][dy, :LOCAL, :] for dc in range(2)], axis=0)
        term = dot(jnp.concatenate(near, axis=1), rows)
        total = term if total is None else total + term
    for k in range(WIDTH // LOCAL):
        scratch[k * COLUMNS : (k + 1) * COLUMNS, :] = total[:, k * LOCAL : (k + 1) * LOCAL]
    scratch[16 * PIECE :, :] = jnp.zeros((8, LOCAL), F32)
    for i in range(16):
        out_ref[i] = scratch[i * PIECE : i * PIECE + SLOT, :].astype(BF16)
    for y in range(4):
        keep_ref[y] = cols[y * 2 + here]
        give_ref[y] = cols[y * 2 + 1 - here]


def output_kernel(in_ref, ext_ref, att_ref):
    sub_rows = iota((ROWS, LOCAL), 0).astype(F32)
    head_lanes = iota((LOCAL, LOCAL), 1) < HEAD
    dests = ext_ref[0, LOCAL:, :].astype(F32)[:1]
    for k in range(HEADS // 2):
        rows = in_ref[:, HEADS + k].reshape(ROWS, LOCAL)
        found = []
        for h in (2 * k, 2 * k + 1):
            route = (sub_rows == dests[:, h * LOCAL : (h + 1) * LOCAL]).astype(BF16)
            found.append(dot(route, rows, ((0,), (0,))))
        both = jnp.where(head_lanes, found[0], found[1])
        att_ref[:, k * LOCAL : (k + 1) * LOCAL] = both.astype(BF16)


def pack_kernel(block_ref, keep_ref, got_ref, out_ref, scratch):
    for i in range(16):
        scratch[i * PIECE : (i + 1) * PIECE, :] = block_ref[i].astype(F32)[:PIECE]
    block = scratch[...].astype(BF16)
    for y in range(4):
        out_ref[y, :WHOLE, :] = block
        out_ref[y, WHOLE : WHOLE + MESSAGE, :] = keep_ref[y]
        out_ref[y, WHOLE + MESSAGE :, :] = got_ref[y]


def return_kernel(place_ref, all_ref, ws_ref, wv_ref, grad_ref, held):
    here = place_ref[1]
    for y in range(4):
        held[y * 2 + here] = all_ref[y, WHOLE : WHOLE + MESSAGE, :]
        held[y * 2 + 1 - here] = all_ref[y, WHOLE + MESSAGE :, :]

    def columns(first):
        rows = [
            held[n // 6, n % 6 * BLOCK : (n % 6 + 1) * BLOCK, :]
            for h in range(HEADS)
            for n in range(h * 8 + first, h * 8 + first + 4)
        ]
        return jnp.concatenate(rows, axis=0).astype(F32).T.astype(BF16)

    left = columns(0)
    right = columns(4)
    total = dot(left, ws_ref[...], ((1,), (1,))) + dot(right, wv_ref[...], ((1,), (1,)))
    grad_ref[...] = total.astype(BF16)


def sum_kernel(in_ref, out_ref):
    total = in_ref[0].astype(F32)
    for i in range(1, in_ref.shape[0]):
        total = total + in_ref[i].astype(F32)
    total = total.astype(BF16)
    for i in range(out_ref.shape[0]):
        out_ref[i] = total


def finish_kernel(place_ref, mine_ref, other_ref, shared_ref, value_ref, held, sems):
    first = place_ref[1] == 0
    copies = []
    for k in range(WIDTH // LOCAL):
        rows = slice(k * COLUMNS, (k + 1) * COLUMNS)
        strip = []
        for y in range(4):
            mine = mine_ref[y, rows, :]
            other = other_ref[y, rows, :]
            strip += [jnp.where(first, mine, other), jnp.where(first, other, mine)]
        strip = jnp.concatenate(strip, axis=0)
        lines = slice(k * LOCAL, (k + 1) * LOCAL)
        for half, ref in enumerate((shared_ref, value_ref)):
            heads = [
                strip[h * LOCAL + half * HEAD : h * LOCAL + (half + 1) * HEAD]
                for h in range(HEADS)
            ]
            held[half, lines, :] = jnp.concatenate(heads, axis=0).T
            copies.append(
                pltpu.make_async_copy(held.at[half, lines], ref.at[lines], sems.at[half, k])
            )
            copies[-1].start()
    for copy in copies:
        copy.wait()


def call(kernel, out, *args, scratch=(), scalars=0, held=False, far=()):
    if held:
        args = [pltpu.with_memory_space_constraint(arg, pltpu.HBM) for arg in args]
    specs = [pl.BlockSpec(memory_space=pltpu.SMEM)] * scalars
    specs += [pl.BlockSpec(memory_space=pl.ANY if held else pltpu.VMEM)] * (len(args) - scalars)
    outs = [
        pl.BlockSpec(memory_space=pl.ANY if n in far else pltpu.VMEM) for n in range(len(out))
    ]
    return pl.pallas_call(
        kernel,
        out_shape=out,
        in_specs=specs,
        out_specs=outs,
        scratch_shapes=scratch,
        compiler_params=pltpu.CompilerParams(vmem_limit_bytes=48 * 1024 * 1024),
    )(*args)


def shape(*dims):
    return jax.ShapeDtypeStruct(dims, BF16)


def swap(rows, axes, groups=None):
    return lax.all_to_all(
        rows, axes, split_axis=0, concat_axis=0, tiled=True, axis_index_groups=groups
    )


def body(tokens, w_shared, w_value, cluster_ids, slot_index, cotangent):
    rows = tokens[0]
    place = jnp.stack([lax.axis_index("y"), lax.axis_index("c")]).astype(jnp.int32)
    sent, ext = call(
        send_kernel,
        (shape(LOCAL, 9, 2, LOCAL), shape(LOCAL + 16, WIDTH)),
        cluster_ids.transpose(1, 0, 2),
        rows,
        w_shared,
        w_value,
        cotangent[0],
        scratch=[
            pltpu.VMEM((HEADS, 1, LOCAL), jnp.int32),
            pltpu.VMEM((LOCAL, WIDTH), BF16),
            pltpu.VMEM((WIDTH, PROJ), BF16),
            pltpu.VMEM((WIDTH, PROJ), BF16),
            pltpu.VMEM((LOCAL, PROJ), BF16),
            pltpu.SemaphoreType.DMA((5,)),
        ],
        held=True,
    )

    def shift(pair, dy):
        return lax.ppermute(pair, "y", [(y, (y + dy) % 4) for y in range(4)])

    def flip(part):
        return lax.ppermute(part, "c", [(0, 1), (1, 0)])

    arrived = swap(sent, OWNERS)
    arrived, ext = lax.optimization_barrier((arrived, ext))
    mine = jnp.stack([ext] + [shift(ext, dy) for dy in range(1, 4)])
    exts = [mine, flip(mine)]
    arrived = arrived.transpose(1, 0, 2, 3).reshape(9, ROWS, LOCAL)
    (worked,) = call(
        attend_kernel,
        [shape(LOCAL, 9, 2, LOCAL)],
        arrived,
    )
    back = swap(worked, OWNERS)
    part, keep, give = call(
        partial_kernel,
        [shape(16, SLOT, LOCAL), shape(4, MESSAGE, LOCAL), shape(4, MESSAGE, LOCAL)],
        place,
        back,
        *exts,
        scratch=[
            pltpu.VMEM((2, 8, 8, LOCAL), F32),
            pltpu.VMEM((8, COLUMNS, LOCAL), BF16),
            pltpu.VMEM((16 * PIECE + 8, LOCAL), F32),
        ],
        scalars=1,
    )
    part = swap(part, ("x", "z"), NEAR)
    part, back, give = lax.optimization_barrier((part, back, give))
    (attention,) = call(output_kernel, [shape(LOCAL, PROJ)], back, mine)
    (part,) = call(sum_kernel, [shape(4, SLOT, LOCAL)], part)
    part = swap(part, "z", FAR)
    part, got, attention = lax.optimization_barrier((part, flip(give), attention))
    (block,) = call(sum_kernel, [shape(16, SLOT, LOCAL)], part)
    (block,) = call(
        pack_kernel,
        [shape(4, WHOLE + 2 * MESSAGE, LOCAL)],
        swap(block, ("x", "z"), NEAR),
        keep,
        got,
        scratch=[pltpu.VMEM((WHOLE, LOCAL), F32)],
    )
    block = swap(block, "y")
    other = flip(block)
    (grad_tokens,) = call(
        return_kernel,
        [shape(LOCAL, WIDTH)],
        place,
        block,
        w_shared,
        w_value,
        scratch=[pltpu.VMEM((8, MESSAGE, LOCAL), BF16)],
        scalars=1,
    )
    grad_shared, grad_value = call(
        finish_kernel,
        (shape(WIDTH, PROJ), shape(WIDTH, PROJ)),
        place,
        block,
        other,
        scratch=[
            pltpu.VMEM((2, WIDTH, PROJ), BF16),
            pltpu.SemaphoreType.DMA((2, WIDTH // LOCAL)),
        ],
        scalars=1,
        far=(0, 1),
    )
    return (attention[None], grad_tokens[None], grad_shared, grad_value)


def solution(mesh):
    fine = Mesh(mesh.devices.reshape(4, 4, 16, 2), ("x", "y", "z", "c"))
    in_specs = (
        P("x", TOK, None),
        P(),
        P(),
        P("x", None, TOK),
        P("x", None, TOK),
        P("x", TOK, None),
    )
    out_specs = (P("x", TOK, None), P("x", TOK, None), P(), P())
    return jax.shard_map(body, mesh=fine, in_specs=in_specs, out_specs=out_specs, check_vma=False)
```

```python
import jax
import jax.numpy as jnp
from jax import lax
from jax.experimental import pallas as pl
from jax.experimental.pallas import tpu as pltpu
from jax.sharding import Mesh
from jax.sharding import PartitionSpec as P

F32 = jnp.float32
BF16 = jnp.bfloat16
HEADS = 6
HEAD = 64
ROWS = 256
LOCAL = 128
WIDTH = 768
PROJ = 384
UNUSED = 65536.0
PLANE = ("y", "c")
TOK = ("y", "z", "c")
OWNERS = ("y", "c", "z")
RING = [(3, 4, 9, 14), (2, 7, 8, 13), (1, 6, 11, 12), (0, 5, 10, 15)]
FAR = [list(group) for group in RING]
NEAR = [[x * 16 + RING[n][b] for x in range(4) for n in range(4)] for b in range(4)]
STEPS = [(dy, dc) for dy in range(4) for dc in range(2)]
COLUMNS = 96
PIECE = 36
SLOT = 40
BLOCK = 16
WHOLE = 576
MESSAGE = 96


def iota(shape, dim):
    return lax.broadcasted_iota(jnp.int32, shape, dim)


def dot(a, b, dims=((1,), (0,))):
    return lax.dot_general(a, b, (dims, ((), ())), preferred_element_type=F32)


def send_kernel(*refs):
    sources, (out_ref, ext_ref), targets, sems = refs[:5], refs[5:7], refs[7:11], refs[11]
    places = [targets[0], targets[1], targets[2].at[:, :PROJ], targets[2].at[:, PROJ:], targets[3]]
    copies = [
        pltpu.make_async_copy(source, place, sems.at[n])
        for n, (source, place) in enumerate(zip(sources, places))
    ]
    for copy in copies:
        copy.start()
    cluster_ref, tok_ref, both_ref, cot_ref = targets
    sub = iota((LOCAL, LOCAL), 0)
    lane = iota((LOCAL, LOCAL), 1)
    sub_rows = iota((ROWS, LOCAL), 0)
    lane_rows = iota((ROWS, LOCAL), 1)
    copies[0].wait()
    hits = []
    marks = []
    for h in range(HEADS):
        cluster = cluster_ref[h]
        member = (sub == cluster).astype(BF16)
        same = dot(member, member, ((0,), (0,)))
        order = jnp.sum(jnp.where(sub < lane, same, 0.0), axis=0, keepdims=True)
        owner = (cluster & 96) + (cluster & 1) * 16 + ((cluster >> 1) & 15)
        dest = owner * 2 + order.astype(jnp.int32)
        ext_ref[LOCAL:, h * LOCAL : (h + 1) * LOCAL] = jnp.broadcast_to(
            dest.astype(F32), (16, LOCAL)
        ).astype(BF16)
        hit = sub_rows == dest
        used = jnp.sum(jnp.where(hit, 1.0, 0.0), axis=1, keepdims=True)
        hits.append(hit.astype(BF16))
        marks.append(jnp.where((lane_rows == 0) & (used < 0.5), UNUSED, 0.0))
    for copy in copies[1:]:
        copy.wait()
    tokens = tok_ref[...]
    ext_ref[:LOCAL, :] = tokens
    both = dot(tokens, both_ref[...]).astype(BF16)
    shared, value = both[:, :PROJ], both[:, PROJ:]
    cot = cot_ref[...]
    blank = jnp.zeros((LOCAL, HEAD), BF16)
    moved = []
    for h in range(HEADS):
        cols = slice(h * HEAD, (h + 1) * HEAD)
        tail = [cot[:, cols], blank] if h % 2 == 0 else [blank, cot[:, cols]]
        packed = jnp.concatenate([shared[:, cols], value[:, cols]] + tail, axis=1)
        moved.append(dot(hits[h], packed))
    for h in range(HEADS):
        rows = (moved[h][:, :LOCAL] + marks[h]).astype(BF16)
        out_ref[:, h] = rows.reshape(LOCAL, 2, LOCAL)
    for k in range(HEADS // 2):
        rows = (moved[2 * k][:, LOCAL:] + moved[2 * k + 1][:, LOCAL:]).astype(BF16)
        out_ref[:, HEADS + k] = rows.reshape(LOCAL, 2, LOCAL)


def position(row):
    return (row & 192) + ((row >> 1) & 15) * 4 + ((row >> 5) & 1) * 2 + (row & 1)


def spread(block, slot):
    rows = block.shape[0] // 8
    parts = [block[p * rows : (p + 1) * rows] for p in range(8)]
    for bit in (1, 2, 4):
        odd = (slot & bit) != 0
        after = list(parts)
        for p in range(8):
            if p & bit == 0:
                low, high = parts[p], parts[p + bit]
                after[p] = jnp.where(odd, pltpu.roll(high, BLOCK * bit, 1), low)
                after[p + bit] = jnp.where(odd, high, pltpu.roll(low, LOCAL - BLOCK * bit, 1))
        parts = after
    return parts


def attend_kernel(in_ref, out_ref):
    half = ROWS // 2
    lane_rows = iota((ROWS, LOCAL), 1)
    first = lane_rows == 0
    bias_lane = lane_rows == HEAD
    head_lanes = lane_rows < HEAD
    left_causal = position(iota((half, half), 0)) <= position(iota((half, half), 1))
    right_causal = position(iota((ROWS, half), 0)) <= position(iota((ROWS, half), 1) + half)
    slot = iota((ROWS // 8, LOCAL), 1) >> 4
    hidden = jnp.zeros((half, half), BF16)
    pending = None
    for start in range(0, HEADS, 3):
        group = range(start, start + 3)
        blocks, keys, queries, cots = {}, {}, {}, {}
        for h in group:
            block = in_ref[h].astype(F32)
            empty = block[:, :1] > 32768.0
            block = jnp.where(empty & first, 0.0, block)
            query = jnp.where(head_lanes, block * 0.125, jnp.where(bias_lane, 1.0, 0.0))
            queries[h] = query.astype(BF16)
            keys[h] = jnp.where(
                head_lanes, block, jnp.where(bias_lane & empty, -1e30, 0.0)
            ).astype(BF16)
            blocks[h] = block.astype(BF16)
            pair = in_ref[HEADS + h // 2]
            cots[h] = pair[:, :HEAD] if h % 2 == 0 else pair[:, HEAD:]
        tiles = (
            (slice(0, half), slice(0, half), left_causal),
            (slice(0, ROWS), slice(half, ROWS), right_causal),
        )
        scores, d_probs = {}, {}
        for h in group:
            scores[h] = dot(keys[h], queries[h], ((1,), (1,)))
            d_probs[h] = dot(blocks[h][:, HEAD:], cots[h], ((1,), (1,)))
        probs, d_scores = {}, {}
        for h in group:
            parts = []
            for rows, cols, causal in tiles:
                tile = jnp.where(causal, scores[h][rows, cols], -1e30)
                weights = jnp.exp(tile - jnp.max(tile, axis=0, keepdims=True))
                scale = 1.0 / jnp.sum(weights, axis=0, keepdims=True)
                parts.append((weights * scale).astype(BF16))
            lower = [
                (parts[n].astype(F32), d_probs[h][rows, cols])
                for n, (rows, cols, causal) in enumerate(tiles)
            ]
            slopes = [
                (wide * (d_prob - jnp.sum(wide * d_prob, axis=0, keepdims=True))).astype(BF16)
                for wide, d_prob in lower
            ]
            for held, done in ((probs, parts), (d_scores, slopes)):
                left = jnp.concatenate([done[0], hidden], axis=0)
                held[h] = jnp.concatenate([left, done[1]], axis=1)
        for h in group:
            turned = blocks[h].T
            above = dot(turned[:HEAD], d_scores[h])
            above = above + dot(turned[:HEAD], d_scores[h], ((1,), (1,)))
            out = dot(turned[HEAD:], probs[h])
            d_value = dot(cots[h].T, probs[h], ((1,), (1,)))
            grads = jnp.concatenate([above * 0.125, d_value], axis=0).T
            for m, part in enumerate(spread(grads, slot)):
                n = h * 8 + m
                part = part.astype(BF16).reshape(16, 2, LOCAL)
                out_ref[n // 6 * 16 : (n // 6 + 1) * 16, n % 6] = part
            if h % 2 == 0:
                pending = out
            else:
                k = HEADS + h // 2
                joined = jnp.concatenate([pending, out], axis=0).T.astype(BF16)
                out_ref[:, k] = joined.reshape(LOCAL, 2, LOCAL)


def index_of(place_ref, dy, dc):
    return lax.rem(place_ref[0] + dy, 4) * 2 + lax.rem(place_ref[1] + dc, 2)


def partial_kernel(place_ref, in_ref, *refs):
    exts, (out_ref, keep_ref, give_ref), (dests, cols, scratch) = refs[:2], refs[2:5], refs[5:]
    here = place_ref[1]
    j = place_ref[0] * 2 + here
    head = (j * 3 // 4, (j * 6 + 5) // 8)
    lane_slot = iota((ROWS, LOCAL), 1) >> 4
    sub_rows = iota((ROWS, LOCAL), 0).astype(F32)
    for n, (dy, dc) in enumerate(STEPS):
        source = index_of(place_ref, 4 - dy, dc)
        for i in range(2):
            lanes = pl.ds(pl.multiple_of(head[i] * LOCAL, LOCAL), LOCAL)
            dests[i, source] = exts[dc][dy, LOCAL:, lanes].astype(F32)[:8]
    turned = [in_ref[:, b].reshape(ROWS, LOCAL) for b in range(6)]
    turned = [pltpu.roll(rows.astype(F32), BLOCK * b, 1).astype(BF16) if b else rows for b, rows in enumerate(turned)]
    limit = lax.rem(j, 4)
    limit = jnp.where(limit == 1, 2, jnp.where(limit == 2, 4, 6))
    for p in range(8):
        rows = turned[0]
        for b in range(1, 6):
            rows = jnp.where(lane_slot == (b + p) % 8, turned[b], rows)
        routes = [(sub_rows == dests[i, p, :1]).astype(BF16) for i in range(2)]
        found = dot(rows, jnp.concatenate(routes, axis=1), ((0,), (0,)))
        blocks = []
        for b in range(6):
            cut = slice((b + p) % 8 * BLOCK, ((b + p) % 8 + 1) * BLOCK)
            blocks.append(jnp.where(b < limit, found[cut, :LOCAL], found[cut, LOCAL:]))
        cols[p] = jnp.concatenate(blocks, axis=0).astype(BF16)
    total = None
    for dy in range(4):
        near = [cols[index_of(place_ref, 4 - dy, dc)] for dc in range(2)]
        rows = jnp.concatenate([exts[dc][dy, :LOCAL, :] for dc in range(2)], axis=0)
        term = dot(jnp.concatenate(near, axis=1), rows)
        total = term if total is None else total + term
    for k in range(WIDTH // LOCAL):
        scratch[k * COLUMNS : (k + 1) * COLUMNS, :] = total[:, k * LOCAL : (k + 1) * LOCAL]
    scratch[16 * PIECE :, :] = jnp.zeros((8, LOCAL), F32)
    for i in range(16):
        out_ref[i] = scratch[i * PIECE : i * PIECE + SLOT, :].astype(BF16)
    for y in range(4):
        keep_ref[y] = cols[y * 2 + here]
        give_ref[y] = cols[y * 2 + 1 - here]


def output_kernel(in_ref, ext_ref, att_ref):
    sub_rows = iota((ROWS, LOCAL), 0).astype(F32)
    head_lanes = iota((LOCAL, LOCAL), 1) < HEAD
    dests = ext_ref[0, LOCAL:, :].astype(F32)[:1]
    for k in range(HEADS // 2):
        rows = in_ref[:, HEADS + k].reshape(ROWS, LOCAL)
        found = []
        for h in (2 * k, 2 * k + 1):
            route = (sub_rows == dests[:, h * LOCAL : (h + 1) * LOCAL]).astype(BF16)
            found.append(dot(route, rows, ((0,), (0,))))
        both = jnp.where(head_lanes, found[0], found[1])
        att_ref[:, k * LOCAL : (k + 1) * LOCAL] = both.astype(BF16)


def pack_kernel(block_ref, keep_ref, got_ref, out_ref, scratch):
    for i in range(16):
        scratch[i * PIECE : (i + 1) * PIECE, :] = block_ref[i].astype(F32)[:PIECE]
    block = scratch[...].astype(BF16)
    for y in range(4):
        out_ref[y, :WHOLE, :] = block
        out_ref[y, WHOLE : WHOLE + MESSAGE, :] = keep_ref[y]
        out_ref[y, WHOLE + MESSAGE :, :] = got_ref[y]


def return_kernel(place_ref, all_ref, ws_ref, wv_ref, grad_ref, held):
    here = place_ref[1]
    for y in range(4):
        held[y * 2 + here] = all_ref[y, WHOLE : WHOLE + MESSAGE, :]
        held[y * 2 + 1 - here] = all_ref[y, WHOLE + MESSAGE :, :]

    def columns(first):
        rows = [
            held[n // 6, n % 6 * BLOCK : (n % 6 + 1) * BLOCK, :]
            for h in range(HEADS)
            for n in range(h * 8 + first, h * 8 + first + 4)
        ]
        return jnp.concatenate(rows, axis=0).astype(F32).T.astype(BF16)

    left = columns(0)
    right = columns(4)
    total = dot(left, ws_ref[...], ((1,), (1,))) + dot(right, wv_ref[...], ((1,), (1,)))
    grad_ref[...] = total.astype(BF16)


def sum_kernel(in_ref, out_ref):
    total = in_ref[0].astype(F32)
    for i in range(1, in_ref.shape[0]):
        total = total + in_ref[i].astype(F32)
    total = total.astype(BF16)
    for i in range(out_ref.shape[0]):
        out_ref[i] = total


def finish_kernel(place_ref, mine_ref, other_ref, shared_ref, value_ref, held, sems):
    first = place_ref[1] == 0
    copies = []
    for k in range(WIDTH // LOCAL):
        rows = slice(k * COLUMNS, (k + 1) * COLUMNS)
        strip = []
        for y in range(4):
            mine = mine_ref[y, rows, :]
            other = other_ref[y, rows, :]
            strip += [jnp.where(first, mine, other), jnp.where(first, other, mine)]
        strip = jnp.concatenate(strip, axis=0)
        lines = slice(k * LOCAL, (k + 1) * LOCAL)
        for half, ref in enumerate((shared_ref, value_ref)):
            heads = [
                strip[h * LOCAL + half * HEAD : h * LOCAL + (half + 1) * HEAD]
                for h in range(HEADS)
            ]
            held[half, lines, :] = jnp.concatenate(heads, axis=0).T
            copies.append(
                pltpu.make_async_copy(held.at[half, lines], ref.at[lines], sems.at[half, k])
            )
            copies[-1].start()
    for copy in copies:
        copy.wait()


def call(kernel, out, *args, scratch=(), scalars=0, held=False, far=()):
    if held:
        args = [pltpu.with_memory_space_constraint(arg, pltpu.HBM) for arg in args]
    specs = [pl.BlockSpec(memory_space=pltpu.SMEM)] * scalars
    specs += [pl.BlockSpec(memory_space=pl.ANY if held else pltpu.VMEM)] * (len(args) - scalars)
    outs = [
        pl.BlockSpec(memory_space=pl.ANY if n in far else pltpu.VMEM) for n in range(len(out))
    ]
    return pl.pallas_call(
        kernel,
        out_shape=out,
        in_specs=specs,
        out_specs=outs,
        scratch_shapes=scratch,
        compiler_params=pltpu.CompilerParams(vmem_limit_bytes=48 * 1024 * 1024),
    )(*args)


def shape(*dims):
    return jax.ShapeDtypeStruct(dims, BF16)


def swap(rows, axes, groups=None):
    return lax.all_to_all(
        rows, axes, split_axis=0, concat_axis=0, tiled=True, axis_index_groups=groups
    )


def body(tokens, w_shared, w_value, cluster_ids, slot_index, cotangent):
    rows = tokens[0]
    place = jnp.stack([lax.axis_index("y"), lax.axis_index("c")]).astype(jnp.int32)
    sent, ext = call(
        send_kernel,
        (shape(LOCAL, 9, 2, LOCAL), shape(LOCAL + 16, WIDTH)),
        cluster_ids.transpose(1, 0, 2),
        rows,
        w_shared,
        w_value,
        cotangent[0],
        scratch=[
            pltpu.VMEM((HEADS, 1, LOCAL), jnp.int32),
            pltpu.VMEM((LOCAL, WIDTH), BF16),
            pltpu.VMEM((WIDTH, 2 * PROJ), BF16),
            pltpu.VMEM((LOCAL, PROJ), BF16),
            pltpu.SemaphoreType.DMA((5,)),
        ],
        held=True,
    )

    def shift(pair, dy):
        return lax.ppermute(pair, "y", [(y, (y + dy) % 4) for y in range(4)])

    def flip(part):
        return lax.ppermute(part, "c", [(0, 1), (1, 0)])

    arrived = swap(sent, OWNERS)
    arrived, ext = lax.optimization_barrier((arrived, ext))
    mine = jnp.stack([ext] + [shift(ext, dy) for dy in range(1, 4)])
    exts = [mine, flip(mine)]
    arrived = arrived.transpose(1, 0, 2, 3).reshape(9, ROWS, LOCAL)
    (worked,) = call(
        attend_kernel,
        [shape(LOCAL, 9, 2, LOCAL)],
        arrived,
    )
    back = swap(worked, OWNERS)
    part, keep, give = call(
        partial_kernel,
        [shape(16, SLOT, LOCAL), shape(4, MESSAGE, LOCAL), shape(4, MESSAGE, LOCAL)],
        place,
        back,
        *exts,
        scratch=[
            pltpu.VMEM((2, 8, 8, LOCAL), F32),
            pltpu.VMEM((8, COLUMNS, LOCAL), BF16),
            pltpu.VMEM((16 * PIECE + 8, LOCAL), F32),
        ],
        scalars=1,
    )
    part = swap(part, ("x", "z"), NEAR)
    part, back, give = lax.optimization_barrier((part, back, give))
    (attention,) = call(output_kernel, [shape(LOCAL, PROJ)], back, mine)
    (part,) = call(sum_kernel, [shape(4, SLOT, LOCAL)], part)
    part = swap(part, "z", FAR)
    part, got, attention = lax.optimization_barrier((part, flip(give), attention))
    (block,) = call(sum_kernel, [shape(16, SLOT, LOCAL)], part)
    (block,) = call(
        pack_kernel,
        [shape(4, WHOLE + 2 * MESSAGE, LOCAL)],
        swap(block, ("x", "z"), NEAR),
        keep,
        got,
        scratch=[pltpu.VMEM((WHOLE, LOCAL), F32)],
    )
    block = swap(block, "y")
    other = flip(block)
    (grad_tokens,) = call(
        return_kernel,
        [shape(LOCAL, WIDTH)],
        place,
        block,
        w_shared,
        w_value,
        scratch=[pltpu.VMEM((8, MESSAGE, LOCAL), BF16)],
        scalars=1,
    )
    grad_shared, grad_value = call(
        finish_kernel,
        (shape(WIDTH, PROJ), shape(WIDTH, PROJ)),
        place,
        block,
        other,
        scratch=[
            pltpu.VMEM((2, WIDTH, PROJ), BF16),
            pltpu.SemaphoreType.DMA((2, WIDTH // LOCAL)),
        ],
        scalars=1,
        far=(0, 1),
    )
    return (attention[None], grad_tokens[None], grad_shared, grad_value)


def solution(mesh):
    fine = Mesh(mesh.devices.reshape(4, 4, 16, 2), ("x", "y", "z", "c"))
    in_specs = (
        P("x", TOK, None),
        P(),
        P(),
        P("x", None, TOK),
        P("x", None, TOK),
        P("x", TOK, None),
    )
    out_specs = (P("x", TOK, None), P("x", TOK, None), P(), P())
    return jax.shard_map(body, mesh=fine, in_specs=in_specs, out_specs=out_specs, check_vma=False)
```

```python
import jax
import jax.numpy as jnp
from jax import lax
from jax.experimental import pallas as pl
from jax.experimental.pallas import tpu as pltpu
from jax.sharding import Mesh
from jax.sharding import PartitionSpec as P

F32 = jnp.float32
BF16 = jnp.bfloat16
HEADS = 6
HEAD = 64
ROWS = 256
LOCAL = 128
WIDTH = 768
PROJ = 384
UNUSED = 65536.0
PLANE = ("y", "c")
TOK = ("y", "z", "c")
OWNERS = ("y", "c", "z")
RING = [(3, 4, 9, 14), (2, 7, 8, 13), (1, 6, 11, 12), (0, 5, 10, 15)]
FAR = [list(group) for group in RING]
NEAR = [[x * 16 + RING[n][b] for x in range(4) for n in range(4)] for b in range(4)]
STEPS = [(dy, dc) for dy in range(4) for dc in range(2)]
COLUMNS = 96
PIECE = 36
SLOT = 40
BLOCK = 16
WHOLE = 576
MESSAGE = 96


def iota(shape, dim):
    return lax.broadcasted_iota(jnp.int32, shape, dim)


def dot(a, b, dims=((1,), (0,))):
    return lax.dot_general(a, b, (dims, ((), ())), preferred_element_type=F32)


def send_kernel(*refs):
    sources, (out_ref, ext_ref), targets, sems = refs[:5], refs[5:7], refs[7:12], refs[12]
    copies = [
        pltpu.make_async_copy(source, target, sems.at[n])
        for n, (source, target) in enumerate(zip(sources, targets))
    ]
    for copy in copies:
        copy.start()
    cluster_ref, tok_ref, ws_ref, wv_ref, cot_ref = targets
    sub = iota((LOCAL, LOCAL), 0)
    lane = iota((LOCAL, LOCAL), 1)
    sub_rows = iota((ROWS, LOCAL), 0)
    lane_rows = iota((ROWS, LOCAL), 1)
    copies[0].wait()
    hits = []
    marks = []
    for h in range(HEADS):
        cluster = cluster_ref[h]
        member = (sub == cluster).astype(BF16)
        same = dot(member, member, ((0,), (0,)))
        order = jnp.sum(jnp.where(sub < lane, same, 0.0), axis=0, keepdims=True)
        owner = (cluster & 96) + (cluster & 1) * 16 + ((cluster >> 1) & 15)
        dest = owner * 2 + order.astype(jnp.int32)
        ext_ref[LOCAL:, h * LOCAL : (h + 1) * LOCAL] = jnp.broadcast_to(
            dest.astype(F32), (16, LOCAL)
        ).astype(BF16)
        hit = sub_rows == dest
        used = jnp.sum(jnp.where(hit, 1.0, 0.0), axis=1, keepdims=True)
        hits.append(hit.astype(BF16))
        marks.append(jnp.where((lane_rows == 0) & (used < 0.5), UNUSED, 0.0))
    for copy in copies[1:]:
        copy.wait()
    tokens = tok_ref[...]
    ext_ref[:LOCAL, :] = tokens
    shared = dot(tokens, ws_ref[...]).astype(BF16)
    value = dot(tokens, wv_ref[...]).astype(BF16)
    cot = cot_ref[...]
    blank = jnp.zeros((LOCAL, HEAD), BF16)
    pending = None
    for h in range(HEADS):
        cols = slice(h * HEAD, (h + 1) * HEAD)
        tail = [cot[:, cols], blank] if h % 2 == 0 else [blank, cot[:, cols]]
        packed = jnp.concatenate([shared[:, cols], value[:, cols]] + tail, axis=1)
        moved = dot(hits[h], packed)
        out_ref[:, h] = (moved[:, :LOCAL] + marks[h]).astype(BF16).reshape(LOCAL, 2, LOCAL)
        if h % 2 == 0:
            pending = moved[:, LOCAL:]
        else:
            packed = (pending + moved[:, LOCAL:]).astype(BF16)
            out_ref[:, HEADS + h // 2] = packed.reshape(LOCAL, 2, LOCAL)


def position(row):
    return (row & 192) + ((row >> 1) & 15) * 4 + ((row >> 5) & 1) * 2 + (row & 1)


def spread(block, slot):
    rows = block.shape[0] // 8
    parts = [block[p * rows : (p + 1) * rows] for p in range(8)]
    for bit in (1, 2, 4):
        odd = (slot & bit) != 0
        after = list(parts)
        for p in range(8):
            if p & bit == 0:
                low, high = parts[p], parts[p + bit]
                after[p] = jnp.where(odd, pltpu.roll(high, BLOCK * bit, 1), low)
                after[p + bit] = jnp.where(odd, high, pltpu.roll(low, LOCAL - BLOCK * bit, 1))
        parts = after
    return parts


def attend_kernel(in_ref, out_ref):
    half = ROWS // 2
    lane_rows = iota((ROWS, LOCAL), 1)
    first = lane_rows == 0
    bias_lane = lane_rows == HEAD
    head_lanes = lane_rows < HEAD
    left_causal = position(iota((half, half), 0)) <= position(iota((half, half), 1))
    right_causal = position(iota((ROWS, half), 0)) <= position(iota((ROWS, half), 1) + half)
    slot = iota((ROWS // 8, LOCAL), 1) >> 4
    hidden = jnp.zeros((half, half), BF16)
    pending = None
    for start in range(0, HEADS, 3):
        group = range(start, start + 3)
        blocks, keys, queries, cots = {}, {}, {}, {}
        for h in group:
            block = in_ref[h].astype(F32)
            empty = block[:, :1] > 32768.0
            block = jnp.where(empty & first, 0.0, block)
            query = jnp.where(head_lanes, block * 0.125, jnp.where(bias_lane, 1.0, 0.0))
            queries[h] = query.astype(BF16)
            keys[h] = jnp.where(
                head_lanes, block, jnp.where(bias_lane & empty, -1e30, 0.0)
            ).astype(BF16)
            blocks[h] = block.astype(BF16)
            pair = in_ref[HEADS + h // 2]
            cots[h] = pair[:, :HEAD] if h % 2 == 0 else pair[:, HEAD:]
        tiles = (
            (slice(0, half), slice(0, half), left_causal),
            (slice(0, ROWS), slice(half, ROWS), right_causal),
        )
        scores, d_probs = {}, {}
        for h in group:
            scores[h] = dot(keys[h], queries[h], ((1,), (1,)))
            d_probs[h] = dot(blocks[h][:, HEAD:], cots[h], ((1,), (1,)))
        probs, d_scores = {}, {}
        for h in group:
            parts = []
            for rows, cols, causal in tiles:
                tile = jnp.where(causal, scores[h][rows, cols], -1e30)
                weights = jnp.exp(tile - jnp.max(tile, axis=0, keepdims=True))
                scale = 1.0 / jnp.sum(weights, axis=0, keepdims=True)
                parts.append((weights * scale).astype(BF16))
            lower = [
                (parts[n].astype(F32), d_probs[h][rows, cols])
                for n, (rows, cols, causal) in enumerate(tiles)
            ]
            slopes = [
                (wide * (d_prob - jnp.sum(wide * d_prob, axis=0, keepdims=True))).astype(BF16)
                for wide, d_prob in lower
            ]
            for held, done in ((probs, parts), (d_scores, slopes)):
                left = jnp.concatenate([done[0], hidden], axis=0)
                held[h] = jnp.concatenate([left, done[1]], axis=1)
        for h in group:
            turned = blocks[h].T
            above = dot(turned[:HEAD], d_scores[h])
            above = above + dot(turned[:HEAD], d_scores[h], ((1,), (1,)))
            out = dot(turned[HEAD:], probs[h])
            d_value = dot(cots[h].T, probs[h], ((1,), (1,)))
            grads = jnp.concatenate([above * 0.125, d_value], axis=0).T
            for m, part in enumerate(spread(grads, slot)):
                n = h * 8 + m
                part = part.astype(BF16).reshape(16, 2, LOCAL)
                out_ref[n // 6 * 16 : (n // 6 + 1) * 16, n % 6] = part
            if h % 2 == 0:
                pending = out
            else:
                k = HEADS + h // 2
                joined = jnp.concatenate([pending, out], axis=0).T.astype(BF16)
                out_ref[:, k] = joined.reshape(LOCAL, 2, LOCAL)


def index_of(place_ref, dy, dc):
    return lax.rem(place_ref[0] + dy, 4) * 2 + lax.rem(place_ref[1] + dc, 2)


def partial_kernel(place_ref, in_ref, *refs):
    exts, (out_ref, keep_ref, give_ref), (dests, cols, scratch) = refs[:2], refs[2:5], refs[5:]
    here = place_ref[1]
    j = place_ref[0] * 2 + here
    head = (j * 3 // 4, (j * 6 + 5) // 8)
    lane_slot = iota((ROWS, LOCAL), 1) >> 4
    sub_rows = iota((ROWS, LOCAL), 0).astype(F32)
    for n, (dy, dc) in enumerate(STEPS):
        source = index_of(place_ref, 4 - dy, dc)
        for i in range(2):
            lanes = pl.ds(pl.multiple_of(head[i] * LOCAL, LOCAL), LOCAL)
            dests[i, source] = exts[dc][dy, LOCAL:, lanes].astype(F32)[:8]
    turned = [in_ref[:, b].reshape(ROWS, LOCAL) for b in range(6)]
    turned = [pltpu.roll(rows.astype(F32), BLOCK * b, 1).astype(BF16) if b else rows for b, rows in enumerate(turned)]
    limit = lax.rem(j, 4)
    limit = jnp.where(limit == 1, 2, jnp.where(limit == 2, 4, 6))
    for p in range(8):
        rows = turned[0]
        for b in range(1, 6):
            rows = jnp.where(lane_slot == (b + p) % 8, turned[b], rows)
        routes = [(sub_rows == dests[i, p, :1]).astype(BF16) for i in range(2)]
        found = dot(rows, jnp.concatenate(routes, axis=1), ((0,), (0,)))
        blocks = []
        for b in range(6):
            cut = slice((b + p) % 8 * BLOCK, ((b + p) % 8 + 1) * BLOCK)
            blocks.append(jnp.where(b < limit, found[cut, :LOCAL], found[cut, LOCAL:]))
        cols[p] = jnp.concatenate(blocks, axis=0).astype(BF16)
    total = None
    for dy in range(4):
        near = [cols[index_of(place_ref, 4 - dy, dc)] for dc in range(2)]
        rows = jnp.concatenate([exts[dc][dy, :LOCAL, :] for dc in range(2)], axis=0)
        term = dot(jnp.concatenate(near, axis=1), rows)
        total = term if total is None else total + term
    for k in range(WIDTH // LOCAL):
        scratch[k * COLUMNS : (k + 1) * COLUMNS, :] = total[:, k * LOCAL : (k + 1) * LOCAL]
    scratch[16 * PIECE :, :] = jnp.zeros((8, LOCAL), F32)
    for i in range(16):
        out_ref[i] = scratch[i * PIECE : i * PIECE + SLOT, :].astype(BF16)
    for y in range(4):
        keep_ref[y] = cols[y * 2 + here]
        give_ref[y] = cols[y * 2 + 1 - here]


def output_kernel(in_ref, ext_ref, att_ref):
    sub_rows = iota((ROWS, LOCAL), 0).astype(F32)
    head_lanes = iota((LOCAL, LOCAL), 1) < HEAD
    dests = ext_ref[0, LOCAL:, :].astype(F32)[:1]
    for k in range(HEADS // 2):
        rows = in_ref[:, HEADS + k].reshape(ROWS, LOCAL)
        found = []
        for h in (2 * k, 2 * k + 1):
            route = (sub_rows == dests[:, h * LOCAL : (h + 1) * LOCAL]).astype(BF16)
            found.append(dot(route, rows, ((0,), (0,))))
        both = jnp.where(head_lanes, found[0], found[1])
        att_ref[:, k * LOCAL : (k + 1) * LOCAL] = both.astype(BF16)


def pack_kernel(block_ref, keep_ref, got_ref, out_ref, scratch):
    for i in range(16):
        scratch[i * PIECE : (i + 1) * PIECE, :] = block_ref[i].astype(F32)[:PIECE]
    block = scratch[...].astype(BF16)
    for y in range(4):
        out_ref[y, :WHOLE, :] = block
        out_ref[y, WHOLE : WHOLE + MESSAGE, :] = keep_ref[y]
        out_ref[y, WHOLE + MESSAGE :, :] = got_ref[y]


def return_kernel(place_ref, all_ref, ws_ref, wv_ref, grad_ref, held):
    here = place_ref[1]
    for y in range(4):
        held[y * 2 + here] = all_ref[y, WHOLE : WHOLE + MESSAGE, :]
        held[y * 2 + 1 - here] = all_ref[y, WHOLE + MESSAGE :, :]

    def columns(first):
        rows = [
            held[n // 6, n % 6 * BLOCK : (n % 6 + 1) * BLOCK, :]
            for h in range(HEADS)
            for n in range(h * 8 + first, h * 8 + first + 4)
        ]
        return jnp.concatenate(rows, axis=0).astype(F32).T.astype(BF16)

    left = columns(0)
    right = columns(4)
    total = dot(left, ws_ref[...], ((1,), (1,))) + dot(right, wv_ref[...], ((1,), (1,)))
    grad_ref[...] = total.astype(BF16)


def sum_kernel(in_ref, out_ref):
    total = in_ref[0].astype(F32)
    for i in range(1, in_ref.shape[0]):
        total = total + in_ref[i].astype(F32)
    total = total.astype(BF16)
    for i in range(out_ref.shape[0]):
        out_ref[i] = total


def finish_kernel(place_ref, mine_ref, other_ref, shared_ref, value_ref, held, sems):
    first = place_ref[1] == 0
    copies = []
    for k in range(WIDTH // LOCAL):
        rows = slice(k * COLUMNS, (k + 1) * COLUMNS)
        strip = []
        for y in range(4):
            mine = mine_ref[y, rows, :]
            other = other_ref[y, rows, :]
            strip += [jnp.where(first, mine, other), jnp.where(first, other, mine)]
        strip = jnp.concatenate(strip, axis=0)
        lines = slice(k * LOCAL, (k + 1) * LOCAL)
        for half, ref in enumerate((shared_ref, value_ref)):
            heads = [
                strip[h * LOCAL + half * HEAD : h * LOCAL + (half + 1) * HEAD]
                for h in range(HEADS)
            ]
            held[half, lines, :] = jnp.concatenate(heads, axis=0).T
            copies.append(
                pltpu.make_async_copy(held.at[half, lines], ref.at[lines], sems.at[half, k])
            )
            copies[-1].start()
    for copy in copies:
        copy.wait()


def call(kernel, out, *args, scratch=(), scalars=0, held=False, far=()):
    if held:
        args = [pltpu.with_memory_space_constraint(arg, pltpu.HBM) for arg in args]
    specs = [pl.BlockSpec(memory_space=pltpu.SMEM)] * scalars
    specs += [pl.BlockSpec(memory_space=pl.ANY if held else pltpu.VMEM)] * (len(args) - scalars)
    outs = [
        pl.BlockSpec(memory_space=pl.ANY if n in far else pltpu.VMEM) for n in range(len(out))
    ]
    return pl.pallas_call(
        kernel,
        out_shape=out,
        in_specs=specs,
        out_specs=outs,
        scratch_shapes=scratch,
        compiler_params=pltpu.CompilerParams(vmem_limit_bytes=48 * 1024 * 1024),
    )(*args)


def shape(*dims):
    return jax.ShapeDtypeStruct(dims, BF16)


def swap(rows, axes, groups=None):
    return lax.all_to_all(
        rows, axes, split_axis=0, concat_axis=0, tiled=True, axis_index_groups=groups
    )


def body(tokens, w_shared, w_value, cluster_ids, slot_index, cotangent):
    rows = tokens[0]
    place = jnp.stack([lax.axis_index("y"), lax.axis_index("c")]).astype(jnp.int32)
    sent, ext = call(
        send_kernel,
        (shape(LOCAL, 9, 2, LOCAL), shape(LOCAL + 16, WIDTH)),
        cluster_ids.transpose(1, 0, 2),
        rows,
        w_shared,
        w_value,
        cotangent[0],
        scratch=[
            pltpu.VMEM((HEADS, 1, LOCAL), jnp.int32),
            pltpu.VMEM((LOCAL, WIDTH), BF16),
            pltpu.VMEM((WIDTH, PROJ), BF16),
            pltpu.VMEM((WIDTH, PROJ), BF16),
            pltpu.VMEM((LOCAL, PROJ), BF16),
            pltpu.SemaphoreType.DMA((5,)),
        ],
        held=True,
    )

    def shift(pair, dy):
        return lax.ppermute(pair, "y", [(y, (y + dy) % 4) for y in range(4)])

    def flip(part):
        return lax.ppermute(part, "c", [(0, 1), (1, 0)])

    arrived = swap(sent, OWNERS)
    mine = jnp.stack([ext] + [shift(ext, dy) for dy in range(1, 4)])
    exts = [mine, flip(mine)]
    arrived = arrived.transpose(1, 0, 2, 3).reshape(9, ROWS, LOCAL)
    (worked,) = call(
        attend_kernel,
        [shape(LOCAL, 9, 2, LOCAL)],
        arrived,
    )
    worked, mine, exts, place = lax.optimization_barrier((worked, mine, exts, place))
    back = swap(worked, OWNERS)
    part, keep, give = call(
        partial_kernel,
        [shape(16, SLOT, LOCAL), shape(4, MESSAGE, LOCAL), shape(4, MESSAGE, LOCAL)],
        place,
        back,
        *exts,
        scratch=[
            pltpu.VMEM((2, 8, 8, LOCAL), F32),
            pltpu.VMEM((8, COLUMNS, LOCAL), BF16),
            pltpu.VMEM((16 * PIECE + 8, LOCAL), F32),
        ],
        scalars=1,
    )
    part = swap(part, ("x", "z"), NEAR)
    part, back, give = lax.optimization_barrier((part, back, give))
    (attention,) = call(output_kernel, [shape(LOCAL, PROJ)], back, mine)
    (part,) = call(sum_kernel, [shape(4, SLOT, LOCAL)], part)
    part = swap(part, "z", FAR)
    part, got, attention = lax.optimization_barrier((part, flip(give), attention))
    (block,) = call(sum_kernel, [shape(16, SLOT, LOCAL)], part)
    (block,) = call(
        pack_kernel,
        [shape(4, WHOLE + 2 * MESSAGE, LOCAL)],
        swap(block, ("x", "z"), NEAR),
        keep,
        got,
        scratch=[pltpu.VMEM((WHOLE, LOCAL), F32)],
    )
    block = swap(block, "y")
    other = flip(block)
    (grad_tokens,) = call(
        return_kernel,
        [shape(LOCAL, WIDTH)],
        place,
        block,
        w_shared,
        w_value,
        scratch=[pltpu.VMEM((8, MESSAGE, LOCAL), BF16)],
        scalars=1,
    )
    grad_shared, grad_value = call(
        finish_kernel,
        (shape(WIDTH, PROJ), shape(WIDTH, PROJ)),
        place,
        block,
        other,
        scratch=[
            pltpu.VMEM((2, WIDTH, PROJ), BF16),
            pltpu.SemaphoreType.DMA((2, WIDTH // LOCAL)),
        ],
        scalars=1,
        far=(0, 1),
    )
    return (attention[None], grad_tokens[None], grad_shared, grad_value)


def solution(mesh):
    fine = Mesh(mesh.devices.reshape(4, 4, 16, 2), ("x", "y", "z", "c"))
    in_specs = (
        P("x", TOK, None),
        P(),
        P(),
        P("x", None, TOK),
        P("x", None, TOK),
        P("x", TOK, None),
    )
    out_specs = (P("x", TOK, None), P("x", TOK, None), P(), P())
    return jax.shard_map(body, mesh=fine, in_specs=in_specs, out_specs=out_specs, check_vma=False)
```
